256 devices in a mesh: tm: 4 (over y), row: 8 (over z_lo, core), col: 8 (over z_hi, x).
Axes of the slice: x: 4, y: 4, z: 8 (z_hi: 2, z_lo: 4; z = z_hi * 4 + z_lo), core: 2. Of those that a mesh axis runs over, the one named last changes fastest.
Arguments:
- states: float32 [4, 1280, 3072], P('tm', 'row', 'col'), may hold values from -45 to 45
- anchor: float32 [1280, 3072], P('row', 'col'), may hold values from -2.25 to 2.25
- timesteps: int32 [4], P('tm'), may hold values from 0 to 999
- step_sizes: float32 [4], P('tm'), may hold values from 0.25 to 1
- weight_in: bfloat16 [3072, 12288], P('col', 'row'), may hold values from -0.109375 to 0.109375
- weight_out: bfloat16 [12288, 3072], P('row', 'col'), may hold values from -0.0546875 to 0.0546875
- mod_weight: bfloat16 [3072, 3, 3072], P('row', None, 'col'), may hold values from -0.109375 to 0.109375
Outputs:
- advanced: float32 [4, 1280, 3072], P('tm', 'row', 'col')
The draws below stay inside these ranges and needn't reach their ends.
All inputs are finite; a program needn't handle non-finite values.
Results may differ from the reference program's by a relative error of at most 0.028.
Values may be sent and summed in bfloat16 or wider, within the bound.
A program may use at most 64 MiB of HBM per device.

```python
import math
import jax
import jax.numpy as jnp
from jax import lax

D = 3072
FF = 12288
ITERS = 2
TOKENS = 1280
STEPS = 4
N_ROW = 8
N_COL = 8


def column_scaled(key, base_draw, columns):
    column_ramp = jnp.exp(math.log(4.0) * jnp.arange(columns, dtype=jnp.float32) / columns)
    roughness = jnp.exp(jax.random.uniform(key, (columns,), jnp.float32, 0.0, math.log(2.5)))
    return base_draw * column_ramp * roughness


def draw_states(key, part):
    key = jax.random.fold_in(key, 11)
    key_base, key_cols = jax.random.split(key, 2)
    full_shape = (STEPS, TOKENS, D)
    base_draw = jnp.clip(jax.random.normal(key_base, full_shape, jnp.float32), -4.0, 4.0)
    return column_scaled(key_cols, base_draw, D)


def draw_anchor(key, part):
    key = jax.random.fold_in(key, 23)
    key_base, key_cols = jax.random.split(key, 2)
    full_shape = (TOKENS, D)
    base_draw = jnp.clip(jax.random.normal(key_base, full_shape, jnp.float32), -4.0, 4.0)
    return 0.05 * column_scaled(key_cols, base_draw, D)


def plant(array, stream_key, low, top_value):
    dims = array.shape
    spot = [jax.random.randint(jax.random.fold_in(stream_key, axis), (), 0, dims[axis]) for axis in range(len(dims))]
    array = array.at[tuple(spot)].set(low)
    longest = dims.index(max(dims))
    spot[longest] = (spot[longest] + 1) % dims[longest]
    return array.at[tuple(spot)].set(top_value)


def block_levels(rng, extent, cuts, low, largest):
    factor_of, own = 1.0, jax.random.fold_in(rng, 6)
    for position, shards_of in cuts:
        draws = jnp.exp(jax.random.uniform(jax.random.fold_in(own, position), (shards_of,), jnp.float32, low / len(cuts), largest / len(cuts)))
        factor_of = factor_of * jnp.repeat(draws, extent[position] // shards_of).reshape([-1 if axis == position else 1 for axis in range(len(extent))])
    return factor_of


def gaussian(stream_key, dims, deviation, bound, cuts=(), kind=jnp.bfloat16):
    drawn = deviation * jax.random.normal(stream_key, dims, jnp.float32)
    if cuts:
        drawn = drawn * block_levels(stream_key, dims, cuts, -0.22, 0.18)
    return jnp.clip(drawn, -bound, bound).astype(kind)


def setup_inputs(seed: int = 0) -> dict:
    arg_keys = jax.random.split(jax.random.key(seed), 8)
    states = draw_states(jax.random.fold_in(arg_keys[7], 71), 0)
    anchor = draw_anchor(jax.random.fold_in(arg_keys[7], 71), 0)
    timesteps = plant(jax.random.randint(arg_keys[2], (STEPS,), 0, 1000), jax.random.fold_in(arg_keys[2], 1), 0, 999).astype(jnp.int32)
    step_sizes = jnp.clip(jnp.exp(math.log(1.0) - 1.3862944 * jax.random.uniform(arg_keys[3], (STEPS,), jnp.float32) ** block_levels(arg_keys[3], (STEPS,), ((0, 4),), -0.2, 0.2)), 0.25, 1.0)
    weight_in = gaussian(arg_keys[4], (D, FF), D ** -0.5, 0.109375, ((0, 8), (1, 8)))
    weight_out = gaussian(arg_keys[5], (FF, D), FF ** -0.5, 0.0546875, ((0, 8), (1, 8)))
    mod_weight = gaussian(arg_keys[6], (D, 3, D), D ** -0.5, 0.109375, ((0, 8), (2, 8)))
    return dict(states=states, anchor=anchor, timesteps=timesteps, step_sizes=step_sizes, weight_in=weight_in, weight_out=weight_out, mod_weight=mod_weight)


EPSILON = 1e-06

def timestep_embedding(timesteps):
    half_width = D // 2
    positions = jnp.arange(half_width, dtype=jnp.float32)
    frequency = jnp.exp(-math.log(10000.0) * positions / half_width)
    phases = timesteps.astype(jnp.float32)[:, None] * frequency[None, :]
    return jnp.concatenate([jnp.cos(phases), jnp.sin(phases)], axis=1)

def rounded(values):
    return lax.optimization_barrier(values.astype(jnp.bfloat16)).astype(jnp.float32)

def block_output(current, weight_in, weight_out, shift_mod, scale_mod):
    row_sum = lax.optimization_barrier(jnp.sum(current, axis=1))
    squares = lax.optimization_barrier(jnp.sum(current * current, axis=1))
    row_mean = row_sum / D
    row_var = squares / D - row_mean * row_mean
    normed = ((current - row_mean[:, None]) * lax.rsqrt(row_var + EPSILON)[:, None] * (1.0 + scale_mod) + shift_mod).astype(jnp.bfloat16)
    width_col = D // N_COL
    pre_act = jnp.zeros((current.shape[0], FF), jnp.float32)
    for block_index in range(N_COL):
        lower = block_index * width_col
        pre_act = pre_act + rounded(jnp.dot(normed[:, lower:lower + width_col], weight_in[lower:lower + width_col, :], preferred_element_type=jnp.float32))
    hidden = jax.nn.gelu(pre_act, approximate=True).astype(jnp.bfloat16)
    width_row = FF // N_ROW
    result = jnp.zeros((current.shape[0], D), jnp.float32)
    for block_index in range(N_ROW):
        lower = block_index * width_row
        result = result + rounded(jnp.dot(hidden[:, lower:lower + width_row], weight_out[lower:lower + width_row, :], preferred_element_type=jnp.float32))
    return result

def reference(states, anchor, timesteps, step_sizes, weight_in, weight_out, mod_weight):
    embedding = timestep_embedding(timesteps)
    modulation = jnp.einsum('se,ekd->skd', embedding, mod_weight.astype(jnp.float32), precision=lax.Precision.HIGHEST)
    currents = [states[group] for group in range(STEPS)]
    for sweep in range(ITERS):
        drifts = []
        for group in range(STEPS):
            output = block_output(currents[group], weight_in, weight_out, modulation[group, 0], modulation[group, 1])
            drifts.append(step_sizes[group] * modulation[group, 2] * output)
        prefixes = []
        running = jnp.zeros(anchor.shape, jnp.float32)
        for group in range(STEPS):
            prefixes.append(running)
            running = running + drifts[group]
        if sweep + 1 < ITERS:
            currents = [anchor + prefixes[group] for group in range(STEPS)]
    return jnp.stack([anchor + prefixes[group] + drifts[group] for group in range(STEPS)])
```

```python
import functools
import math

import jax
import jax.numpy as jnp
from jax import lax
from jax.experimental import pallas as pl
from jax.experimental.pallas import tpu as pltpu
from jax.sharding import PartitionSpec as P

D = 3072
ITERS = 2
EPSILON = 1e-06
MESH = pl.DeviceIdType.MESH
F32 = jnp.float32
BF16 = jnp.bfloat16

T = 80
W = 384
U = 768

COPIES = 192


def timestep_embedding(timesteps):
    half_width = D // 2
    positions = jnp.arange(half_width, dtype=jnp.float32)
    frequency = jnp.exp(-math.log(10000.0) * positions / half_width)
    phases = timesteps.astype(jnp.float32)[:, None] * frequency[None, :]
    return jnp.concatenate([jnp.cos(phases), jnp.sin(phases)], axis=1)


def kernel(
    step_ref, s_ref, a_ref, m_ref, wi_ref, wo_ref, out_ref,
    sbuf, abuf, mbuf, m1, m2, mrecv, modall, stat, statr,
    xall, win, wout, hid, obs, obr, part, rss, rsr, dsend, drecv, pref, fsend, frecv,
    send, recv,
):
    y = lax.axis_index("tm")
    row = lax.axis_index("row")
    col = lax.axis_index("col")
    l, c = row // 2, lax.rem(row, 2)
    h, x = col // 4, lax.rem(col, 4)
    z = 4 * h + l

    def dev(x_=None, y_=None, z_=None, c_=None):
        x_ = x if x_ is None else x_
        y_ = y if y_ is None else y_
        z_ = z if z_ is None else z_
        c_ = c if c_ is None else c_
        return (y_, 2 * lax.rem(z_, 4) + c_, 4 * (z_ // 4) + x_)

    def xo(k):
        return lax.rem(x + k + 4, 4)

    def yo(k):
        return lax.rem(y + k + 4, 4)

    def zo(k):
        return lax.rem(z + k + 8, 8)

    sib = dev(c_=1 - c)
    z4 = dev(z_=zo(4))
    z4sib = dev(z_=zo(4), c_=1 - c)

    def lo(k):
        return dev(z_=4 * h + lax.rem(l + k, 4))

    ids = iter(range(COPIES))
    pending = []

    def remote(src, dst, ss, rs, to):
        return pltpu.make_async_remote_copy(
            src_ref=src, dst_ref=dst, send_sem=send.at[ss], recv_sem=recv.at[rs],
            device_id=to, device_id_type=MESH,
        )

    def put(k, src, dst, to):
        copy = remote(src, dst, k, k, to)
        copy.start()
        pending.append(copy)

    def got(k, dst):
        remote(dst, dst, k, k, sib).wait_recv()

    partners = [sib, z4, z4sib, dev(z_=zo(1)), dev(z_=zo(-1))]
    partners += [dev(x_=xo(k)) for k in (1, 2, 3)]
    partners += [dev(y_=yo(k)) for k in (1, 2, 3)]
    partners += [lo(k) for k in (1, 2, 3)]
    barrier = pltpu.get_barrier_semaphore()
    for p in partners:
        pl.semaphore_signal(barrier, inc=1, device_id=p, device_id_type=MESH)
    half = lax.rem(x, 2)
    same = x // 2 == c
    swap = [dev(x_=2 * c + i, c_=x // 2) for i in range(2)]
    own = [jnp.logical_and(same, half == i) for i in range(2)]
    for i in range(2):

        @pl.when(jnp.logical_not(own[i]))
        def _(i=i):
            pl.semaphore_signal(barrier, inc=1, device_id=swap[i], device_id_type=MESH)

    pl.semaphore_wait(barrier, len(partners) + 2 - same.astype(jnp.int32))

    swaps = []

    def swap_out(src_of, dst):
        ks = (next(ids), next(ids))
        for i in range(2):

            @pl.when(own[i])
            def _(i=i):
                pltpu.make_async_copy(src_of(i), dst.at[half], recv.at[ks[0] + half]).start()

            @pl.when(jnp.logical_not(own[i]))
            def _(i=i):
                remote(src_of(i), dst.at[half], ks[i], ks[0] + half, swap[i]).start()

        swaps.append((ks, src_of, dst))
        return ks

    def swap_in(ks, dst):
        for i in range(2):
            got(ks[i], dst.at[i])

    ks_state = swap_out(lambda i: s_ref.at[pl.ds(T * i, T)], sbuf)

    mbuf[...] = jnp.zeros_like(mbuf)
    mbuf[0:3, :] = m_ref[...]
    k_ms = next(ids)
    put(k_ms, mbuf, mrecv.at[0], sib)

    mine = 4 * h + x
    far = 4 * (1 - h)

    def win_slot(hx, first=0, rows=W):
        return win.at[pl.ds(pl.multiple_of(hx * W + first, 16), rows), :]

    def wout_slot(hx, first=0, rows=U):
        return wout.at[
            hx // 2, pl.ds(pl.multiple_of(first, 16), rows), pl.ds(pl.multiple_of(lax.rem(hx, 2) * W, 128), W)
        ]

    def wi_part(hd, first, rows):
        return wi_ref.at[pl.ds(pl.multiple_of(first, 16), rows), pl.ds(pl.multiple_of(hd * U, 128), U)]

    def wo_part(hd, first, rows):
        return wo_ref.at[pl.ds(pl.multiple_of(hd * U + first, 16), rows), :]

    sides = ((wi_part, win_slot, W), (wo_part, wout_slot, U))
    ids_w = []
    local = []
    for part_of, slot_of, rows in sides:
        k_x = {k: next(ids) for k in (1, 3)}
        k_fwd = {k: next(ids) for k in (1, 3)}
        k_z = next(ids)
        k_xq = {k: next(ids) for k in (1, 2, 3)}
        k_y = {(s, k): next(ids) for s in range(4) for k in (1, 2, 3)}
        k_own = next(ids)
        ids_w.append((k_x, k_fwd, k_z, k_xq, k_y, k_own))

    def weight_start(w):
        part_of, slot_of, rows = sides[w]
        k_x, k_fwd, k_z, k_xq, k_y, k_own = ids_w[w]
        q = rows // 4
        put(k_z, part_of(1 - h, y * q, q), slot_of(mine, y * q, q), z4)
        for k in (1, 3):
            put(k_x[k], part_of(h, 0, rows), slot_of(mine), dev(x_=xo(k)))
        copy = pltpu.make_async_copy(part_of(h, 0, rows), slot_of(mine), recv.at[k_own])
        copy.start()
        local.append(copy)

    def weight_far(w):
        part_of, slot_of, rows = sides[w]
        k_x, k_fwd, k_z, k_xq, k_y, k_own = ids_w[w]
        q = rows // 4
        here = slot_of(far + x, y * q, q)
        got(k_z, here)
        for k in (1, 3, 2):
            put(k_xq[k], here, here, dev(x_=xo(k)))
        for k in (1, 3, 2):
            put(k_y[0, k], here, here, dev(y_=yo(k)))

    def weight_far_x(w, s):
        part_of, slot_of, rows = sides[w]
        k_x, k_fwd, k_z, k_xq, k_y, k_own = ids_w[w]
        q = rows // 4
        here = slot_of(far + xo(-s), y * q, q)
        got(k_xq[s], here)
        for k in (1, 3, 2):
            put(k_y[s, k], here, here, dev(y_=yo(k)))

    def weight_near(w):
        part_of, slot_of, rows = sides[w]
        k_x, k_fwd, k_z, k_xq, k_y, k_own = ids_w[w]
        for k, first in ((1, 0), (3, rows // 2)):
            got(k_x[k], slot_of(4 * h + xo(-k)))
            there = slot_of(4 * h + xo(-k), first, rows // 2)
            put(k_fwd[k], there, there, dev(x_=xo(k)))

    def weight_end(w):
        part_of, slot_of, rows = sides[w]
        k_x, k_fwd, k_z, k_xq, k_y, k_own = ids_w[w]
        q = rows // 4
        for k, first in ((1, 0), (3, rows // 2)):
            got(k_fwd[k], slot_of(4 * h + xo(2), first, rows // 2))
        for s in range(4):
            for k in (1, 2, 3):
                got(k_y[s, k], slot_of(far + xo(-s), yo(-k) * q, q))
        local[w].wait()

    weight_start(0)
    ks_anchor = swap_out(lambda i: a_ref.at[pl.ds(T * i, T)], abuf)
    weight_start(1)

    def stats_send(it, cur):
        total = sum(jnp.sum(v, axis=1, keepdims=True) for v in cur)
        squares = sum(jnp.sum(v * v, axis=1, keepdims=True) for v in cur)
        lane = lax.broadcasted_iota(jnp.int32, (T, 128), 1)
        stat[it] = jnp.where(lane < 64, total, squares)
        ks = [next(ids) for _ in range(3)]
        for k, to in zip(ks, (z4, z4sib, sib)):
            put(k, stat.at[it], statr.at[it, ks.index(k)], to)
        return ks

    def mod(j, r):
        return modall[2 * c + j, r : r + 1, :]

    def x_slot(it, zz, cc, j):
        hh, ll = zz // 4, lax.rem(zz, 4)
        return xall.at[
            it,
            pl.ds(pl.multiple_of(ll * T, 16), T),
            pl.ds(pl.multiple_of((4 * hh + 2 * cc + j) * W, 128), W),
        ]

    def normalise(it, cur, ks):
        for i, k in enumerate(ks):
            got(k, statr.at[it, i])
        total = stat[it] + statr[it, 0] + statr[it, 1] + statr[it, 2]
        mean = total[:, 0:1] / D
        var = total[:, 64:65] / D - mean * mean
        scale = lax.rsqrt(var + EPSILON)
        for j in range(2):
            value = (cur[j] - mean) * scale * (1.0 + mod(j, 1)) + mod(j, 0)
            xall[
                it,
                pl.ds(pl.multiple_of(l * T, 16), T),
                pl.ds(pl.multiple_of((4 * h + 2 * c + j) * W, 128), W),
            ] = value.astype(BF16)

    def ring_dirs(s):
        return [(g, j) for j in range(2) for g in (0, 1) if s < 4 or g == j]

    sign = (1, -1)

    class Gather:
        def __init__(self, it):
            self.it = it
            self.k = {(s, g, j): next(ids) for s in range(1, 5) for g, j in ring_dirs(s)}
            self.ks = {(s, g, j): next(ids) for s in range(1, 5) for g, j in ring_dirs(s)}
            self.k0 = [next(ids) for _ in range(2)]

        def first(self):
            for j in range(2):
                slot = x_slot(self.it, z, c, j)
                for g in range(2):
                    put(self.k[1, g, j], slot, slot, dev(z_=zo(sign[g])))
                put(self.k0[j], slot, slot, sib)

        def step(self, s):
            for g, j in ring_dirs(s):
                slot = x_slot(self.it, zo(-sign[g] * s), c, j)
                got(self.k[s, g, j], slot)
                if (s + 1, g, j) in self.k:
                    put(self.k[s + 1, g, j], slot, slot, dev(z_=zo(sign[g])))
                put(self.ks[s, g, j], slot, slot, sib)

        def end(self):
            for j in range(2):
                got(self.k0[j], x_slot(self.it, z, 1 - c, j))
            for s in range(1, 5):
                for g, j in ring_dirs(s):
                    got(self.ks[s, g, j], x_slot(self.it, zo(-sign[g] * s), 1 - c, j))

    def first_matmul(it):
        def tile(n, _):
            cols = pl.ds(pl.multiple_of(n * 256, 256), 256)
            pre = jnp.dot(xall[it], win[:, cols], preferred_element_type=F32)
            hid[:, cols] = jax.nn.gelu(pre, approximate=True).astype(BF16)
            return 0

        lax.fori_loop(0, U // 256, tile, 0)

    def second_matmul(it):
        ks = [next(ids) for _ in range(2)]
        for hh in range(2):

            def tile(n, _, hh=hh):
                cols = pl.ds(pl.multiple_of(n * 256, 256), 256)
                other = jnp.dot(hid[...], wout[2 * hh + 1 - c, :, cols], preferred_element_type=F32)
                obs[it, hh, :, cols] = other.astype(BF16)
                return 0

            lax.fori_loop(0, 3, tile, 0)
            put(ks[hh], obs.at[it, hh], obr.at[it, hh], sib)
        for hh in range(2):

            def tile(n, _, hh=hh):
                cols = pl.ds(pl.multiple_of(n * 256, 256), 256)
                kept = jnp.dot(hid[...], wout[2 * hh + c, :, cols], preferred_element_type=F32)
                part[hh, :, :, cols] = kept.reshape(4, T, 256)
                return 0

            lax.fori_loop(0, 3, tile, 0)
        for hh in range(2):
            got(ks[hh], obr.at[it, hh])
            part[hh] += obr[it, hh].astype(F32).reshape(4, T, 2 * W)

    def scatter(it):
        k = {(s, g, j): next(ids) for s in range(1, 5) for g in range(2) for j in range(2) if s > 1 or g == j}

        def term(d, j):
            return part[d // 4, lax.rem(d, 4), :, W * j : W * (j + 1)]

        for s in range(1, 5):
            for j in range(2):
                for g in range(2):
                    if (s, g, j) not in k:
                        continue
                    value = term(zo(sign[g] * (5 - s)), j)
                    if (s - 1, g, j) in k:
                        got(k[s - 1, g, j], rsr.at[it, s - 2, g, j])
                        value = value + rsr[it, s - 2, g, j].astype(F32)
                    rss[it, s - 1, g, j] = value.astype(BF16)
                    put(k[s, g, j], rss.at[it, s - 1, g, j], rsr.at[it, s - 1, g, j], dev(z_=zo(sign[g])))
        result = []
        for j in range(2):
            value = term(z, j)
            for g in range(2):
                got(k[4, g, j], rsr.at[it, 3, g, j])
                value = value + rsr[it, 3, g, j].astype(F32)
            result.append(value)
        return result

    def prefix(it, drift):
        ks = {i: next(ids) for i in (1, 2, 3)}
        for j in range(2):
            dsend[it, j] = drift[j].astype(BF16)
            pref[j] = jnp.zeros((T, W), F32)
        for i in (1, 2, 3):

            @pl.when(y + i < 4)
            def _(i=i):
                remote(dsend.at[it], drecv.at[it, i - 1], ks[i], ks[i], dev(y_=yo(i))).start()

        for i in (3, 2, 1):

            @pl.when(y - i >= 0)
            def _(i=i):
                got(ks[i], drecv.at[it, i - 1])
                for j in range(2):
                    pref[j] += drecv[it, i - 1, j].astype(F32)

        def done():
            for i in (1, 2, 3):

                @pl.when(y + i < 4)
                def _(i=i):
                    remote(dsend.at[it], drecv.at[it, i - 1], ks[i], ks[i], dev(y_=yo(i))).wait_send()

        return done

    swap_in(ks_state, sbuf)
    cur = [sbuf[j] for j in range(2)]
    k_stat = stats_send(0, cur)
    got(k_ms, mrecv.at[0])
    m1[...] = mbuf[...] + mrecv[0]
    k_ml = {k: next(ids) for k in (1, 2, 3)}
    for k in (1, 2, 3):
        put(k_ml[k], m1, mrecv.at[k], lo(k))
    for k in (1, 2, 3):
        got(k_ml[k], mrecv.at[k])
    m2[...] = m1[...] + mrecv[1] + mrecv[2] + mrecv[3]
    k_mx = {k: next(ids) for k in (1, 2, 3)}
    for k in (1, 2, 3):
        put(k_mx[k], m2, modall.at[x], dev(x_=xo(k)))
    modall[x] = m2[...]
    weight_far(0)
    for k in (1, 2, 3):
        got(k_mx[k], modall.at[xo(-k)])
    normalise(0, cur, k_stat)
    gather = Gather(0)
    gather.first()
    weight_near(0)
    gather.step(1)
    weight_far_x(0, 1)
    weight_far_x(0, 3)
    gather.step(2)
    weight_far(1)
    weight_far_x(0, 2)
    gather.step(3)
    weight_near(1)
    gather.step(4)
    weight_far_x(1, 1)
    weight_far_x(1, 3)
    weight_far_x(1, 2)
    gather.end()
    swap_in(ks_anchor, abuf)
    weight_end(0)
    first_matmul(0)
    weight_end(1)
    dones = []
    for it in range(ITERS):
        if it:
            cur = [abuf[j] + pref[j] for j in range(2)]
            k_stat = stats_send(it, cur)
            normalise(it, cur, k_stat)
            gather = Gather(it)
            gather.first()
            for s in range(1, 5):
                gather.step(s)
            gather.end()
            first_matmul(it)
        second_matmul(it)
        block = scatter(it)
        step = step_ref[0]
        drift = [step * mod(j, 2) * block[j] for j in range(2)]
        dones.append(prefix(it, drift))
    for j in range(2):
        fsend[j] = (pref[j] + drift[j]).astype(BF16)
    ks_out = swap_out(lambda j: fsend.at[j], frecv)
    swap_in(ks_out, frecv)
    for i in range(2):
        out_ref[T * i : T * (i + 1), :] = a_ref[T * i : T * (i + 1), :] + frecv[i].astype(F32)

    for copy in pending:
        copy.wait_send()
    for done in dones:
        done()
    for ks, src_of, dst in swaps:
        for i in range(2):

            @pl.when(jnp.logical_not(own[i]))
            def _(i=i):
                remote(src_of(i), dst.at[half], ks[i], ks[0] + half, swap[i]).wait_send()


def local(states, anchor, timesteps, step_sizes, weight_in, weight_out, mod_weight):
    embedding = timestep_embedding(timesteps)[0]
    rows_here = mod_weight.shape[0]
    embed_part = lax.dynamic_slice_in_dim(
        embedding, lax.axis_index("row") * rows_here, rows_here, 0
    )
    mod_part = jnp.einsum(
        "e,ekd->kd", embed_part, mod_weight.astype(jnp.float32), precision=lax.Precision.HIGHEST
    )
    vmem = pl.BlockSpec(memory_space=pltpu.VMEM)
    scratch = [
        pltpu.VMEM((2, T, W), F32),
        pltpu.VMEM((2, T, W), F32),
        pltpu.VMEM((8, W), F32),
        pltpu.VMEM((8, W), F32),
        pltpu.VMEM((8, W), F32),
        pltpu.VMEM((4, 8, W), F32),
        pltpu.VMEM((4, 8, W), F32),
        pltpu.VMEM((ITERS, T, 128), F32),
        pltpu.VMEM((ITERS, 3, T, 128), F32),
        pltpu.VMEM((ITERS, 4 * T, D), BF16),
        pltpu.VMEM((D, U), BF16),
        pltpu.VMEM((4, U, 2 * W), BF16),
        pltpu.VMEM((4 * T, U), BF16),
        pltpu.VMEM((ITERS, 2, 4 * T, 2 * W), BF16),
        pltpu.VMEM((ITERS, 2, 4 * T, 2 * W), BF16),
        pltpu.VMEM((2, 4, T, 2 * W), F32),
        pltpu.VMEM((ITERS, 4, 2, 2, T, W), BF16),
        pltpu.VMEM((ITERS, 4, 2, 2, T, W), BF16),
        pltpu.VMEM((ITERS, 2, T, W), BF16),
        pltpu.VMEM((ITERS, 3, 2, T, W), BF16),
        pltpu.VMEM((2, T, W), F32),
        pltpu.VMEM((2, T, W), BF16),
        pltpu.VMEM((2, T, W), BF16),
        pltpu.SemaphoreType.DMA((COPIES,)),
        pltpu.SemaphoreType.DMA((COPIES,)),
    ]
    out = pl.pallas_call(
        kernel,
        out_shape=jax.ShapeDtypeStruct(anchor.shape, F32),
        in_specs=[pl.BlockSpec(memory_space=pltpu.SMEM), vmem, vmem, vmem]
        + [pl.BlockSpec(memory_space=pl.ANY)] * 2,
        out_specs=vmem,
        scratch_shapes=scratch,
        compiler_params=pltpu.CompilerParams(
            collective_id=0, has_side_effects=True, vmem_limit_bytes=48 << 20
        ),
        name="picard",
    )(step_sizes, states[0], anchor, mod_part, weight_in, weight_out)
    return out[None]


def solution(mesh):
    placed = (
        P("tm", "row", "col"),
        P("row", "col"),
        P("tm"),
        P("tm"),
        P("col", "row"),
        P("row", "col"),
        P("row", None, "col"),
    )
    return jax.shard_map(
        local, mesh=mesh, in_specs=placed, out_specs=P("tm", "row", "col"), check_vma=False
    )
```

```python
import math

import jax
import jax.numpy as jnp
from jax import lax
from jax.experimental import pallas as pl
from jax.experimental.pallas import tpu as pltpu
from jax.sharding import PartitionSpec as P

D = 3072
ITERS = 2
EPSILON = 1e-06
MESH = pl.DeviceIdType.MESH
F32 = jnp.float32
BF16 = jnp.bfloat16

T = 80
W = 384
U = 768

PARTS = ((0, 48), (48, 32))

COPIES = 304


def timestep_embedding(timesteps):
    half_width = D // 2
    positions = jnp.arange(half_width, dtype=jnp.float32)
    frequency = jnp.exp(-math.log(10000.0) * positions / half_width)
    phases = timesteps.astype(jnp.float32)[:, None] * frequency[None, :]
    return jnp.concatenate([jnp.cos(phases), jnp.sin(phases)], axis=1)


def kernel(
    step_ref, s_ref, a_ref, m_ref, wi_ref, wo_ref, out_ref,
    sbuf, abuf, mbuf, m1, m2, mrecv, modall, win, wout, pref, frecv,
    stat, statr, xall, hid, obs, obr, part, rss, rsr, dsend, drecv, fsend,
    send, recv,
):
    y = lax.axis_index("tm")
    row = lax.axis_index("row")
    col = lax.axis_index("col")
    l, c = row // 2, lax.rem(row, 2)
    h, x = col // 4, lax.rem(col, 4)
    z = 4 * h + l

    def dev(x_=None, y_=None, z_=None, c_=None):
        x_ = x if x_ is None else x_
        y_ = y if y_ is None else y_
        z_ = z if z_ is None else z_
        c_ = c if c_ is None else c_
        return (y_, 2 * lax.rem(z_, 4) + c_, 4 * (z_ // 4) + x_)

    def xo(k):
        return lax.rem(x + k + 4, 4)

    def yo(k):
        return lax.rem(y + k + 4, 4)

    def zo(k):
        return lax.rem(z + k + 8, 8)

    sib = dev(c_=1 - c)
    z4 = dev(z_=zo(4))
    z4sib = dev(z_=zo(4), c_=1 - c)

    def lo(k):
        return dev(z_=4 * h + lax.rem(l + k, 4))

    ids = iter(range(COPIES))
    pending = []

    def remote(src, dst, ss, rs, to):
        return pltpu.make_async_remote_copy(
            src_ref=src, dst_ref=dst, send_sem=send.at[ss], recv_sem=recv.at[rs],
            device_id=to, device_id_type=MESH,
        )

    def put(k, src, dst, to):
        copy = remote(src, dst, k, k, to)
        copy.start()
        pending.append(copy)

    def got(k, dst):
        remote(dst, dst, k, k, sib).wait_recv()

    partners = [sib, z4, z4sib, dev(z_=zo(1)), dev(z_=zo(-1))]
    partners += [dev(x_=xo(k)) for k in (1, 2, 3)]
    partners += [dev(y_=yo(k)) for k in (1, 2, 3)]
    partners += [lo(k) for k in (1, 2, 3)]
    barrier = pltpu.get_barrier_semaphore()
    for p in partners:
        pl.semaphore_signal(barrier, inc=1, device_id=p, device_id_type=MESH)
    half = lax.rem(x, 2)
    same = x // 2 == c
    swap = [dev(x_=2 * c + i, c_=x // 2) for i in range(2)]
    swap_y = {(i, k): dev(x_=2 * c + i, c_=x // 2, y_=yo(k)) for i in range(2) for k in (1, 2, 3)}
    for p in swap_y.values():
        pl.semaphore_signal(barrier, inc=1, device_id=p, device_id_type=MESH)
    own = [jnp.logical_and(same, half == i) for i in range(2)]
    for i in range(2):

        @pl.when(jnp.logical_not(own[i]))
        def _(i=i):
            pl.semaphore_signal(barrier, inc=1, device_id=swap[i], device_id_type=MESH)

    pl.semaphore_wait(barrier, len(partners) + len(swap_y) + 2 - same.astype(jnp.int32))

    swaps = []

    def swap_out(src_of, dst):
        ks = (next(ids), next(ids))
        for i in range(2):

            @pl.when(own[i])
            def _(i=i):
                pltpu.make_async_copy(src_of(i), dst.at[half], recv.at[ks[0] + half]).start()

            @pl.when(jnp.logical_not(own[i]))
            def _(i=i):
                remote(src_of(i), dst.at[half], ks[i], ks[0] + half, swap[i]).start()

        swaps.append((ks, src_of, dst))
        return ks

    def swap_in(ks, dst):
        for i in range(2):
            got(ks[i], dst.at[i])

    ks_state = swap_out(lambda i: s_ref.at[pl.ds(T * i, T)], sbuf)

    mbuf[...] = jnp.zeros_like(mbuf)
    mbuf[0:3, :] = m_ref[...]
    k_ms = next(ids)
    put(k_ms, mbuf, mrecv.at[0], sib)

    mine = 4 * h + x
    far = 4 * (1 - h)

    def win_slot(hx, first=0, rows=W):
        return win.at[pl.ds(pl.multiple_of(hx * W + first, 16), rows), :]

    def wout_slot(hx, first=0, rows=U):
        return wout.at[
            hx // 2, pl.ds(pl.multiple_of(first, 16), rows), pl.ds(pl.multiple_of(lax.rem(hx, 2) * W, 128), W)
        ]

    def wi_part(hd, first, rows):
        return wi_ref.at[pl.ds(pl.multiple_of(first, 16), rows), pl.ds(pl.multiple_of(hd * U, 128), U)]

    def wo_part(hd, first, rows):
        return wo_ref.at[pl.ds(pl.multiple_of(hd * U + first, 16), rows), :]

    sides = ((wi_part, win_slot, W), (wo_part, wout_slot, U))
    ids_w = []
    local = [None, None]
    for part_of, slot_of, rows in sides:
        k_x = {k: next(ids) for k in (1, 3)}
        k_fwd = {k: next(ids) for k in (1, 3)}
        k_z = next(ids)
        k_xq = {k: next(ids) for k in (1, 2, 3)}
        k_y = {(s, k, f): next(ids) for s in range(4) for k in (1, 3) for f in range(2)}
        k_own = next(ids)
        ids_w.append((k_x, k_fwd, k_z, k_xq, k_y, k_own))

    def far_start(w):
        part_of, slot_of, rows = sides[w]
        k_x, k_fwd, k_z, k_xq, k_y, k_own = ids_w[w]
        q = rows // 4
        put(k_z, part_of(1 - h, y * q, q), slot_of(mine, y * q, q), z4)

    def near_start(w):
        part_of, slot_of, rows = sides[w]
        k_x, k_fwd, k_z, k_xq, k_y, k_own = ids_w[w]
        for k in (1, 3):
            put(k_x[k], part_of(h, 0, rows), slot_of(mine), dev(x_=xo(k)))
        copy = pltpu.make_async_copy(part_of(h, 0, rows), slot_of(mine), recv.at[k_own])
        copy.start()
        local[w] = copy

    def weight_far(w):
        part_of, slot_of, rows = sides[w]
        k_x, k_fwd, k_z, k_xq, k_y, k_own = ids_w[w]
        q = rows // 4
        here = slot_of(far + x, y * q, q)
        got(k_z, here)
        for k in (2, 1, 3):
            put(k_xq[k], here, here, dev(x_=xo(k)))
        for k in (1, 3):
            put(k_y[0, k, 0], here, here, dev(y_=yo(k)))

    def weight_far_x(w, s):
        part_of, slot_of, rows = sides[w]
        k_x, k_fwd, k_z, k_xq, k_y, k_own = ids_w[w]
        q = rows // 4
        here = slot_of(far + xo(-s), y * q, q)
        got(k_xq[s], here)
        for k in (1, 3):
            put(k_y[s, k, 0], here, here, dev(y_=yo(k)))

    def weight_far_y(w, s):
        part_of, slot_of, rows = sides[w]
        k_x, k_fwd, k_z, k_xq, k_y, k_own = ids_w[w]
        q = rows // 4
        for k, first in ((1, 0), (3, q // 2)):
            got(k_y[s, k, 0], slot_of(far + xo(-s), yo(-k) * q, q))
            there = slot_of(far + xo(-s), yo(-k) * q + first, q // 2)
            put(k_y[s, k, 1], there, there, dev(y_=yo(k)))

    def weight_near(w):
        part_of, slot_of, rows = sides[w]
        k_x, k_fwd, k_z, k_xq, k_y, k_own = ids_w[w]
        for k, first in ((1, 0), (3, rows // 2)):
            got(k_x[k], slot_of(4 * h + xo(-k)))
            there = slot_of(4 * h + xo(-k), first, rows // 2)
            put(k_fwd[k], there, there, dev(x_=xo(k)))

    def weight_end(w):
        part_of, slot_of, rows = sides[w]
        k_x, k_fwd, k_z, k_xq, k_y, k_own = ids_w[w]
        q = rows // 4
        for k, first in ((1, 0), (3, rows // 2)):
            got(k_fwd[k], slot_of(4 * h + xo(2), first, rows // 2))
        for s in range(4):
            for k, first in ((1, 0), (3, q // 2)):
                got(k_y[s, k, 1], slot_of(far + xo(-s), yo(2) * q + first, q // 2))
        local[w].wait()

    far_start(0)
    far_start(1)
    near_start(0)
    ks_anchor = swap_out(lambda i: a_ref.at[pl.ds(T * i, T)], abuf)

    def mod(j, r):
        return modall[2 * c + j, r : r + 1, :]

    sign = (1, -1)

    class Part:
        def __init__(self, it, p):
            self.it, self.p = it, p
            self.first, self.n = PARTS[p]
            self.x, self.hid, self.part = xall[p].at[it], hid[p], part[p]
            self.k_stat = [next(ids) for _ in range(3)]
            steps = [(s, g, j) for s in range(1, 5) for j in range(2) for g in range(2)]
            self.k_ring = {key: next(ids) for key in steps if key[0] < 4 or key[1] == key[2]}
            self.k_sib = {key: next(ids) for key in self.k_ring}
            self.k_own = [next(ids) for _ in range(2)]
            self.k_half = [next(ids) for _ in range(2)]
            self.k_sum = {key: next(ids) for key in steps if key[0] > 1 or key[1] == key[2]}
            self.k_prefix = {i: next(ids) for i in (1, 2, 3)}

        def rows(self):
            return slice(self.first, self.first + self.n)

        def stats(self, cur):
            self.cur = cur
            own, there = stat[self.p].at[self.it], statr[self.p].at[self.it]
            total = sum(jnp.sum(v, axis=1, keepdims=True) for v in cur)
            squares = sum(jnp.sum(v * v, axis=1, keepdims=True) for v in cur)
            lane = lax.broadcasted_iota(jnp.int32, (self.n, 128), 1)
            own[...] = jnp.where(lane < 64, total, squares)
            for i, to in enumerate((z4, z4sib, sib)):
                put(self.k_stat[i], own, there.at[i], to)

        def slot(self, zz, cc, j):
            hh, ll = zz // 4, lax.rem(zz, 4)
            return self.x.at[
                pl.ds(pl.multiple_of(ll * self.n, 16), self.n),
                pl.ds(pl.multiple_of((4 * hh + 2 * cc + j) * W, 128), W),
            ]

        def normalise(self):
            own, there = stat[self.p].at[self.it], statr[self.p].at[self.it]
            for i, k in enumerate(self.k_stat):
                got(k, there.at[i])
            total = own[...] + there[0] + there[1] + there[2]
            mean = total[:, 0:1] / D
            var = total[:, 64:65] / D - mean * mean
            scale = lax.rsqrt(var + EPSILON)
            for j in range(2):
                value = (self.cur[j] - mean) * scale * (1.0 + mod(j, 1)) + mod(j, 0)
                slot = self.slot(z, c, j)
                slot[...] = value.astype(BF16)
                for g in range(2):
                    put(self.k_ring[1, g, j], slot, slot, dev(z_=zo(sign[g])))
                put(self.k_own[j], slot, slot, sib)

        def gather(self, s):
            for j in range(2):
                for g in range(2):
                    if (s, g, j) not in self.k_ring:
                        continue
                    slot = self.slot(zo(-sign[g] * s), c, j)
                    got(self.k_ring[s, g, j], slot)
                    if (s + 1, g, j) in self.k_ring:
                        put(self.k_ring[s + 1, g, j], slot, slot, dev(z_=zo(sign[g])))
                    put(self.k_sib[s, g, j], slot, slot, sib)

        def gathered(self):
            for j in range(2):
                got(self.k_own[j], self.slot(z, 1 - c, j))
            for (s, g, j), k in self.k_sib.items():
                got(k, self.slot(zo(-sign[g] * s), 1 - c, j))

        def first_matmul(self):
            def tile(n, _):
                cols = pl.ds(pl.multiple_of(n * 256, 256), 256)
                pre = jnp.dot(self.x[...], win[:, cols], preferred_element_type=F32)
                self.hid[:, cols] = jax.nn.gelu(pre, approximate=True).astype(BF16)
                return 0

            lax.fori_loop(0, U // 256, tile, 0)

        def second_other(self):
            there, back = obs[self.p].at[self.it], obr[self.p].at[self.it]
            for hh in range(2):

                def tile(n, _, hh=hh):
                    cols = pl.ds(pl.multiple_of(n * 256, 256), 256)
                    other = jnp.dot(self.hid[...], wout[2 * hh + 1 - c, :, cols], preferred_element_type=F32)
                    there[hh, :, cols] = other.astype(BF16)
                    return 0

                lax.fori_loop(0, 3, tile, 0)
                put(self.k_half[hh], there.at[hh], back.at[hh], sib)

        def second_own(self):
            for hh in range(2):

                def tile(n, _, hh=hh):
                    cols = pl.ds(pl.multiple_of(n * 256, 256), 256)
                    kept = jnp.dot(self.hid[...], wout[2 * hh + c, :, cols], preferred_element_type=F32)
                    self.part[hh, :, :, cols] = kept.reshape(4, self.n, 256)
                    return 0

                lax.fori_loop(0, 3, tile, 0)

        def halves(self):
            back = obr[self.p].at[self.it]
            for hh in range(2):
                got(self.k_half[hh], back.at[hh])
                self.part[hh] += back[hh].astype(F32).reshape(4, self.n, 2 * W)

        def term(self, d, j):
            return self.part[d // 4, lax.rem(d, 4), :, W * j : W * (j + 1)]

        def scatter(self, s):
            out, back = rss[self.p].at[self.it], rsr[self.p].at[self.it]
            for j in range(2):
                for g in range(2):
                    if (s, g, j) not in self.k_sum:
                        continue
                    value = self.term(zo(sign[g] * (5 - s)), j)
                    if (s - 1, g, j) in self.k_sum:
                        got(self.k_sum[s - 1, g, j], back.at[s - 2, g, j])
                        value = value + back[s - 2, g, j].astype(F32)
                    out[s - 1, g, j] = value.astype(BF16)
                    put(self.k_sum[s, g, j], out.at[s - 1, g, j], back.at[s - 1, g, j], dev(z_=zo(sign[g])))

        def scattered(self):
            back = rsr[self.p].at[self.it]
            self.drift = []
            for j in range(2):
                value = self.term(z, j)
                for g in range(2):
                    got(self.k_sum[4, g, j], back.at[3, g, j])
                    value = value + back[3, g, j].astype(F32)
                self.drift.append(step_ref[0] * mod(j, 2) * value)

        def prefix_copy(self, i):
            return remote(
                dsend[self.p], drecv[self.p].at[i - 1], self.k_prefix[i], self.k_prefix[i], dev(y_=yo(i))
            )

        def prefix_send(self):
            for j in range(2):
                dsend[self.p][j] = self.drift[j].astype(BF16)
            for i in (1, 2, 3):

                @pl.when(y + i < 4)
                def _(i=i):
                    self.prefix_copy(i).start()

        def prefix_add(self):
            pref[:, self.rows(), :] = jnp.zeros((2, self.n, W), F32)
            for i in (3, 2, 1):

                @pl.when(y - i >= 0)
                def _(i=i):
                    got(self.k_prefix[i], drecv[self.p].at[i - 1])
                    for j in range(2):
                        pref[j, self.rows(), :] += drecv[self.p][i - 1, j].astype(F32)

        def prefix_sent(self):
            for i in (1, 2, 3):

                @pl.when(y + i < 4)
                def _(i=i):
                    self.prefix_copy(i).wait_send()

        def current(self):
            return [abuf[j, self.rows(), :] + pref[j, self.rows(), :] for j in range(2)]

        def out_copy(self, k, i):
            there = frecv.at[k, half, pl.ds(self.first, self.n)]
            to = swap[i] if k == 0 else swap_y[i, k]
            return remote(fsend[self.p].at[i], there, self.k_out[k, i], self.k_out[k, 0] + half, to)

        def out_send(self):
            self.k_out = {(k, i): next(ids) for k in range(4) for i in range(2)}
            for i in range(2):
                fsend[self.p][i] = self.drift[i].astype(BF16)
            for k in (3, 2, 1, 0):
                for i in range(2):
                    if k:

                        @pl.when(y + k < 4)
                        def _(i=i, k=k):
                            self.out_copy(k, i).start()

                    else:
                        there = frecv.at[0, half, pl.ds(self.first, self.n)]

                        @pl.when(own[i])
                        def _(i=i):
                            pltpu.make_async_copy(
                                fsend[self.p].at[i], there, recv.at[self.k_out[0, 0] + half]
                            ).start()

                        @pl.when(jnp.logical_not(own[i]))
                        def _(i=i):
                            self.out_copy(0, i).start()

        def out_sent(self):
            for k in range(4):
                for i in range(2):

                    @pl.when(y + k < 4 if k else jnp.logical_not(own[i]))
                    def _(i=i, k=k):
                        self.out_copy(k, i).wait_send()

        def out_add(self):
            for i in range(2):
                rows = slice(T * i + self.first, T * i + self.first + self.n)
                out_ref[rows, :] = a_ref[rows, :]
                for k in (3, 2, 1, 0):

                    @pl.when(y - k >= 0)
                    def _(i=i, k=k):
                        got(self.k_out[k, i], frecv.at[k, i, pl.ds(self.first, self.n)])
                        out_ref[rows, :] += frecv[k, i, self.rows(), :].astype(F32)

    parts = [[Part(it, p) for p in range(2)] for it in range(ITERS)]
    a, b = parts[0]

    swap_in(ks_state, sbuf)
    for v in (a, b):
        v.stats([sbuf[j, v.rows(), :] for j in range(2)])
    got(k_ms, mrecv.at[0])
    m1[...] = mbuf[...] + mrecv[0]
    k_ml = {k: next(ids) for k in (1, 2, 3)}
    for k in (1, 2, 3):
        put(k_ml[k], m1, mrecv.at[k], lo(k))
    weight_far(0)
    for k in (1, 2, 3):
        got(k_ml[k], mrecv.at[k])
    m2[...] = m1[...] + mrecv[1] + mrecv[2] + mrecv[3]
    k_mx = {k: next(ids) for k in (1, 2, 3)}
    for k in (1, 2, 3):
        put(k_mx[k], m2, modall.at[x], dev(x_=xo(k)))
    modall[x] = m2[...]
    weight_far(1)
    near_start(1)
    for k in (1, 2, 3):
        got(k_mx[k], modall.at[xo(-k)])
    for v in (a, b):
        v.normalise()
    weight_near(0)
    weight_far_y(0, 0)
    for v in (a, b):
        v.gather(1)
    weight_far_x(0, 1)
    weight_far_x(0, 3)
    weight_far_y(1, 0)
    for v in (a, b):
        v.gather(2)
    weight_far_x(0, 2)
    weight_far_x(1, 1)
    weight_far_x(1, 3)
    weight_far_y(0, 1)
    for v in (a, b):
        v.gather(3)
    weight_far_y(0, 3)
    weight_far_x(1, 2)
    weight_far_y(0, 2)
    for v in (a, b):
        v.gather(4)
    weight_near(1)
    weight_far_y(1, 1)
    weight_far_y(1, 3)
    swap_in(ks_anchor, abuf)
    a.gathered()
    b.gathered()
    weight_far_y(1, 2)
    weight_end(0)
    a.first_matmul()
    b.first_matmul()
    weight_end(1)
    for it in range(ITERS):
        a, b = parts[it]
        if it:
            a.gathered()
            a.first_matmul()
        a.second_other()
        a.second_own()
        if it:
            b.gather(4)
            b.gathered()
        a.halves()
        a.scatter(1)
        if it:
            b.first_matmul()
        b.second_other()
        a.scatter(2)
        b.second_own()
        b.halves()
        b.scatter(1)
        a.scatter(3)
        b.scatter(2)
        a.scatter(4)
        b.scatter(3)
        a.scattered()
        if it + 1 == ITERS:
            a.out_send()
            b.scatter(4)
            b.scattered()
            b.out_send()
            a.out_add()
            b.out_add()
            continue
        a.prefix_send()
        b.scatter(4)
        b.scattered()
        b.prefix_send()
        c1, d1 = parts[it + 1]
        a.prefix_add()
        c1.stats(a.current())
        b.prefix_add()
        d1.stats(b.current())
        c1.normalise()
        d1.normalise()
        for s in range(1, 4):
            c1.gather(s)
            d1.gather(s)
        c1.gather(4)

    for copy in pending:
        copy.wait_send()
    for v in parts[0]:
        v.prefix_sent()
    for v in parts[1]:
        v.out_sent()
    for ks, src_of, dst in swaps:
        for i in range(2):

            @pl.when(jnp.logical_not(own[i]))
            def _(i=i):
                remote(src_of(i), dst.at[half], ks[i], ks[0] + half, swap[i]).wait_send()


def local(states, anchor, timesteps, step_sizes, weight_in, weight_out, mod_weight):
    embedding = timestep_embedding(timesteps)[0]
    rows_here = mod_weight.shape[0]
    embed_part = lax.dynamic_slice_in_dim(
        embedding, lax.axis_index("row") * rows_here, rows_here, 0
    )
    mod_part = jnp.einsum(
        "e,ekd->kd", embed_part, mod_weight.astype(jnp.float32), precision=lax.Precision.HIGHEST
    )
    vmem = pl.BlockSpec(memory_space=pltpu.VMEM)

    def each(make):
        return [make(n) for _, n in PARTS]

    scratch = [
        pltpu.VMEM((2, T, W), F32),
        pltpu.VMEM((2, T, W), F32),
        pltpu.VMEM((8, W), F32),
        pltpu.VMEM((8, W), F32),
        pltpu.VMEM((8, W), F32),
        pltpu.VMEM((4, 8, W), F32),
        pltpu.VMEM((4, 8, W), F32),
        pltpu.VMEM((D, U), BF16),
        pltpu.VMEM((4, U, 2 * W), BF16),
        pltpu.VMEM((2, T, W), F32),
        pltpu.VMEM((4, 2, T, W), BF16),
        each(lambda n: pltpu.VMEM((ITERS, n, 128), F32)),
        each(lambda n: pltpu.VMEM((ITERS, 3, n, 128), F32)),
        each(lambda n: pltpu.VMEM((ITERS, 4 * n, D), BF16)),
        each(lambda n: pltpu.VMEM((4 * n, U), BF16)),
        each(lambda n: pltpu.VMEM((ITERS, 2, 4 * n, 2 * W), BF16)),
        each(lambda n: pltpu.VMEM((ITERS, 2, 4 * n, 2 * W), BF16)),
        each(lambda n: pltpu.VMEM((2, 4, n, 2 * W), F32)),
        each(lambda n: pltpu.VMEM((ITERS, 4, 2, 2, n, W), BF16)),
        each(lambda n: pltpu.VMEM((ITERS, 4, 2, 2, n, W), BF16)),
        each(lambda n: pltpu.VMEM((2, n, W), BF16)),
        each(lambda n: pltpu.VMEM((3, 2, n, W), BF16)),
        each(lambda n: pltpu.VMEM((2, n, W), BF16)),
        pltpu.SemaphoreType.DMA((COPIES,)),
        pltpu.SemaphoreType.DMA((COPIES,)),
    ]
    out = pl.pallas_call(
        kernel,
        out_shape=jax.ShapeDtypeStruct(anchor.shape, F32),
        in_specs=[pl.BlockSpec(memory_space=pltpu.SMEM), vmem, vmem, vmem]
        + [pl.BlockSpec(memory_space=pl.ANY)] * 2,
        out_specs=vmem,
        scratch_shapes=scratch,
        compiler_params=pltpu.CompilerParams(
            collective_id=0, has_side_effects=True, vmem_limit_bytes=60 << 20
        ),
        name="picard",
    )(step_sizes, states[0], anchor, mod_part, weight_in, weight_out)
    return out[None]


def solution(mesh):
    placed = (
        P("tm", "row", "col"),
        P("row", "col"),
        P("tm"),
        P("tm"),
        P("col", "row"),
        P("row", "col"),
        P("row", None, "col"),
    )
    return jax.shard_map(
        local, mesh=mesh, in_specs=placed, out_specs=P("tm", "row", "col"), check_vma=False
    )
```

```python
import math

import jax
import jax.numpy as jnp
from jax import lax
from jax.experimental import pallas as pl
from jax.experimental.pallas import tpu as pltpu
from jax.sharding import PartitionSpec as P

D = 3072
ITERS = 2
EPSILON = 1e-06
MESH = pl.DeviceIdType.MESH
F32 = jnp.float32
BF16 = jnp.bfloat16

T = 80
W = 384
U = 768

PARTS = ((0, 48), (48, 32))

UNITS = ((0, 256), (256, 128))
COPIES = 400


def timestep_embedding(timesteps):
    half_width = D // 2
    positions = jnp.arange(half_width, dtype=jnp.float32)
    frequency = jnp.exp(-math.log(10000.0) * positions / half_width)
    phases = timesteps.astype(jnp.float32)[:, None] * frequency[None, :]
    return jnp.concatenate([jnp.cos(phases), jnp.sin(phases)], axis=1)


def kernel(
    step_ref, s_ref, a_ref, m_ref, wi_ref, wo_ref, out_ref,
    sbuf, abuf, mbuf, m1, m2, mrecv, modall, win, wout, pref, frecv,
    stat, statr, xall, hid, obs, obr, part, rss, rsr, dsend, drecv, fsend, drift,
    send, recv,
):
    y = lax.axis_index("tm")
    row = lax.axis_index("row")
    col = lax.axis_index("col")
    l, c = row // 2, lax.rem(row, 2)
    h, x = col // 4, lax.rem(col, 4)
    z = 4 * h + l

    def dev(x_=None, y_=None, z_=None, c_=None):
        x_ = x if x_ is None else x_
        y_ = y if y_ is None else y_
        z_ = z if z_ is None else z_
        c_ = c if c_ is None else c_
        return (y_, 2 * lax.rem(z_, 4) + c_, 4 * (z_ // 4) + x_)

    def xo(k):
        return lax.rem(x + k + 4, 4)

    def yo(k):
        return lax.rem(y + k + 4, 4)

    def zo(k):
        return lax.rem(z + k + 8, 8)

    sib = dev(c_=1 - c)
    z4 = dev(z_=zo(4))
    z4sib = dev(z_=zo(4), c_=1 - c)

    def lo(k):
        return dev(z_=4 * h + lax.rem(l + k, 4))

    ids = iter(range(COPIES))
    pending = []

    def remote(src, dst, ss, rs, to):
        return pltpu.make_async_remote_copy(
            src_ref=src, dst_ref=dst, send_sem=send.at[ss], recv_sem=recv.at[rs],
            device_id=to, device_id_type=MESH,
        )

    def put(k, src, dst, to):
        copy = remote(src, dst, k, k, to)
        copy.start()
        pending.append(copy)

    def got(k, dst):
        remote(dst, dst, k, k, sib).wait_recv()

    partners = [sib, z4, z4sib, dev(z_=zo(1)), dev(z_=zo(-1))]
    partners += [dev(x_=xo(k)) for k in (1, 2, 3)]
    partners += [dev(y_=yo(k)) for k in (1, 2, 3)]
    partners += [lo(k) for k in (1, 2, 3)]
    barrier = pltpu.get_barrier_semaphore()
    for p in partners:
        pl.semaphore_signal(barrier, inc=1, device_id=p, device_id_type=MESH)
    half = lax.rem(x, 2)
    same = x // 2 == c
    swap = [dev(x_=2 * c + i, c_=x // 2) for i in range(2)]
    swap_y = {(i, k): dev(x_=2 * c + i, c_=x // 2, y_=yo(k)) for i in range(2) for k in (1, 2, 3)}
    for p in swap_y.values():
        pl.semaphore_signal(barrier, inc=1, device_id=p, device_id_type=MESH)
    own = [jnp.logical_and(same, half == i) for i in range(2)]
    for i in range(2):

        @pl.when(jnp.logical_not(own[i]))
        def _(i=i):
            pl.semaphore_signal(barrier, inc=1, device_id=swap[i], device_id_type=MESH)

    pl.semaphore_wait(barrier, len(partners) + len(swap_y) + 2 - same.astype(jnp.int32))

    swaps = []

    def swap_out(src_of, dst):
        ks = (next(ids), next(ids))
        for i in range(2):

            @pl.when(own[i])
            def _(i=i):
                pltpu.make_async_copy(src_of(i), dst.at[half], recv.at[ks[0] + half]).start()

            @pl.when(jnp.logical_not(own[i]))
            def _(i=i):
                remote(src_of(i), dst.at[half], ks[i], ks[0] + half, swap[i]).start()

        swaps.append((ks, src_of, dst))
        return ks

    def swap_in(ks, dst):
        for i in range(2):
            got(ks[i], dst.at[i])

    ks_state = swap_out(lambda i: s_ref.at[pl.ds(T * i, T)], sbuf)

    mbuf[...] = jnp.zeros_like(mbuf)
    mbuf[0:3, :] = m_ref[...]
    k_ms = next(ids)
    put(k_ms, mbuf, mrecv.at[0], sib)

    mine = 4 * h + x
    far = 4 * (1 - h)

    def win_side():
        def slot_of(hx, first=0, rows=W):
            return win.at[pl.ds(pl.multiple_of(hx * W + first, 16), rows), :]

        def part_of(hd, first, rows):
            return wi_ref.at[pl.ds(pl.multiple_of(first, 16), rows), pl.ds(pl.multiple_of(hd * U, 128), U)]

        return part_of, slot_of, W

    def wout_side(col, cols):
        def slot_of(hx, first=0, rows=U):
            return wout.at[
                hx // 2,
                pl.ds(pl.multiple_of(first, 16), rows),
                pl.ds(pl.multiple_of(lax.rem(hx, 2) * W + col, 128), cols),
            ]

        def part_of(hd, first, rows):
            return wo_ref.at[pl.ds(pl.multiple_of(hd * U + first, 16), rows), col : col + cols]

        return part_of, slot_of, U

    class Side:
        def __init__(self, part_of, slot_of, rows):
            self.part_of, self.slot_of, self.rows, self.q = part_of, slot_of, rows, rows // 4
            self.k_x = {k: next(ids) for k in (1, 3)}
            self.k_in = [next(ids) for _ in range(5)]
            self.k_y = {(s, k, f): next(ids) for s in range(5) for k in (1, 3) for f in range(2)}
            self.k_own = next(ids)

        def quarter(self, s, yy, first=0, rows=None):
            hx = 4 * h + xo(2) if s == 4 else far + xo(-s)
            return self.slot_of(hx, yy * self.q + first, rows or self.q)

        def far_start(self):
            put(self.k_in[0], self.part_of(1 - h, y * self.q, self.q), self.slot_of(mine, y * self.q, self.q), z4)

        def cross_start(self):
            to = dev(x_=xo(2))
            put(self.k_in[4], self.part_of(h, y * self.q, self.q), self.slot_of(mine, y * self.q, self.q), to)

        def near_start(self):
            for k in (1, 3):
                put(self.k_x[k], self.part_of(h, 0, self.rows), self.slot_of(mine), dev(x_=xo(k)))
            self.copy = pltpu.make_async_copy(self.part_of(h, 0, self.rows), self.slot_of(mine), recv.at[self.k_own])
            self.copy.start()

        def arrive(self, s):
            here = self.quarter(s, y)
            got(self.k_in[s], here)
            if s == 0:
                for k in (2, 1, 3):
                    put(self.k_in[k], here, here, dev(x_=xo(k)))
            for k in (1, 3):
                put(self.k_y[s, k, 0], here, here, dev(y_=yo(k)))

        def spread(self, s):
            for k, first in ((1, 0), (3, self.q // 2)):
                got(self.k_y[s, k, 0], self.quarter(s, yo(-k)))
                there = self.quarter(s, yo(-k), first, self.q // 2)
                put(self.k_y[s, k, 1], there, there, dev(y_=yo(k)))

        def end(self):
            for k in (1, 3):
                got(self.k_x[k], self.slot_of(4 * h + xo(-k)))
            for s in range(5):
                for k, first in ((1, 0), (3, self.q // 2)):
                    got(self.k_y[s, k, 1], self.quarter(s, yo(2), first, self.q // 2))
            self.copy.wait()

    w_in = Side(*win_side())
    w_a, w_b = (Side(*wout_side(*unit)) for unit in UNITS)
    w_in.cross_start()
    w_in.far_start()
    w_in.near_start()
    w_a.far_start()
    w_a.cross_start()
    w_b.far_start()

    def mod(j, r):
        return modall[2 * c + j, r : r + 1, :]

    sign = (1, -1)

    class Part:
        def __init__(self, it, p):
            self.it, self.p = it, p
            self.first, self.n = PARTS[p]
            self.x, self.hid, self.part = xall[p].at[it], hid[p], part[p]
            self.k_stat = [next(ids) for _ in range(3)]
            steps = [(s, g, j) for s in range(1, 5) for j in range(2) for g in range(2)]
            self.k_ring = {key: next(ids) for key in steps if key[0] < 4 or key[1] == key[2]}
            self.k_sib = {key: next(ids) for key in self.k_ring}
            self.k_own = [next(ids) for _ in range(2)]
            self.units = ((0, W),) if it else UNITS
            self.k_half = {(u, hh): next(ids) for u in self.units for hh in range(2)}
            self.k_sum = {
                u: {key: next(ids) for key in steps if key[0] > 1 or key[1] == key[2]} for u in self.units
            }
            self.k_prefix = {i: next(ids) for i in (1, 2, 3)}

        def rows(self):
            return slice(self.first, self.first + self.n)

        def stats(self, cur):
            self.cur = cur
            own, there = stat[self.p].at[self.it], statr[self.p].at[self.it]
            total = sum(jnp.sum(v, axis=1, keepdims=True) for v in cur)
            squares = sum(jnp.sum(v * v, axis=1, keepdims=True) for v in cur)
            lane = lax.broadcasted_iota(jnp.int32, (self.n, 128), 1)
            own[...] = jnp.where(lane < 64, total, squares)
            for i, to in enumerate((z4, z4sib, sib)):
                put(self.k_stat[i], own, there.at[i], to)

        def slot(self, zz, cc, j):
            hh, ll = zz // 4, lax.rem(zz, 4)
            return self.x.at[
                pl.ds(pl.multiple_of(ll * self.n, 16), self.n),
                pl.ds(pl.multiple_of((4 * hh + 2 * cc + j) * W, 128), W),
            ]

        def normalise(self):
            own, there = stat[self.p].at[self.it], statr[self.p].at[self.it]
            for i, k in enumerate(self.k_stat):
                got(k, there.at[i])
            total = own[...] + there[0] + there[1] + there[2]
            mean = total[:, 0:1] / D
            var = total[:, 64:65] / D - mean * mean
            scale = lax.rsqrt(var + EPSILON)
            for j in range(2):
                value = (self.cur[j] - mean) * scale * (1.0 + mod(j, 1)) + mod(j, 0)
                slot = self.slot(z, c, j)
                slot[...] = value.astype(BF16)
                for g in range(2):
                    put(self.k_ring[1, g, j], slot, slot, dev(z_=zo(sign[g])))
                put(self.k_own[j], slot, slot, sib)

        def gather(self, s):
            for j in range(2):
                for g in range(2):
                    if (s, g, j) not in self.k_ring:
                        continue
                    slot = self.slot(zo(-sign[g] * s), c, j)
                    got(self.k_ring[s, g, j], slot)
                    if (s + 1, g, j) in self.k_ring:
                        put(self.k_ring[s + 1, g, j], slot, slot, dev(z_=zo(sign[g])))
                    put(self.k_sib[s, g, j], slot, slot, sib)

        def gathered(self):
            for j in range(2):
                got(self.k_own[j], self.slot(z, 1 - c, j))
            for (s, g, j), k in self.k_sib.items():
                got(k, self.slot(zo(-sign[g] * s), 1 - c, j))

        def first_matmul(self):
            def tile(n, _):
                cols = pl.ds(pl.multiple_of(n * 256, 256), 256)
                pre = jnp.dot(self.x[...], win[:, cols], preferred_element_type=F32)
                self.hid[:, cols] = jax.nn.gelu(pre, approximate=True).astype(BF16)
                return 0

            lax.fori_loop(0, U // 256, tile, 0)

        def tiles(self, u):
            if u[1] < W:
                return [(j, u[0], u[1]) for j in range(2)]
            return [(None, 256 * n, 256) for n in range(3)]

        def second(self, cc, hh, u):
            for j, col, cols in self.tiles(u):
                at = col if j is None else W * j + col
                yield at, cols, jnp.dot(self.hid[...], wout[2 * hh + cc, :, at : at + cols], preferred_element_type=F32)

        def second_other(self, u):
            there, back = obs[self.p].at[self.it], obr[self.p].at[self.it]
            for hh in range(2):
                for at, cols, value in self.second(1 - c, hh, u):
                    for j, col in ((n // 3, n % 3 * 128) for n in range(at // 128, (at + cols) // 128)):
                        first = W * j + col - at
                        there[hh, j, :, col : col + 128] = value[:, first : first + 128].astype(BF16)
                cols = slice(u[0], u[0] + u[1])
                put(self.k_half[u, hh], there.at[hh, :, :, cols], back.at[hh, :, :, cols], sib)

        def second_own(self, u):
            for hh in range(2):
                for at, cols, value in self.second(c, hh, u):
                    self.part[hh, :, :, at : at + cols] = value.reshape(4, self.n, cols)

        def halves(self, u):
            back = obr[self.p].at[self.it]
            cols = slice(u[0], u[0] + u[1])
            for hh in range(2):
                got(self.k_half[u, hh], back.at[hh, :, :, cols])
                for j in range(2):
                    at = slice(W * j + u[0], W * j + u[0] + u[1])
                    self.part[hh, :, :, at] += back[hh, j, :, cols].astype(F32).reshape(4, self.n, u[1])

        def term(self, d, j, u):
            return self.part[d // 4, lax.rem(d, 4), :, W * j + u[0] : W * j + u[0] + u[1]]

        def scatter(self, s, u):
            k = self.k_sum[u]
            cols = slice(u[0], u[0] + u[1])
            out, back = rss[self.p].at[self.it], rsr[self.p].at[self.it]
            for j in range(2):
                for g in range(2):
                    if (s, g, j) not in k:
                        continue
                    value = self.term(zo(sign[g] * (5 - s)), j, u)
                    if (s - 1, g, j) in k:
                        got(k[s - 1, g, j], back.at[s - 2, g, j, :, cols])
                        value = value + back[s - 2, g, j, :, cols].astype(F32)
                    out[s - 1, g, j, :, cols] = value.astype(BF16)
                    here, there = out.at[s - 1, g, j, :, cols], back.at[s - 1, g, j, :, cols]
                    put(k[s, g, j], here, there, dev(z_=zo(sign[g])))

        def scattered(self, u):
            k = self.k_sum[u]
            cols = slice(u[0], u[0] + u[1])
            back = rsr[self.p].at[self.it]
            for j in range(2):
                value = self.term(z, j, u)
                for g in range(2):
                    got(k[4, g, j], back.at[3, g, j, :, cols])
                    value = value + back[3, g, j, :, cols].astype(F32)
                drift[self.p][j, :, cols] = step_ref[0] * mod(j, 2)[:, cols] * value

        def prefix_copy(self, i):
            return remote(
                dsend[self.p], drecv[self.p].at[i - 1], self.k_prefix[i], self.k_prefix[i], dev(y_=yo(i))
            )

        def prefix_send(self):
            for j in range(2):
                dsend[self.p][j] = drift[self.p][j].astype(BF16)
            for i in (1, 2, 3):

                @pl.when(y + i < 4)
                def _(i=i):
                    self.prefix_copy(i).start()

        def prefix_add(self):
            pref[:, self.rows(), :] = jnp.zeros((2, self.n, W), F32)
            for i in (3, 2, 1):

                @pl.when(y - i >= 0)
                def _(i=i):
                    got(self.k_prefix[i], drecv[self.p].at[i - 1])
                    for j in range(2):
                        pref[j, self.rows(), :] += drecv[self.p][i - 1, j].astype(F32)

        def prefix_sent(self):
            for i in (1, 2, 3):

                @pl.when(y + i < 4)
                def _(i=i):
                    self.prefix_copy(i).wait_send()

        def current(self):
            return [abuf[j, self.rows(), :] + pref[j, self.rows(), :] for j in range(2)]

        def out_copy(self, k, i):
            there = frecv.at[k, half, pl.ds(self.first, self.n)]
            to = swap[i] if k == 0 else swap_y[i, k]
            return remote(fsend[self.p].at[i], there, self.k_out[k, i], self.k_out[k, 0] + half, to)

        def out_send(self):
            self.k_out = {(k, i): next(ids) for k in range(4) for i in range(2)}
            for i in range(2):
                fsend[self.p][i] = drift[self.p][i].astype(BF16)
            for k in (3, 2, 1, 0):
                for i in range(2):
                    if k:

                        @pl.when(y + k < 4)
                        def _(i=i, k=k):
                            self.out_copy(k, i).start()

                    else:
                        there = frecv.at[0, half, pl.ds(self.first, self.n)]

                        @pl.when(own[i])
                        def _(i=i):
                            pltpu.make_async_copy(
                                fsend[self.p].at[i], there, recv.at[self.k_out[0, 0] + half]
                            ).start()

                        @pl.when(jnp.logical_not(own[i]))
                        def _(i=i):
                            self.out_copy(0, i).start()

        def out_sent(self):
            for k in range(4):
                for i in range(2):

                    @pl.when(y + k < 4 if k else jnp.logical_not(own[i]))
                    def _(i=i, k=k):
                        self.out_copy(k, i).wait_send()

        def out_add(self):
            for i in range(2):
                rows = slice(T * i + self.first, T * i + self.first + self.n)
                out_ref[rows, :] = a_ref[rows, :]
                for k in (3, 2, 1, 0):

                    @pl.when(y - k >= 0)
                    def _(i=i, k=k):
                        got(self.k_out[k, i], frecv.at[k, i, pl.ds(self.first, self.n)])
                        out_ref[rows, :] += frecv[k, i, self.rows(), :].astype(F32)

    parts = [[Part(it, p) for p in range(2)] for it in range(ITERS)]
    a, b = parts[0]

    swap_in(ks_state, sbuf)
    for v in (a, b):
        v.stats([sbuf[j, v.rows(), :] for j in range(2)])
    w_in.arrive(4)
    got(k_ms, mrecv.at[0])
    m1[...] = mbuf[...] + mrecv[0]
    k_ml = {k: next(ids) for k in (1, 2, 3)}
    for k in (1, 2, 3):
        put(k_ml[k], m1, mrecv.at[k], lo(k))
    w_in.arrive(0)
    w_a.near_start()
    w_b.cross_start()
    for k in (1, 2, 3):
        got(k_ml[k], mrecv.at[k])
    m2[...] = m1[...] + mrecv[1] + mrecv[2] + mrecv[3]
    k_mx = {k: next(ids) for k in (1, 2, 3)}
    for k in (1, 2, 3):
        put(k_mx[k], m2, modall.at[x], dev(x_=xo(k)))
    modall[x] = m2[...]
    w_a.arrive(4)
    w_in.spread(4)
    for k in (1, 2, 3):
        got(k_mx[k], modall.at[xo(-k)])
    for v in (a, b):
        v.normalise()
    w_in.arrive(1)
    w_in.arrive(3)
    w_in.spread(0)
    for v in (a, b):
        v.gather(1)
    w_in.arrive(2)
    w_a.arrive(0)
    w_b.near_start()
    w_a.spread(4)
    for v in (a, b):
        v.gather(2)
    w_in.spread(1)
    w_in.spread(3)
    w_a.arrive(1)
    w_a.arrive(3)
    for v in (a, b):
        v.gather(3)
    w_in.spread(2)
    w_a.arrive(2)
    w_a.spread(0)
    w_b.arrive(4)
    w_b.arrive(0)
    for v in (a, b):
        v.gather(4)
    w_a.spread(1)
    w_a.spread(3)
    w_b.arrive(1)
    w_b.arrive(3)
    w_b.arrive(2)
    w_a.spread(2)
    w_b.spread(4)
    a.gathered()
    b.gathered()
    w_in.end()
    a.first_matmul()
    w_b.spread(0)
    b.first_matmul()
    w_b.spread(1)
    w_b.spread(3)
    ua, ub = UNITS
    w_a.end()
    for v in (a, b):
        v.second_other(ua)
    w_b.spread(2)
    for v in (a, b):
        v.second_own(ua)
    ks_anchor = swap_out(lambda i: a_ref.at[pl.ds(T * i, T)], abuf)
    for v in (a, b):
        v.halves(ua)
        v.scatter(1, ua)
    for v in (a, b):
        v.scatter(2, ua)
    w_b.end()
    a.second_other(ub)
    a.scatter(3, ua)
    a.second_own(ub)
    b.scatter(3, ua)
    b.second_other(ub)
    a.scatter(4, ua)
    b.second_own(ub)
    b.scatter(4, ua)
    for v in (a, b):
        v.halves(ub)
        v.scatter(1, ub)
    for s in (2, 3, 4):
        for v in (a, b):
            v.scatter(s, ub)
            if s == 2:
                v.scattered(ua)
    swap_in(ks_anchor, abuf)
    for v in (a, b):
        v.scattered(ub)
        v.prefix_send()
    e, f = parts[1]
    a.prefix_add()
    e.stats(a.current())
    b.prefix_add()
    f.stats(b.current())
    e.normalise()
    f.normalise()
    for s in range(1, 4):
        e.gather(s)
        f.gather(s)
    e.gather(4)
    e.gathered()
    u = (0, W)
    e.first_matmul()
    e.second_other(u)
    e.second_own(u)
    f.gather(4)
    f.gathered()
    e.halves(u)
    e.scatter(1, u)
    f.first_matmul()
    f.second_other(u)
    e.scatter(2, u)
    f.second_own(u)
    f.halves(u)
    f.scatter(1, u)
    e.scatter(3, u)
    f.scatter(2, u)
    e.scatter(4, u)
    f.scatter(3, u)
    e.scattered(u)
    e.out_send()
    f.scatter(4, u)
    f.scattered(u)
    f.out_send()
    e.out_add()
    f.out_add()

    for copy in pending:
        copy.wait_send()
    for v in parts[0]:
        v.prefix_sent()
    for v in parts[1]:
        v.out_sent()
    for ks, src_of, dst in swaps:
        for i in range(2):

            @pl.when(jnp.logical_not(own[i]))
            def _(i=i):
                remote(src_of(i), dst.at[half], ks[i], ks[0] + half, swap[i]).wait_send()


def local(states, anchor, timesteps, step_sizes, weight_in, weight_out, mod_weight):
    embedding = timestep_embedding(timesteps)[0]
    rows_here = mod_weight.shape[0]
    embed_part = lax.dynamic_slice_in_dim(
        embedding, lax.axis_index("row") * rows_here, rows_here, 0
    )
    mod_part = jnp.einsum(
        "e,ekd->kd", embed_part, mod_weight.astype(jnp.float32), precision=lax.Precision.HIGHEST
    )
    vmem = pl.BlockSpec(memory_space=pltpu.VMEM)

    def each(make):
        return [make(n) for _, n in PARTS]

    scratch = [
        pltpu.VMEM((2, T, W), F32),
        pltpu.VMEM((2, T, W), F32),
        pltpu.VMEM((8, W), F32),
        pltpu.VMEM((8, W), F32),
        pltpu.VMEM((8, W), F32),
        pltpu.VMEM((4, 8, W), F32),
        pltpu.VMEM((4, 8, W), F32),
        pltpu.VMEM((D, U), BF16),
        pltpu.VMEM((4, U, 2 * W), BF16),
        pltpu.VMEM((2, T, W), F32),
        pltpu.VMEM((4, 2, T, W), BF16),
        each(lambda n: pltpu.VMEM((ITERS, n, 128), F32)),
        each(lambda n: pltpu.VMEM((ITERS, 3, n, 128), F32)),
        each(lambda n: pltpu.VMEM((ITERS, 4 * n, D), BF16)),
        each(lambda n: pltpu.VMEM((4 * n, U), BF16)),
        each(lambda n: pltpu.VMEM((ITERS, 2, 2, 4 * n, W), BF16)),
        each(lambda n: pltpu.VMEM((ITERS, 2, 2, 4 * n, W), BF16)),
        each(lambda n: pltpu.VMEM((2, 4, n, 2 * W), F32)),
        each(lambda n: pltpu.VMEM((ITERS, 4, 2, 2, n, W), BF16)),
        each(lambda n: pltpu.VMEM((ITERS, 4, 2, 2, n, W), BF16)),
        each(lambda n: pltpu.VMEM((2, n, W), BF16)),
        each(lambda n: pltpu.VMEM((3, 2, n, W), BF16)),
        each(lambda n: pltpu.VMEM((2, n, W), BF16)),
        each(lambda n: pltpu.VMEM((2, n, W), F32)),
        pltpu.SemaphoreType.DMA((COPIES,)),
        pltpu.SemaphoreType.DMA((COPIES,)),
    ]
    out = pl.pallas_call(
        kernel,
        out_shape=jax.ShapeDtypeStruct(anchor.shape, F32),
        in_specs=[pl.BlockSpec(memory_space=pltpu.SMEM), vmem, vmem, vmem]
        + [pl.BlockSpec(memory_space=pl.ANY)] * 2,
        out_specs=vmem,
        scratch_shapes=scratch,
        compiler_params=pltpu.CompilerParams(
            collective_id=0, has_side_effects=True, vmem_limit_bytes=60 << 20
        ),
        name="picard",
    )(step_sizes, states[0], anchor, mod_part, weight_in, weight_out)
    return out[None]


def solution(mesh):
    placed = (
        P("tm", "row", "col"),
        P("row", "col"),
        P("tm"),
        P("tm"),
        P("col", "row"),
        P("row", "col"),
        P("row", None, "col"),
    )
    return jax.shard_map(
        local, mesh=mesh, in_specs=placed, out_specs=P("tm", "row", "col"), check_vma=False
    )
```

```python
import math

import jax
import jax.numpy as jnp
from jax import lax
from jax.experimental import pallas as pl
from jax.experimental.pallas import tpu as pltpu
from jax.sharding import PartitionSpec as P

D = 3072
ITERS = 2
EPSILON = 1e-06
MESH = pl.DeviceIdType.MESH
F32 = jnp.float32
BF16 = jnp.bfloat16

T = 80
W = 384
U = 768

PARTS = ((0, 48), (48, 32))

COPIES = 304


def timestep_embedding(timesteps):
    half_width = D // 2
    positions = jnp.arange(half_width, dtype=jnp.float32)
    frequency = jnp.exp(-math.log(10000.0) * positions / half_width)
    phases = timesteps.astype(jnp.float32)[:, None] * frequency[None, :]
    return jnp.concatenate([jnp.cos(phases), jnp.sin(phases)], axis=1)


def kernel(
    step_ref, s_ref, a_ref, m_ref, wi_ref, wo_ref, out_ref,
    sbuf, abuf, modx, msib, m1, mrecv, modall, win, wout, pref, frecv,
    stat, statr, xall, hid, obs, obr, part, rss, rsr, dsend, drecv, fsend, drift,
    send, recv,
):
    y = lax.axis_index("tm")
    row = lax.axis_index("row")
    col = lax.axis_index("col")
    l, c = row // 2, lax.rem(row, 2)
    h, x = col // 4, lax.rem(col, 4)
    z = 4 * h + l

    def dev(x_=None, y_=None, z_=None, c_=None):
        x_ = x if x_ is None else x_
        y_ = y if y_ is None else y_
        z_ = z if z_ is None else z_
        c_ = c if c_ is None else c_
        return (y_, 2 * lax.rem(z_, 4) + c_, 4 * (z_ // 4) + x_)

    def xo(k):
        return lax.rem(x + k + 4, 4)

    def yo(k):
        return lax.rem(y + k + 4, 4)

    def zo(k):
        return lax.rem(z + k + 8, 8)

    sib = dev(c_=1 - c)
    z4 = dev(z_=zo(4))
    z4sib = dev(z_=zo(4), c_=1 - c)

    def lo(k):
        return dev(z_=4 * h + lax.rem(l + k, 4))

    ids = iter(range(COPIES))
    pending = []

    def remote(src, dst, ss, rs, to):
        return pltpu.make_async_remote_copy(
            src_ref=src, dst_ref=dst, send_sem=send.at[ss], recv_sem=recv.at[rs],
            device_id=to, device_id_type=MESH,
        )

    def put(k, src, dst, to):
        copy = remote(src, dst, k, k, to)
        copy.start()
        pending.append(copy)

    def got(k, dst):
        remote(dst, dst, k, k, sib).wait_recv()

    partners = [sib, z4, z4sib, dev(z_=zo(1)), dev(z_=zo(-1))]
    partners += [dev(x_=xo(k)) for k in (1, 2, 3)]
    partners += [dev(y_=yo(k)) for k in (1, 2, 3)]
    partners += [lo(k) for k in (1, 2, 3)]
    barrier = pltpu.get_barrier_semaphore()
    for p in partners:
        pl.semaphore_signal(barrier, inc=1, device_id=p, device_id_type=MESH)
    half = lax.rem(x, 2)
    same = x // 2 == c
    swap = [dev(x_=2 * c + i, c_=x // 2) for i in range(2)]
    swap_y = {(i, k): dev(x_=2 * c + i, c_=x // 2, y_=yo(k)) for i in range(2) for k in (1, 2, 3)}
    for p in swap_y.values():
        pl.semaphore_signal(barrier, inc=1, device_id=p, device_id_type=MESH)
    own = [jnp.logical_and(same, half == i) for i in range(2)]
    for i in range(2):

        @pl.when(jnp.logical_not(own[i]))
        def _(i=i):
            pl.semaphore_signal(barrier, inc=1, device_id=swap[i], device_id_type=MESH)

    pl.semaphore_wait(barrier, len(partners) + len(swap_y) + 2 - same.astype(jnp.int32))

    swaps = []

    def swap_out(src_of, dst):
        ks = (next(ids), next(ids))
        for i in range(2):

            @pl.when(own[i])
            def _(i=i):
                pltpu.make_async_copy(src_of(i), dst.at[half], recv.at[ks[0] + half]).start()

            @pl.when(jnp.logical_not(own[i]))
            def _(i=i):
                remote(src_of(i), dst.at[half], ks[i], ks[0] + half, swap[i]).start()

        swaps.append((ks, src_of, dst))
        return ks

    def swap_in(ks, dst):
        for i in range(2):
            got(ks[i], dst.at[i])

    k_mx = {k: next(ids) for k in (1, 2, 3)}
    modx[x] = jnp.zeros((8, W), F32)
    modx[x, 0:3, :] = m_ref[...]
    for k in (1, 2, 3):
        put(k_mx[k], modx.at[x], modx.at[x], dev(x_=xo(k)))
    ks_state = swap_out(lambda i: s_ref.at[pl.ds(T * i, T)], sbuf)

    mine = 4 * h + x
    far = 4 * (1 - h)

    def win_side():
        def slot_of(hx, first=0, rows=W):
            return win.at[pl.ds(pl.multiple_of(hx * W + first, 16), rows), :]

        def part_of(hd, first, rows):
            return wi_ref.at[pl.ds(pl.multiple_of(first, 16), rows), pl.ds(pl.multiple_of(hd * U, 128), U)]

        return part_of, slot_of, W

    def wout_side(col, cols):
        def slot_of(hx, first=0, rows=U):
            return wout.at[
                hx // 2,
                pl.ds(pl.multiple_of(first, 16), rows),
                pl.ds(pl.multiple_of(lax.rem(hx, 2) * W + col, 128), cols),
            ]

        def part_of(hd, first, rows):
            return wo_ref.at[pl.ds(pl.multiple_of(hd * U + first, 16), rows), col : col + cols]

        return part_of, slot_of, U

    class Side:
        def __init__(self, part_of, slot_of, rows, cross):
            self.part_of, self.slot_of, self.rows, self.q = part_of, slot_of, rows, rows // 4
            self.flows = range(5 if cross else 4)
            self.k_x = {k: next(ids) for k in (1, 3)}
            self.k_fwd = {} if cross else {k: next(ids) for k in (1, 3)}
            self.k_in = [next(ids) for _ in self.flows]
            self.k_y = {(s, k, f): next(ids) for s in self.flows for k in (1, 3) for f in range(2)}
            self.k_own = next(ids)

        def quarter(self, s, yy, first=0, rows=None):
            hx = 4 * h + xo(2) if s == 4 else far + xo(-s)
            return self.slot_of(hx, yy * self.q + first, rows or self.q)

        def far_start(self):
            put(self.k_in[0], self.part_of(1 - h, y * self.q, self.q), self.slot_of(mine, y * self.q, self.q), z4)

        def cross_start(self):
            to = dev(x_=xo(2))
            put(self.k_in[4], self.part_of(h, y * self.q, self.q), self.slot_of(mine, y * self.q, self.q), to)

        def near_start(self):
            for k in (1, 3):
                put(self.k_x[k], self.part_of(h, 0, self.rows), self.slot_of(mine), dev(x_=xo(k)))
            self.copy = pltpu.make_async_copy(self.part_of(h, 0, self.rows), self.slot_of(mine), recv.at[self.k_own])
            self.copy.start()

        def arrive(self, s):
            here = self.quarter(s, y)
            got(self.k_in[s], here)
            if s == 0:
                for k in (2, 1, 3):
                    put(self.k_in[k], here, here, dev(x_=xo(k)))
            for k in (1, 3):
                put(self.k_y[s, k, 0], here, here, dev(y_=yo(k)))

        def spread(self, s):
            for k, first in ((1, 0), (3, self.q // 2)):
                got(self.k_y[s, k, 0], self.quarter(s, yo(-k)))
                there = self.quarter(s, yo(-k), first, self.q // 2)
                put(self.k_y[s, k, 1], there, there, dev(y_=yo(k)))

        def forward(self):
            for k, first in ((1, 0), (3, self.rows // 2)):
                got(self.k_x[k], self.slot_of(4 * h + xo(-k)))
                there = self.slot_of(4 * h + xo(-k), first, self.rows // 2)
                put(self.k_fwd[k], there, there, dev(x_=xo(k)))

        def end(self):
            for k, first in ((1, 0), (3, self.rows // 2)):
                if self.k_fwd:
                    got(self.k_fwd[k], self.slot_of(4 * h + xo(2), first, self.rows // 2))
                else:
                    got(self.k_x[k], self.slot_of(4 * h + xo(-k)))
            for s in self.flows:
                for k, first in ((1, 0), (3, self.q // 2)):
                    got(self.k_y[s, k, 1], self.quarter(s, yo(2), first, self.q // 2))
            self.copy.wait()

    w_in = Side(*win_side(), True)
    w_out = Side(*wout_side(0, W), False)
    w_in.cross_start()
    w_in.far_start()
    w_in.near_start()

    def mod(j, r):
        return modall[j, r : r + 1, :]

    sign = (1, -1)

    class Part:
        def __init__(self, it, p):
            self.it, self.p = it, p
            self.first, self.n = PARTS[p]
            self.x, self.hid, self.part = xall[p].at[it], hid[p], part[p]
            self.k_stat = [next(ids) for _ in range(3)]
            steps = [(s, g, j) for s in range(1, 5) for j in range(2) for g in range(2)]
            self.k_ring = {key: next(ids) for key in steps if key[0] < 4 or key[1] == key[2]}
            self.k_sib = {key: next(ids) for key in self.k_ring}
            self.k_own = [next(ids) for _ in range(2)]
            self.units = ((0, W),)
            self.k_half = {(u, hh): next(ids) for u in self.units for hh in range(2)}
            self.k_sum = {
                u: {key: next(ids) for key in steps if key[0] > 1 or key[1] == key[2]} for u in self.units
            }
            self.k_prefix = {i: next(ids) for i in (1, 2, 3)}

        def rows(self):
            return slice(self.first, self.first + self.n)

        def stats(self, cur):
            self.cur = cur
            own, there = stat[self.p].at[self.it], statr[self.p].at[self.it]
            total = sum(jnp.sum(v, axis=1, keepdims=True) for v in cur)
            squares = sum(jnp.sum(v * v, axis=1, keepdims=True) for v in cur)
            lane = lax.broadcasted_iota(jnp.int32, (self.n, 128), 1)
            own[...] = jnp.where(lane < 64, total, squares)
            for i, to in enumerate((z4, z4sib, sib)):
                put(self.k_stat[i], own, there.at[i], to)

        def slot(self, zz, cc, j):
            hh, ll = zz // 4, lax.rem(zz, 4)
            return self.x.at[
                pl.ds(pl.multiple_of(ll * self.n, 16), self.n),
                pl.ds(pl.multiple_of((4 * hh + 2 * cc + j) * W, 128), W),
            ]

        def normalise(self):
            own, there = stat[self.p].at[self.it], statr[self.p].at[self.it]
            for i, k in enumerate(self.k_stat):
                got(k, there.at[i])
            total = own[...] + there[0] + there[1] + there[2]
            mean = total[:, 0:1] / D
            var = total[:, 64:65] / D - mean * mean
            scale = lax.rsqrt(var + EPSILON)
            for j in range(2):
                value = (self.cur[j] - mean) * scale * (1.0 + mod(j, 1)) + mod(j, 0)
                slot = self.slot(z, c, j)
                slot[...] = value.astype(BF16)
                for g in range(2):
                    put(self.k_ring[1, g, j], slot, slot, dev(z_=zo(sign[g])))
                put(self.k_own[j], slot, slot, sib)

        def gather(self, s):
            for j in range(2):
                for g in range(2):
                    if (s, g, j) not in self.k_ring:
                        continue
                    slot = self.slot(zo(-sign[g] * s), c, j)
                    got(self.k_ring[s, g, j], slot)
                    if (s + 1, g, j) in self.k_ring:
                        put(self.k_ring[s + 1, g, j], slot, slot, dev(z_=zo(sign[g])))
                    put(self.k_sib[s, g, j], slot, slot, sib)

        def gathered(self):
            for j in range(2):
                got(self.k_own[j], self.slot(z, 1 - c, j))
            for (s, g, j), k in self.k_sib.items():
                got(k, self.slot(zo(-sign[g] * s), 1 - c, j))

        def first_matmul(self):
            def tile(n, _):
                cols = pl.ds(pl.multiple_of(n * 256, 256), 256)
                pre = jnp.dot(self.x[...], win[:, cols], preferred_element_type=F32)
                self.hid[:, cols] = jax.nn.gelu(pre, approximate=True).astype(BF16)
                return 0

            lax.fori_loop(0, U // 256, tile, 0)

        def tiles(self, u):
            if u[1] < W:
                return [(j, u[0], u[1]) for j in range(2)]
            return [(None, 256 * n, 256) for n in range(3)]

        def second(self, cc, hh, u):
            for j, col, cols in self.tiles(u):
                at = col if j is None else W * j + col
                yield at, cols, jnp.dot(self.hid[...], wout[2 * hh + cc, :, at : at + cols], preferred_element_type=F32)

        def second_other(self, u):
            there, back = obs[self.p].at[self.it], obr[self.p].at[self.it]
            for hh in range(2):
                for at, cols, value in self.second(1 - c, hh, u):
                    for j, col in ((n // 3, n % 3 * 128) for n in range(at // 128, (at + cols) // 128)):
                        first = W * j + col - at
                        there[hh, j, :, col : col + 128] = value[:, first : first + 128].astype(BF16)
                cols = slice(u[0], u[0] + u[1])
                put(self.k_half[u, hh], there.at[hh, :, :, cols], back.at[hh, :, :, cols], sib)

        def second_own(self, u):
            for hh in range(2):
                for at, cols, value in self.second(c, hh, u):
                    self.part[hh, :, :, at : at + cols] = value.reshape(4, self.n, cols)

        def halves(self, u):
            back = obr[self.p].at[self.it]
            cols = slice(u[0], u[0] + u[1])
            for hh in range(2):
                got(self.k_half[u, hh], back.at[hh, :, :, cols])
                for j in range(2):
                    at = slice(W * j + u[0], W * j + u[0] + u[1])
                    self.part[hh, :, :, at] += back[hh, j, :, cols].astype(F32).reshape(4, self.n, u[1])

        def term(self, d, j, u):
            return self.part[d // 4, lax.rem(d, 4), :, W * j + u[0] : W * j + u[0] + u[1]]

        def scatter(self, s, u):
            k = self.k_sum[u]
            cols = slice(u[0], u[0] + u[1])
            out, back = rss[self.p].at[self.it], rsr[self.p].at[self.it]
            for j in range(2):
                for g in range(2):
                    if (s, g, j) not in k:
                        continue
                    value = self.term(zo(sign[g] * (5 - s)), j, u)
                    if (s - 1, g, j) in k:
                        got(k[s - 1, g, j], back.at[s - 2, g, j, :, cols])
                        value = value + back[s - 2, g, j, :, cols].astype(F32)
                    out[s - 1, g, j, :, cols] = value.astype(BF16)
                    here, there = out.at[s - 1, g, j, :, cols], back.at[s - 1, g, j, :, cols]
                    put(k[s, g, j], here, there, dev(z_=zo(sign[g])))

        def scattered(self, u):
            k = self.k_sum[u]
            cols = slice(u[0], u[0] + u[1])
            back = rsr[self.p].at[self.it]
            for j in range(2):
                value = self.term(z, j, u)
                for g in range(2):
                    got(k[4, g, j], back.at[3, g, j, :, cols])
                    value = value + back[3, g, j, :, cols].astype(F32)
                drift[self.p][j, :, cols] = step_ref[0] * mod(j, 2)[:, cols] * value

        def prefix_copy(self, i):
            return remote(
                dsend[self.p], drecv[self.p].at[i - 1], self.k_prefix[i], self.k_prefix[i], dev(y_=yo(i))
            )

        def prefix_send(self):
            for j in range(2):
                dsend[self.p][j] = drift[self.p][j].astype(BF16)
            for i in (1, 2, 3):

                @pl.when(y + i < 4)
                def _(i=i):
                    self.prefix_copy(i).start()

        def prefix_add(self):
            pref[:, self.rows(), :] = jnp.zeros((2, self.n, W), F32)
            for i in (3, 2, 1):

                @pl.when(y - i >= 0)
                def _(i=i):
                    got(self.k_prefix[i], drecv[self.p].at[i - 1])
                    for j in range(2):
                        pref[j, self.rows(), :] += drecv[self.p][i - 1, j].astype(F32)

        def prefix_sent(self):
            for i in (1, 2, 3):

                @pl.when(y + i < 4)
                def _(i=i):
                    self.prefix_copy(i).wait_send()

        def current(self):
            return [abuf[j, self.rows(), :] + pref[j, self.rows(), :] for j in range(2)]

        def out_copy(self, k, i):
            there = frecv.at[k, half, pl.ds(self.first, self.n)]
            to = swap[i] if k == 0 else swap_y[i, k]
            return remote(fsend[self.p].at[i], there, self.k_out[k, i], self.k_out[k, 0] + half, to)

        def out_send(self):
            self.k_out = {(k, i): next(ids) for k in range(4) for i in range(2)}
            for i in range(2):
                fsend[self.p][i] = drift[self.p][i].astype(BF16)
            for k in (3, 2, 1, 0):
                for i in range(2):
                    if k:

                        @pl.when(y + k < 4)
                        def _(i=i, k=k):
                            self.out_copy(k, i).start()

                    else:
                        there = frecv.at[0, half, pl.ds(self.first, self.n)]

                        @pl.when(own[i])
                        def _(i=i):
                            pltpu.make_async_copy(
                                fsend[self.p].at[i], there, recv.at[self.k_out[0, 0] + half]
                            ).start()

                        @pl.when(jnp.logical_not(own[i]))
                        def _(i=i):
                            self.out_copy(0, i).start()

        def out_sent(self):
            for k in range(4):
                for i in range(2):

                    @pl.when(y + k < 4 if k else jnp.logical_not(own[i]))
                    def _(i=i, k=k):
                        self.out_copy(k, i).wait_send()

        def out_add(self):
            for i in range(2):
                rows = slice(T * i + self.first, T * i + self.first + self.n)
                out_ref[rows, :] = a_ref[rows, :]
                for k in (3, 2, 1, 0):

                    @pl.when(y - k >= 0)
                    def _(i=i, k=k):
                        got(self.k_out[k, i], frecv.at[k, i, pl.ds(self.first, self.n)])
                        out_ref[rows, :] += frecv[k, i, self.rows(), :].astype(F32)

    parts = [[Part(it, p) for p in range(2)] for it in range(ITERS)]
    a, b = parts[0]

    for k in (1, 2, 3):
        got(k_mx[k], modx.at[xo(-k)])
    k_ms = next(ids)
    put(k_ms, modx.at[pl.ds(2 * (1 - c), 2)], msib, sib)
    swap_in(ks_state, sbuf)
    for v in (a, b):
        v.stats([sbuf[j, v.rows(), :] for j in range(2)])
    w_out.far_start()
    got(k_ms, msib)
    m1[...] = modx[pl.ds(2 * c, 2)] + msib[...]
    k_ml = {k: next(ids) for k in (1, 2, 3)}
    for k in (1, 2, 3):
        put(k_ml[k], m1, mrecv.at[k - 1], lo(k))
    w_in.arrive(4)
    w_in.arrive(0)
    w_in.spread(4)
    w_out.arrive(0)
    w_out.near_start()
    w_in.spread(0)
    for k in (1, 2, 3):
        got(k_ml[k], mrecv.at[k - 1])
    modall[...] = m1[...] + mrecv[0] + mrecv[1] + mrecv[2]
    for v in (a, b):
        v.normalise()
    w_out.spread(0)
    w_in.arrive(2)
    for v in (a, b):
        v.gather(1)
    w_in.arrive(1)
    w_in.arrive(3)
    for v in (a, b):
        v.gather(2)
    w_in.spread(2)
    w_out.arrive(2)
    w_in.spread(1)
    w_out.arrive(1)
    w_out.arrive(3)
    for v in (a, b):
        v.gather(3)
    w_in.spread(3)
    for v in (a, b):
        v.gather(4)
    w_out.spread(2)
    w_out.spread(1)
    w_out.forward()
    w_out.spread(3)
    a.gathered()
    b.gathered()
    w_in.end()
    a.first_matmul()
    b.first_matmul()
    w_out.end()
    ks_anchor = swap_out(lambda i: a_ref.at[pl.ds(T * i, T)], abuf)

    u = (0, W)
    for it in range(ITERS):
        a, b = parts[it]
        if it:
            a.gathered()
            a.first_matmul()
        a.second_other(u)
        a.second_own(u)
        if it:
            b.gather(4)
            b.gathered()
        a.halves(u)
        a.scatter(1, u)
        if it:
            b.first_matmul()
        b.second_other(u)
        a.scatter(2, u)
        b.second_own(u)
        b.halves(u)
        b.scatter(1, u)
        a.scatter(3, u)
        b.scatter(2, u)
        a.scatter(4, u)
        b.scatter(3, u)
        a.scattered(u)
        if it + 1 == ITERS:
            a.out_send()
            b.scatter(4, u)
            b.scattered(u)
            b.out_send()
            a.out_add()
            b.out_add()
            continue
        a.prefix_send()
        b.scatter(4, u)
        b.scattered(u)
        b.prefix_send()
        swap_in(ks_anchor, abuf)
        after, later = parts[it + 1]
        a.prefix_add()
        after.stats(a.current())
        b.prefix_add()
        later.stats(b.current())
        after.normalise()
        later.normalise()
        for s in range(1, 4):
            after.gather(s)
            later.gather(s)
        after.gather(4)

    for copy in pending:
        copy.wait_send()
    for v in parts[0]:
        v.prefix_sent()
    for v in parts[1]:
        v.out_sent()
    for ks, src_of, dst in swaps:
        for i in range(2):

            @pl.when(jnp.logical_not(own[i]))
            def _(i=i):
                remote(src_of(i), dst.at[half], ks[i], ks[0] + half, swap[i]).wait_send()


def local(states, anchor, timesteps, step_sizes, weight_in, weight_out, mod_weight):
    embedding = timestep_embedding(timesteps)[0]
    rows_here = mod_weight.shape[0]
    embed_part = lax.dynamic_slice_in_dim(
        embedding, lax.axis_index("row") * rows_here, rows_here, 0
    )
    mod_part = jnp.einsum(
        "e,ekd->kd", embed_part, mod_weight.astype(jnp.float32), precision=lax.Precision.HIGHEST
    )
    vmem = pl.BlockSpec(memory_space=pltpu.VMEM)

    def each(make):
        return [make(n) for _, n in PARTS]

    scratch = [
        pltpu.VMEM((2, T, W), F32),
        pltpu.VMEM((2, T, W), F32),
        pltpu.VMEM((4, 8, W), F32),
        pltpu.VMEM((2, 8, W), F32),
        pltpu.VMEM((2, 8, W), F32),
        pltpu.VMEM((3, 2, 8, W), F32),
        pltpu.VMEM((2, 8, W), F32),
        pltpu.VMEM((D, U), BF16),
        pltpu.VMEM((4, U, 2 * W), BF16),
        pltpu.VMEM((2, T, W), F32),
        pltpu.VMEM((4, 2, T, W), BF16),
        each(lambda n: pltpu.VMEM((ITERS, n, 128), F32)),
        each(lambda n: pltpu.VMEM((ITERS, 3, n, 128), F32)),
        each(lambda n: pltpu.VMEM((ITERS, 4 * n, D), BF16)),
        each(lambda n: pltpu.VMEM((4 * n, U), BF16)),
        each(lambda n: pltpu.VMEM((ITERS, 2, 2, 4 * n, W), BF16)),
        each(lambda n: pltpu.VMEM((ITERS, 2, 2, 4 * n, W), BF16)),
        each(lambda n: pltpu.VMEM((2, 4, n, 2 * W), F32)),
        each(lambda n: pltpu.VMEM((ITERS, 4, 2, 2, n, W), BF16)),
        each(lambda n: pltpu.VMEM((ITERS, 4, 2, 2, n, W), BF16)),
        each(lambda n: pltpu.VMEM((2, n, W), BF16)),
        each(lambda n: pltpu.VMEM((3, 2, n, W), BF16)),
        each(lambda n: pltpu.VMEM((2, n, W), BF16)),
        each(lambda n: pltpu.VMEM((2, n, W), F32)),
        pltpu.SemaphoreType.DMA((COPIES,)),
        pltpu.SemaphoreType.DMA((COPIES,)),
    ]
    out = pl.pallas_call(
        kernel,
        out_shape=jax.ShapeDtypeStruct(anchor.shape, F32),
        in_specs=[pl.BlockSpec(memory_space=pltpu.SMEM), vmem, vmem, vmem]
        + [pl.BlockSpec(memory_space=pl.ANY)] * 2,
        out_specs=vmem,
        scratch_shapes=scratch,
        compiler_params=pltpu.CompilerParams(
            collective_id=0, has_side_effects=True, vmem_limit_bytes=60 << 20
        ),
        name="picard",
    )(step_sizes, states[0], anchor, mod_part, weight_in, weight_out)
    return out[None]


def solution(mesh):
    placed = (
        P("tm", "row", "col"),
        P("row", "col"),
        P("tm"),
        P("tm"),
        P("col", "row"),
        P("row", "col"),
        P("row", None, "col"),
    )
    return jax.shard_map(
        local, mesh=mesh, in_specs=placed, out_specs=P("tm", "row", "col"), check_vma=False
    )
```

```python
import math

import jax
import jax.numpy as jnp
from jax import lax
from jax.experimental import pallas as pl
from jax.experimental.pallas import tpu as pltpu
from jax.sharding import PartitionSpec as P

D = 3072
ITERS = 2
EPSILON = 1e-06
MESH = pl.DeviceIdType.MESH
F32 = jnp.float32
BF16 = jnp.bfloat16

T = 80
W = 384
U = 768

PARTS = ((0, 32), (32, 48))

ORDER = ((0, 0), (1, 1), (0, 1), (1, 0))

COPIES = 304


def kernel(
    time_any, step_any, s_ref, a_any, m_any, wi_ref, wo_ref, out_ref,
    time_ref, step_ref, a_ref, m_ref,
    sbuf, abuf, modx, msib, m1, mrecv, modall, win, wout, pref, frecv,
    stat, statr, xall, hid, obs, obr, part, rss, rsr, dsend, drecv, fsend, drift,
    send, recv,
):
    y = lax.axis_index("tm")
    row = lax.axis_index("row")
    col = lax.axis_index("col")
    l, c = row // 2, lax.rem(row, 2)
    h, x = col // 4, lax.rem(col, 4)
    z = 4 * h + l

    def dev(x_=None, y_=None, z_=None, c_=None):
        x_ = x if x_ is None else x_
        y_ = y if y_ is None else y_
        z_ = z if z_ is None else z_
        c_ = c if c_ is None else c_
        return (y_, 2 * lax.rem(z_, 4) + c_, 4 * (z_ // 4) + x_)

    def xo(k):
        return lax.rem(x + k + 4, 4)

    def yo(k):
        return lax.rem(y + k + 4, 4)

    def zo(k):
        return lax.rem(z + k + 8, 8)

    sib = dev(c_=1 - c)
    z4 = dev(z_=zo(4))
    z4sib = dev(z_=zo(4), c_=1 - c)

    def lo(k):
        return dev(z_=4 * h + lax.rem(l + k, 4))

    ids = iter(range(COPIES))
    pending = []

    def remote(src, dst, ss, rs, to):
        return pltpu.make_async_remote_copy(
            src_ref=src, dst_ref=dst, send_sem=send.at[ss], recv_sem=recv.at[rs],
            device_id=to, device_id_type=MESH,
        )

    def put(k, src, dst, to):
        copy = remote(src, dst, k, k, to)
        copy.start()
        pending.append(copy)

    def got(k, dst):
        remote(dst, dst, k, k, sib).wait_recv()

    loads = [(time_any, time_ref), (m_any, m_ref), (step_any, step_ref)]
    loads = [pltpu.make_async_copy(*pair, recv.at[next(ids)]) for pair in loads]
    for copy in loads:
        copy.start()

    partners = [sib, z4, z4sib, dev(z_=zo(1)), dev(z_=zo(-1))]
    partners += [dev(x_=xo(k)) for k in (1, 2, 3)]
    partners += [dev(y_=yo(k)) for k in (1, 2, 3)]
    partners += [lo(k) for k in (1, 2, 3)]
    barrier = pltpu.get_barrier_semaphore()
    for p in partners:
        pl.semaphore_signal(barrier, inc=1, device_id=p, device_id_type=MESH)
    half = lax.rem(x, 2)
    same = x // 2 == c
    swap = [dev(x_=2 * c + i, c_=x // 2) for i in range(2)]
    swap_y = {(i, k): dev(x_=2 * c + i, c_=x // 2, y_=yo(k)) for i in range(2) for k in (1, 2, 3)}
    for p in swap_y.values():
        pl.semaphore_signal(barrier, inc=1, device_id=p, device_id_type=MESH)
    own = [jnp.logical_and(same, half == i) for i in range(2)]
    for i in range(2):

        @pl.when(jnp.logical_not(own[i]))
        def _(i=i):
            pl.semaphore_signal(barrier, inc=1, device_id=swap[i], device_id_type=MESH)

    for copy in loads[:2]:
        copy.wait()

    entry = (lax.rem(row, 4) * W + lax.broadcasted_iota(jnp.int32, (16, W), 1)).astype(F32)
    phase = time_ref[0].astype(F32) * jnp.exp(-math.log(10000.0) * entry / (D // 2))
    embedding = jnp.where(row < 4, jnp.cos(phase), jnp.sin(phase))
    high = embedding.astype(BF16).astype(F32)
    middle = (embedding - high).astype(BF16).astype(F32)
    low = embedding - high - middle
    line = lax.broadcasted_iota(jnp.int32, (16, W), 0)
    terms = jnp.where(line == 0, high, jnp.where(line == 1, middle, jnp.where(line == 2, low, 0.0)))
    modx[x] = jnp.zeros((8, W), F32)
    for r in range(3):
        products = jnp.dot(terms.astype(BF16), m_ref[r], preferred_element_type=F32)
        modx[x, r : r + 1, :] = jnp.sum(products, axis=0, keepdims=True)
    pl.semaphore_wait(barrier, len(partners) + len(swap_y) + 2 - same.astype(jnp.int32))

    swaps = []

    def swap_out(src_of, dst):
        ks = (next(ids), next(ids))
        for i in range(2):

            @pl.when(own[i])
            def _(i=i):
                pltpu.make_async_copy(src_of(i), dst.at[half], recv.at[ks[0] + half]).start()

            @pl.when(jnp.logical_not(own[i]))
            def _(i=i):
                remote(src_of(i), dst.at[half], ks[i], ks[0] + half, swap[i]).start()

        swaps.append((ks, src_of, dst))
        return ks

    def swap_in(ks, dst):
        for i in range(2):
            got(ks[i], dst.at[i])

    k_mx = {k: next(ids) for k in (1, 2, 3)}
    for k in (1, 2, 3):
        put(k_mx[k], modx.at[x], modx.at[x], dev(x_=xo(k)))
    ks_state = swap_out(lambda i: s_ref.at[pl.ds(T * i, T)], sbuf)

    mine = 4 * h + x
    far = 4 * (1 - h)

    def win_side():
        def slot_of(hx, first=0, rows=W):
            return win.at[pl.ds(pl.multiple_of(hx * W + first, 16), rows), :]

        def part_of(hd, first, rows):
            return wi_ref.at[pl.ds(pl.multiple_of(first, 16), rows), pl.ds(pl.multiple_of(hd * U, 128), U)]

        return part_of, slot_of, W

    def wout_side(col, cols):
        def slot_of(hx, first=0, rows=U):
            return wout.at[
                hx // 2,
                pl.ds(pl.multiple_of(first, 16), rows),
                pl.ds(pl.multiple_of(lax.rem(hx, 2) * W + col, 128), cols),
            ]

        def part_of(hd, first, rows):
            return wo_ref.at[pl.ds(pl.multiple_of(hd * U + first, 16), rows), col : col + cols]

        return part_of, slot_of, U

    class Side:
        def __init__(self, part_of, slot_of, rows, cross):
            self.part_of, self.slot_of, self.rows, self.q = part_of, slot_of, rows, rows // 4
            self.flows = range(5 if cross else 4)
            self.k_x = {k: next(ids) for k in (1, 3)}
            self.k_fwd = {} if cross else {k: next(ids) for k in (1, 3)}
            self.k_in = [next(ids) for _ in self.flows]
            self.k_y = {(s, k, f): next(ids) for s in self.flows for k in (1, 3) for f in range(2)}
            self.k_own = next(ids)

        def quarter(self, s, yy, first=0, rows=None):
            hx = 4 * h + xo(2) if s == 4 else far + xo(-s)
            return self.slot_of(hx, yy * self.q + first, rows or self.q)

        def far_start(self):
            put(self.k_in[0], self.part_of(1 - h, y * self.q, self.q), self.slot_of(mine, y * self.q, self.q), z4)

        def cross_start(self):
            to = dev(x_=xo(2))
            put(self.k_in[4], self.part_of(h, y * self.q, self.q), self.slot_of(mine, y * self.q, self.q), to)

        def near_start(self):
            for k in (1, 3):
                put(self.k_x[k], self.part_of(h, 0, self.rows), self.slot_of(mine), dev(x_=xo(k)))
            self.copy = pltpu.make_async_copy(self.part_of(h, 0, self.rows), self.slot_of(mine), recv.at[self.k_own])
            self.copy.start()

        def arrive(self, s):
            here = self.quarter(s, y)
            got(self.k_in[s], here)
            if s == 0:
                for k in (2, 1, 3):
                    put(self.k_in[k], here, here, dev(x_=xo(k)))
            for k in (1, 3):
                put(self.k_y[s, k, 0], here, here, dev(y_=yo(k)))

        def spread(self, s):
            for k, first in ((1, 0), (3, self.q // 2)):
                got(self.k_y[s, k, 0], self.quarter(s, yo(-k)))
                there = self.quarter(s, yo(-k), first, self.q // 2)
                put(self.k_y[s, k, 1], there, there, dev(y_=yo(k)))

        def forward(self):
            for k, first in ((1, 0), (3, self.rows // 2)):
                got(self.k_x[k], self.slot_of(4 * h + xo(-k)))
                there = self.slot_of(4 * h + xo(-k), first, self.rows // 2)
                put(self.k_fwd[k], there, there, dev(x_=xo(k)))

        def end(self):
            for k, first in ((1, 0), (3, self.rows // 2)):
                if self.k_fwd:
                    got(self.k_fwd[k], self.slot_of(4 * h + xo(2), first, self.rows // 2))
                else:
                    got(self.k_x[k], self.slot_of(4 * h + xo(-k)))
            for s in self.flows:
                for k, first in ((1, 0), (3, self.q // 2)):
                    got(self.k_y[s, k, 1], self.quarter(s, yo(2), first, self.q // 2))
            self.copy.wait()

    w_in = Side(*win_side(), True)
    w_out = Side(*wout_side(0, W), False)
    w_in.cross_start()
    w_in.far_start()
    w_in.near_start()

    def mod(j, r):
        return modall[j, r : r + 1, :]

    sign = (1, -1)

    class Part:
        def __init__(self, it, p):
            self.it, self.p = it, p
            self.first, self.n = PARTS[p]
            self.x, self.hid, self.part = xall[p].at[it], hid[p], part[p]
            self.k_stat = [next(ids) for _ in range(3)]
            steps = [(s, g, j) for s in range(1, 5) for j in range(2) for g in range(2)]
            self.k_ring = {key: next(ids) for key in steps if key[0] < 4 or key[1] == key[2]}
            self.k_sib = {key: next(ids) for key in self.k_ring}
            self.k_own = [next(ids) for _ in range(2)]
            self.units = ((0, W),)
            self.k_half = {(u, hh): next(ids) for u in self.units for hh in range(2)}
            self.k_sum = {
                u: {key: next(ids) for key in steps if key[0] > 1 or key[1] == key[2]} for u in self.units
            }
            self.k_prefix = {i: next(ids) for i in (1, 2, 3)}

        def rows(self):
            return slice(self.first, self.first + self.n)

        def stats(self, cur):
            self.cur = cur
            own, there = stat[self.p].at[self.it], statr[self.p].at[self.it]
            total = sum(jnp.sum(v, axis=1, keepdims=True) for v in cur)
            squares = sum(jnp.sum(v * v, axis=1, keepdims=True) for v in cur)
            lane = lax.broadcasted_iota(jnp.int32, (self.n, 128), 1)
            own[...] = jnp.where(lane < 64, total, squares)
            for i, to in enumerate((z4, z4sib, sib)):
                put(self.k_stat[i], own, there.at[i], to)

        def slot(self, zz, cc, j):
            hh, ll = zz // 4, lax.rem(zz, 4)
            return self.x.at[
                pl.ds(pl.multiple_of(ll * self.n, 16), self.n),
                pl.ds(pl.multiple_of((4 * hh + 2 * cc + j) * W, 128), W),
            ]

        def normalise(self):
            own, there = stat[self.p].at[self.it], statr[self.p].at[self.it]
            for i, k in enumerate(self.k_stat):
                got(k, there.at[i])
            total = own[...] + there[0] + there[1] + there[2]
            mean = total[:, 0:1] / D
            var = total[:, 64:65] / D - mean * mean
            scale = lax.rsqrt(var + EPSILON)
            for j in range(2):
                value = (self.cur[j] - mean) * scale * (1.0 + mod(j, 1)) + mod(j, 0)
                slot = self.slot(z, c, j)
                slot[...] = value.astype(BF16)
            for g, j in ORDER:
                slot = self.slot(z, c, j)
                put(self.k_ring[1, g, j], slot, slot, dev(z_=zo(sign[g])))
            for j in range(2):
                slot = self.slot(z, c, j)
                put(self.k_own[j], slot, slot, sib)

        def gather(self, s):
            for g, j in ORDER:
                if (s, g, j) not in self.k_ring:
                    continue
                slot = self.slot(zo(-sign[g] * s), c, j)
                got(self.k_ring[s, g, j], slot)
                if (s + 1, g, j) in self.k_ring:
                    put(self.k_ring[s + 1, g, j], slot, slot, dev(z_=zo(sign[g])))
                put(self.k_sib[s, g, j], slot, slot, sib)

        def gathered(self):
            for j in range(2):
                got(self.k_own[j], self.slot(z, 1 - c, j))
            for (s, g, j), k in self.k_sib.items():
                got(k, self.slot(zo(-sign[g] * s), 1 - c, j))

        def first_matmul(self):
            def tile(n, _):
                cols = pl.ds(pl.multiple_of(n * 256, 256), 256)
                pre = jnp.dot(self.x[...], win[:, cols], preferred_element_type=F32)
                self.hid[:, cols] = jax.nn.gelu(pre, approximate=True).astype(BF16)
                return 0

            lax.fori_loop(0, U // 256, tile, 0)

        def tiles(self, u):
            if u[1] < W:
                return [(j, u[0], u[1]) for j in range(2)]
            return [(None, 256 * n, 256) for n in range(3)]

        def second(self, cc, hh, u):
            for j, col, cols in self.tiles(u):
                at = col if j is None else W * j + col
                yield at, cols, jnp.dot(self.hid[...], wout[2 * hh + cc, :, at : at + cols], preferred_element_type=F32)

        def second_other(self, u):
            there, back = obs[self.p].at[self.it], obr[self.p].at[self.it]
            for hh in range(2):
                for at, cols, value in self.second(1 - c, hh, u):
                    for j, col in ((n // 3, n % 3 * 128) for n in range(at // 128, (at + cols) // 128)):
                        first = W * j + col - at
                        there[hh, j, :, col : col + 128] = value[:, first : first + 128].astype(BF16)
                cols = slice(u[0], u[0] + u[1])
                put(self.k_half[u, hh], there.at[hh, :, :, cols], back.at[hh, :, :, cols], sib)

        def second_own(self, u):
            for hh in range(2):
                for at, cols, value in self.second(c, hh, u):
                    self.part[hh, :, :, at : at + cols] = value.reshape(4, self.n, cols)

        def halves(self, u):
            back = obr[self.p].at[self.it]
            cols = slice(u[0], u[0] + u[1])
            for hh in range(2):
                got(self.k_half[u, hh], back.at[hh, :, :, cols])
                for j in range(2):
                    at = slice(W * j + u[0], W * j + u[0] + u[1])
                    self.part[hh, :, :, at] += back[hh, j, :, cols].astype(F32).reshape(4, self.n, u[1])

        def term(self, d, j, u):
            return self.part[d // 4, lax.rem(d, 4), :, W * j + u[0] : W * j + u[0] + u[1]]

        def scatter(self, s, u):
            k = self.k_sum[u]
            cols = slice(u[0], u[0] + u[1])
            out, back = rss[self.p].at[self.it], rsr[self.p].at[self.it]
            for g, j in ORDER:
                t = s if g == j else s + 1
                if t > 4:
                    continue
                value = self.term(zo(sign[g] * (5 - t)), j, u)
                if (t - 1, g, j) in k:
                    got(k[t - 1, g, j], back.at[t - 2, g, j, :, cols])
                    value = value + back[t - 2, g, j, :, cols].astype(F32)
                out[t - 1, g, j, :, cols] = value.astype(BF16)
                here, there = out.at[t - 1, g, j, :, cols], back.at[t - 1, g, j, :, cols]
                put(k[t, g, j], here, there, dev(z_=zo(sign[g])))

        def scattered(self, u):
            k = self.k_sum[u]
            cols = slice(u[0], u[0] + u[1])
            back = rsr[self.p].at[self.it]
            for j in range(2):
                value = self.term(z, j, u)
                for g in range(2):
                    got(k[4, g, j], back.at[3, g, j, :, cols])
                    value = value + back[3, g, j, :, cols].astype(F32)
                drift[self.p][j, :, cols] = step_ref[0] * mod(j, 2)[:, cols] * value

        def prefix_copy(self, i):
            return remote(
                dsend[self.p], drecv[self.p].at[i - 1], self.k_prefix[i], self.k_prefix[i], dev(y_=yo(i))
            )

        def prefix_send(self):
            for j in range(2):
                dsend[self.p][j] = drift[self.p][j].astype(BF16)
            for i in (1, 2, 3):

                @pl.when(y + i < 4)
                def _(i=i):
                    self.prefix_copy(i).start()

        def prefix_add(self):
            pref[:, self.rows(), :] = jnp.zeros((2, self.n, W), F32)
            for i in (3, 2, 1):

                @pl.when(y - i >= 0)
                def _(i=i):
                    got(self.k_prefix[i], drecv[self.p].at[i - 1])
                    for j in range(2):
                        pref[j, self.rows(), :] += drecv[self.p][i - 1, j].astype(F32)

        def prefix_sent(self):
            for i in (1, 2, 3):

                @pl.when(y + i < 4)
                def _(i=i):
                    self.prefix_copy(i).wait_send()

        def current(self):
            return [abuf[j, self.rows(), :] + pref[j, self.rows(), :] for j in range(2)]

        def out_copy(self, k, i):
            there = frecv.at[k, half, pl.ds(self.first, self.n)]
            to = swap[i] if k == 0 else swap_y[i, k]
            return remote(fsend[self.p].at[i], there, self.k_out[k, i], self.k_out[k, 0] + half, to)

        def out_send(self):
            self.k_out = {(k, i): next(ids) for k in range(4) for i in range(2)}
            for i in range(2):
                fsend[self.p][i] = drift[self.p][i].astype(BF16)
            for k in (3, 2, 1, 0):
                for i in range(2):
                    if k:

                        @pl.when(y + k < 4)
                        def _(i=i, k=k):
                            self.out_copy(k, i).start()

                    else:
                        there = frecv.at[0, half, pl.ds(self.first, self.n)]

                        @pl.when(own[i])
                        def _(i=i):
                            pltpu.make_async_copy(
                                fsend[self.p].at[i], there, recv.at[self.k_out[0, 0] + half]
                            ).start()

                        @pl.when(jnp.logical_not(own[i]))
                        def _(i=i):
                            self.out_copy(0, i).start()

        def out_sent(self):
            for k in range(4):
                for i in range(2):

                    @pl.when(y + k < 4 if k else jnp.logical_not(own[i]))
                    def _(i=i, k=k):
                        self.out_copy(k, i).wait_send()

        def out_add(self):
            for i in range(2):
                rows = slice(T * i + self.first, T * i + self.first + self.n)
                out_ref[rows, :] = jnp.zeros((self.n, W), F32)
                for k in (3, 2, 1, 0):

                    @pl.when(y - k >= 0)
                    def _(i=i, k=k):
                        got(self.k_out[k, i], frecv.at[k, i, pl.ds(self.first, self.n)])
                        out_ref[rows, :] += frecv[k, i, self.rows(), :].astype(F32)

    parts = [[Part(it, p) for p in range(2)] for it in range(ITERS)]
    a, b = parts[0]

    for copy in loads[2:]:
        copy.wait()

    for k in (1, 2, 3):
        got(k_mx[k], modx.at[xo(-k)])
    k_ms = next(ids)
    put(k_ms, modx.at[pl.ds(2 * (1 - c), 2)], msib, sib)
    swap_in(ks_state, sbuf)
    for v in (a, b):
        v.stats([sbuf[j, v.rows(), :] for j in range(2)])
    w_out.far_start()
    got(k_ms, msib)
    m1[...] = modx[pl.ds(2 * c, 2)] + msib[...]
    k_ml = {k: next(ids) for k in (1, 2, 3)}
    for k in (1, 2, 3):
        put(k_ml[k], m1, mrecv.at[k - 1], lo(k))
    w_in.arrive(4)
    w_in.arrive(0)
    w_in.spread(4)
    w_out.arrive(0)
    w_out.near_start()
    w_in.spread(0)
    for k in (1, 2, 3):
        got(k_ml[k], mrecv.at[k - 1])
    modall[...] = m1[...] + mrecv[0] + mrecv[1] + mrecv[2]
    for v in (a, b):
        v.normalise()
    w_out.spread(0)
    w_in.arrive(2)
    for v in (a, b):
        v.gather(1)
    w_in.arrive(1)
    w_in.arrive(3)
    for v in (a, b):
        v.gather(2)
    w_in.spread(2)
    w_out.arrive(2)
    w_in.spread(1)
    w_out.arrive(1)
    w_out.arrive(3)
    for v in (a, b):
        v.gather(3)
    w_in.spread(3)
    for v in (a, b):
        v.gather(4)
    w_out.spread(2)
    w_out.spread(1)
    w_out.forward()
    w_out.spread(3)
    a.gathered()
    b.gathered()
    w_in.end()
    a.first_matmul()
    b.first_matmul()
    w_out.end()
    ks_anchor = swap_out(lambda i: a_any.at[pl.ds(T * i, T)], abuf)

    u = (0, W)
    for it in range(ITERS):
        a, b = parts[it]
        if it:
            a.gathered()
            a.first_matmul()
        a.second_other(u)
        a.second_own(u)
        if it:
            b.gather(4)
            b.gathered()
        a.halves(u)
        a.scatter(1, u)
        if it:
            b.first_matmul()
        b.second_other(u)
        b.second_own(u)
        a.scatter(2, u)
        b.halves(u)
        b.scatter(1, u)
        a.scatter(3, u)
        b.scatter(2, u)
        a.scatter(4, u)
        b.scatter(3, u)
        a.scattered(u)
        if it + 1 == ITERS:
            a.out_send()
            b.scatter(4, u)
            b.scattered(u)
            b.out_send()
            a.out_add()
            b.out_add()
            continue
        a.prefix_send()
        b.scatter(4, u)
        b.scattered(u)
        b.prefix_send()
        swap_in(ks_anchor, abuf)
        after, later = parts[it + 1]
        a.prefix_add()
        after.stats(a.current())
        b.prefix_add()
        later.stats(b.current())
        after.normalise()
        later.normalise()
        for s in range(1, 4):
            after.gather(s)
            later.gather(s)
        after.gather(4)

    for copy in pending:
        copy.wait_send()
    for v in parts[0]:
        v.prefix_sent()
    for v in parts[1]:
        v.out_sent()
    for ks, src_of, dst in swaps:
        for i in range(2):

            @pl.when(jnp.logical_not(own[i]))
            def _(i=i):
                remote(src_of(i), dst.at[half], ks[i], ks[0] + half, swap[i]).wait_send()


def local(states, anchor, timesteps, step_sizes, weight_in, weight_out, mod_weight):
    vmem = pl.BlockSpec(memory_space=pltpu.VMEM)

    def each(make):
        return [make(n) for _, n in PARTS]

    scratch = [
        pltpu.SMEM((1,), jnp.int32),
        pltpu.SMEM((1,), F32),
        pltpu.VMEM(anchor.shape, F32),
        pltpu.VMEM((3, W, W), BF16),
        pltpu.VMEM((2, T, W), F32),
        pltpu.VMEM((2, T, W), F32),
        pltpu.VMEM((4, 8, W), F32),
        pltpu.VMEM((2, 8, W), F32),
        pltpu.VMEM((2, 8, W), F32),
        pltpu.VMEM((3, 2, 8, W), F32),
        pltpu.VMEM((2, 8, W), F32),
        pltpu.VMEM((D, U), BF16),
        pltpu.VMEM((4, U, 2 * W), BF16),
        pltpu.VMEM((2, T, W), F32),
        pltpu.VMEM((4, 2, T, W), BF16),
        each(lambda n: pltpu.VMEM((ITERS, n, 128), F32)),
        each(lambda n: pltpu.VMEM((ITERS, 3, n, 128), F32)),
        each(lambda n: pltpu.VMEM((ITERS, 4 * n, D), BF16)),
        each(lambda n: pltpu.VMEM((4 * n, U), BF16)),
        each(lambda n: pltpu.VMEM((ITERS, 2, 2, 4 * n, W), BF16)),
        each(lambda n: pltpu.VMEM((ITERS, 2, 2, 4 * n, W), BF16)),
        each(lambda n: pltpu.VMEM((2, 4, n, 2 * W), F32)),
        each(lambda n: pltpu.VMEM((ITERS, 4, 2, 2, n, W), BF16)),
        each(lambda n: pltpu.VMEM((ITERS, 4, 2, 2, n, W), BF16)),
        each(lambda n: pltpu.VMEM((2, n, W), BF16)),
        each(lambda n: pltpu.VMEM((3, 2, n, W), BF16)),
        each(lambda n: pltpu.VMEM((2, n, W), BF16)),
        each(lambda n: pltpu.VMEM((2, n, W), F32)),
        pltpu.SemaphoreType.DMA((COPIES,)),
        pltpu.SemaphoreType.DMA((COPIES,)),
    ]
    out = pl.pallas_call(
        kernel,
        out_shape=jax.ShapeDtypeStruct(anchor.shape, F32),
        in_specs=[pl.BlockSpec(memory_space=pl.ANY)] * 7,
        out_specs=vmem,
        scratch_shapes=scratch,
        compiler_params=pltpu.CompilerParams(
            collective_id=0, has_side_effects=True, vmem_limit_bytes=60 << 20
        ),
        name="picard",
    )(timesteps, step_sizes, states[0], anchor, mod_weight.transpose(1, 0, 2), weight_in, weight_out)
    return (anchor + out)[None]


def solution(mesh):
    placed = (
        P("tm", "row", "col"),
        P("row", "col"),
        P("tm"),
        P("tm"),
        P("col", "row"),
        P("row", "col"),
        P("row", None, "col"),
    )
    return jax.shard_map(
        local, mesh=mesh, in_specs=placed, out_specs=P("tm", "row", "col"), check_vma=False
    )
```

```python
import math

import jax
import jax.numpy as jnp
from jax import lax
from jax.experimental import pallas as pl
from jax.experimental.pallas import tpu as pltpu
from jax.sharding import PartitionSpec as P

D = 3072
ITERS = 2
EPSILON = 1e-06
MESH = pl.DeviceIdType.MESH
F32 = jnp.float32
BF16 = jnp.bfloat16

T = 80
W = 384
U = 768

PARTS = ((0, 32), (32, 48))

ORDER = ((0, 0), (1, 1), (0, 1), (1, 0))

COPIES = 304


def kernel(
    time_any, step_any, s_ref, a_any, m_any, wi_ref, wo_ref, out_ref,
    time_ref, step_ref, a_ref, m_ref,
    sbuf, abuf, modx, msib, m1, mrecv, modall, win, wout, pref, frecv,
    stat, statr, xall, hid, obs, obr, part, rss, rsr, dsend, drecv, fsend, drift,
    send, recv,
):
    y = lax.axis_index("tm")
    row = lax.axis_index("row")
    col = lax.axis_index("col")
    l, c = row // 2, lax.rem(row, 2)
    h, x = col // 4, lax.rem(col, 4)
    z = 4 * h + l

    def dev(x_=None, y_=None, z_=None, c_=None):
        x_ = x if x_ is None else x_
        y_ = y if y_ is None else y_
        z_ = z if z_ is None else z_
        c_ = c if c_ is None else c_
        return (y_, 2 * lax.rem(z_, 4) + c_, 4 * (z_ // 4) + x_)

    def xo(k):
        return lax.rem(x + k + 4, 4)

    def yo(k):
        return lax.rem(y + k + 4, 4)

    def zo(k):
        return lax.rem(z + k + 8, 8)

    sib = dev(c_=1 - c)
    z4 = dev(z_=zo(4))
    z4sib = dev(z_=zo(4), c_=1 - c)

    def lo(k):
        return dev(z_=4 * h + lax.rem(l + k, 4))

    ids = iter(range(COPIES))
    pending = []

    def remote(src, dst, ss, rs, to):
        return pltpu.make_async_remote_copy(
            src_ref=src, dst_ref=dst, send_sem=send.at[ss], recv_sem=recv.at[rs],
            device_id=to, device_id_type=MESH,
        )

    def put(k, src, dst, to):
        copy = remote(src, dst, k, k, to)
        copy.start()
        pending.append(copy)

    def got(k, dst):
        remote(dst, dst, k, k, sib).wait_recv()

    loads = [(time_any, time_ref), (m_any, m_ref), (step_any, step_ref)]
    loads = [pltpu.make_async_copy(*pair, recv.at[next(ids)]) for pair in loads]
    for copy in loads:
        copy.start()

    partners = [sib, z4, z4sib, dev(z_=zo(1)), dev(z_=zo(-1))]
    partners += [dev(x_=xo(k)) for k in (1, 2, 3)]
    partners += [dev(y_=yo(k)) for k in (1, 2, 3)]
    partners += [lo(k) for k in (1, 2, 3)]
    barrier = pltpu.get_barrier_semaphore()
    for p in partners:
        pl.semaphore_signal(barrier, inc=1, device_id=p, device_id_type=MESH)
    half = lax.rem(x, 2)
    same = x // 2 == c
    swap = [dev(x_=2 * c + i, c_=x // 2) for i in range(2)]
    swap_y = {(i, k): dev(x_=2 * c + i, c_=x // 2, y_=yo(k)) for i in range(2) for k in (1, 2, 3)}
    for p in swap_y.values():
        pl.semaphore_signal(barrier, inc=1, device_id=p, device_id_type=MESH)
    own = [jnp.logical_and(same, half == i) for i in range(2)]
    for i in range(2):

        @pl.when(jnp.logical_not(own[i]))
        def _(i=i):
            pl.semaphore_signal(barrier, inc=1, device_id=swap[i], device_id_type=MESH)

    for copy in loads[:2]:
        copy.wait()

    entry = (lax.rem(row, 4) * W + lax.broadcasted_iota(jnp.int32, (16, W), 1)).astype(F32)
    phase = time_ref[0].astype(F32) * jnp.exp(-math.log(10000.0) * entry / (D // 2))
    embedding = jnp.where(row < 4, jnp.cos(phase), jnp.sin(phase))
    high = embedding.astype(BF16).astype(F32)
    middle = (embedding - high).astype(BF16).astype(F32)
    low = embedding - high - middle
    line = lax.broadcasted_iota(jnp.int32, (16, W), 0)
    terms = jnp.where(line == 0, high, jnp.where(line == 1, middle, jnp.where(line == 2, low, 0.0)))
    modx[x] = jnp.zeros((8, W), F32)
    for r in range(3):
        products = jnp.dot(terms.astype(BF16), m_ref[r], preferred_element_type=F32)
        modx[x, r : r + 1, :] = jnp.sum(products, axis=0, keepdims=True)
    pl.semaphore_wait(barrier, len(partners) + len(swap_y) + 2 - same.astype(jnp.int32))

    swaps = []

    def swap_out(src_of, dst):
        ks = (next(ids), next(ids))
        for i in range(2):

            @pl.when(own[i])
            def _(i=i):
                pltpu.make_async_copy(src_of(i), dst.at[half], recv.at[ks[0] + half]).start()

            @pl.when(jnp.logical_not(own[i]))
            def _(i=i):
                remote(src_of(i), dst.at[half], ks[i], ks[0] + half, swap[i]).start()

        swaps.append((ks, src_of, dst))
        return ks

    def swap_in(ks, dst):
        for i in range(2):
            got(ks[i], dst.at[i])

    k_mx = {k: next(ids) for k in (1, 2, 3)}
    for k in (1, 2, 3):
        put(k_mx[k], modx.at[x], modx.at[x], dev(x_=xo(k)))
    ks_state = swap_out(lambda i: s_ref.at[pl.ds(T * i, T)], sbuf)

    mine = 4 * h + x
    far = 4 * (1 - h)

    def win_side():
        def slot_of(hx, first=0, rows=W):
            return win.at[pl.ds(pl.multiple_of(hx * W + first, 16), rows), :]

        def part_of(hd, first, rows):
            return wi_ref.at[pl.ds(pl.multiple_of(first, 16), rows), pl.ds(pl.multiple_of(hd * U, 128), U)]

        return part_of, slot_of, W

    def wout_side(col, cols):
        def slot_of(hx, first=0, rows=U):
            return wout.at[
                hx // 2,
                pl.ds(pl.multiple_of(first, 16), rows),
                pl.ds(pl.multiple_of(lax.rem(hx, 2) * W + col, 128), cols),
            ]

        def part_of(hd, first, rows):
            return wo_ref.at[pl.ds(pl.multiple_of(hd * U + first, 16), rows), col : col + cols]

        return part_of, slot_of, U

    class Side:
        def __init__(self, part_of, slot_of, rows, cross):
            self.part_of, self.slot_of, self.rows, self.q = part_of, slot_of, rows, rows // 4
            self.flows = range(5 if cross else 4)
            self.k_x = {k: next(ids) for k in (1, 3)}
            self.k_fwd = {} if cross else {k: next(ids) for k in (1, 3)}
            self.k_in = [next(ids) for _ in self.flows]
            self.k_y = {(s, k, f): next(ids) for s in self.flows for k in (1, 3) for f in range(2)}
            self.k_own = next(ids)

        def quarter(self, s, yy, first=0, rows=None):
            hx = 4 * h + xo(2) if s == 4 else far + xo(-s)
            return self.slot_of(hx, yy * self.q + first, rows or self.q)

        def far_start(self):
            put(self.k_in[0], self.part_of(1 - h, y * self.q, self.q), self.slot_of(mine, y * self.q, self.q), z4)

        def cross_start(self):
            to = dev(x_=xo(2))
            put(self.k_in[4], self.part_of(h, y * self.q, self.q), self.slot_of(mine, y * self.q, self.q), to)

        def near_start(self):
            for k in (1, 3):
                put(self.k_x[k], self.part_of(h, 0, self.rows), self.slot_of(mine), dev(x_=xo(k)))
            self.copy = pltpu.make_async_copy(self.part_of(h, 0, self.rows), self.slot_of(mine), recv.at[self.k_own])
            self.copy.start()

        def arrive(self, s):
            here = self.quarter(s, y)
            got(self.k_in[s], here)
            if s == 0:
                for k in (2, 1, 3):
                    put(self.k_in[k], here, here, dev(x_=xo(k)))
            for k in (1, 3):
                put(self.k_y[s, k, 0], here, here, dev(y_=yo(k)))

        def spread(self, s):
            for k, first in ((1, 0), (3, self.q // 2)):
                got(self.k_y[s, k, 0], self.quarter(s, yo(-k)))
                there = self.quarter(s, yo(-k), first, self.q // 2)
                put(self.k_y[s, k, 1], there, there, dev(y_=yo(k)))

        def forward(self):
            for k, first in ((1, 0), (3, self.rows // 2)):
                got(self.k_x[k], self.slot_of(4 * h + xo(-k)))
                there = self.slot_of(4 * h + xo(-k), first, self.rows // 2)
                put(self.k_fwd[k], there, there, dev(x_=xo(k)))

        def end(self):
            for k, first in ((1, 0), (3, self.rows // 2)):
                if self.k_fwd:
                    got(self.k_fwd[k], self.slot_of(4 * h + xo(2), first, self.rows // 2))
                else:
                    got(self.k_x[k], self.slot_of(4 * h + xo(-k)))
            for s in self.flows:
                for k, first in ((1, 0), (3, self.q // 2)):
                    got(self.k_y[s, k, 1], self.quarter(s, yo(2), first, self.q // 2))
            self.copy.wait()

    w_in = Side(*win_side(), True)
    w_out = Side(*wout_side(0, W), False)
    w_in.cross_start()
    w_in.far_start()
    w_in.near_start()

    def mod(j, r):
        return modall[j, r : r + 1, :]

    sign = (1, -1)

    class Part:
        def __init__(self, it, p):
            self.it, self.p = it, p
            self.first, self.n = PARTS[p]
            self.x, self.hid, self.part = xall[p].at[it], hid[p], part[p]
            self.k_stat = [next(ids) for _ in range(3)]
            steps = [(s, g, j) for s in range(1, 5) for j in range(2) for g in range(2)]
            self.k_ring = {key: next(ids) for key in steps if key[0] < 4 or key[1] == key[2]}
            self.k_sib = {key: next(ids) for key in self.k_ring}
            self.k_own = [next(ids) for _ in range(2)]
            self.units = ((0, W),)
            self.k_half = {(u, hh): next(ids) for u in self.units for hh in range(2)}
            self.k_sum = {
                u: {key: next(ids) for key in steps if key[0] > 1 or key[1] == key[2]} for u in self.units
            }
            self.k_prefix = {i: next(ids) for i in (1, 2, 3)}

        def rows(self):
            return slice(self.first, self.first + self.n)

        def stats(self, cur):
            self.cur = cur
            own, there = stat[self.p].at[self.it], statr[self.p].at[self.it]
            total = sum(jnp.sum(v, axis=1, keepdims=True) for v in cur)
            squares = sum(jnp.sum(v * v, axis=1, keepdims=True) for v in cur)
            lane = lax.broadcasted_iota(jnp.int32, (self.n, 128), 1)
            own[...] = jnp.where(lane < 64, total, squares)
            for i, to in enumerate((z4, z4sib, sib)):
                put(self.k_stat[i], own, there.at[i], to)

        def slot(self, zz, cc, j):
            hh, ll = zz // 4, lax.rem(zz, 4)
            return self.x.at[
                pl.ds(pl.multiple_of(ll * self.n, 16), self.n),
                pl.ds(pl.multiple_of((4 * hh + 2 * cc + j) * W, 128), W),
            ]

        def normalise(self):
            own, there = stat[self.p].at[self.it], statr[self.p].at[self.it]
            for i, k in enumerate(self.k_stat):
                got(k, there.at[i])
            total = own[...] + there[0] + there[1] + there[2]
            mean = total[:, 0:1] / D
            var = total[:, 64:65] / D - mean * mean
            scale = lax.rsqrt(var + EPSILON)
            for j in range(2):
                value = (self.cur[j] - mean) * scale * (1.0 + mod(j, 1)) + mod(j, 0)
                slot = self.slot(z, c, j)
                slot[...] = value.astype(BF16)
            for g, j in ORDER:
                slot = self.slot(z, c, j)
                put(self.k_ring[1, g, j], slot, slot, dev(z_=zo(sign[g])))
            for j in range(2):
                slot = self.slot(z, c, j)
                put(self.k_own[j], slot, slot, sib)

        def gather(self, s):
            for g, j in ORDER:
                if (s, g, j) not in self.k_ring:
                    continue
                slot = self.slot(zo(-sign[g] * s), c, j)
                got(self.k_ring[s, g, j], slot)
                if (s + 1, g, j) in self.k_ring:
                    put(self.k_ring[s + 1, g, j], slot, slot, dev(z_=zo(sign[g])))
                put(self.k_sib[s, g, j], slot, slot, sib)

        def gathered(self):
            for j in range(2):
                got(self.k_own[j], self.slot(z, 1 - c, j))
            for (s, g, j), k in self.k_sib.items():
                got(k, self.slot(zo(-sign[g] * s), 1 - c, j))

        def first_matmul(self):
            def tile(n, _):
                cols = pl.ds(pl.multiple_of(n * 256, 256), 256)
                pre = jnp.dot(self.x[...], win[:, cols], preferred_element_type=F32)
                self.hid[:, cols] = jax.nn.gelu(pre, approximate=True).astype(BF16)
                return 0

            lax.fori_loop(0, U // 256, tile, 0)

        def tiles(self, u):
            if u[1] < W:
                return [(j, u[0], u[1]) for j in range(2)]
            return [(None, 256 * n, 256) for n in range(3)]

        def second(self, cc, hh, u):
            for j, col, cols in self.tiles(u):
                at = col if j is None else W * j + col
                yield at, cols, jnp.dot(self.hid[...], wout[2 * hh + cc, :, at : at + cols], preferred_element_type=F32)

        def second_other(self, u):
            there, back = obs[self.p].at[self.it], obr[self.p].at[self.it]
            for hh in range(2):
                for at, cols, value in self.second(1 - c, hh, u):
                    for j, col in ((n // 3, n % 3 * 128) for n in range(at // 128, (at + cols) // 128)):
                        first = W * j + col - at
                        there[hh, j, :, col : col + 128] = value[:, first : first + 128].astype(BF16)
                cols = slice(u[0], u[0] + u[1])
                put(self.k_half[u, hh], there.at[hh, :, :, cols], back.at[hh, :, :, cols], sib)

        def second_own(self, u):
            for hh in range(2):
                for at, cols, value in self.second(c, hh, u):
                    self.part[hh, :, :, at : at + cols] = value.reshape(4, self.n, cols)

        def halves(self, u):
            back = obr[self.p].at[self.it]
            cols = slice(u[0], u[0] + u[1])
            for hh in range(2):
                got(self.k_half[u, hh], back.at[hh, :, :, cols])
                for j in range(2):
                    at = slice(W * j + u[0], W * j + u[0] + u[1])
                    self.part[hh, :, :, at] += back[hh, j, :, cols].astype(F32).reshape(4, self.n, u[1])

        def term(self, d, j, u):
            return self.part[d // 4, lax.rem(d, 4), :, W * j + u[0] : W * j + u[0] + u[1]]

        def scatter(self, s, u):
            k = self.k_sum[u]
            cols = slice(u[0], u[0] + u[1])
            out, back = rss[self.p].at[self.it], rsr[self.p].at[self.it]
            for g, j in ORDER:
                t = s if g == j else s + 1
                if t > 4:
                    continue
                value = self.term(zo(sign[g] * (5 - t)), j, u)
                if (t - 1, g, j) in k:
                    got(k[t - 1, g, j], back.at[t - 2, g, j, :, cols])
                    value = value + back[t - 2, g, j, :, cols].astype(F32)
                out[t - 1, g, j, :, cols] = value.astype(BF16)
                here, there = out.at[t - 1, g, j, :, cols], back.at[t - 1, g, j, :, cols]
                put(k[t, g, j], here, there, dev(z_=zo(sign[g])))

        def scattered(self, u):
            k = self.k_sum[u]
            cols = slice(u[0], u[0] + u[1])
            back = rsr[self.p].at[self.it]
            for j in range(2):
                value = self.term(z, j, u)
                for g in range(2):
                    got(k[4, g, j], back.at[3, g, j, :, cols])
                    value = value + back[3, g, j, :, cols].astype(F32)
                drift[self.p][j, :, cols] = step_ref[0] * mod(j, 2)[:, cols] * value

        def prefix_copy(self, i):
            return remote(
                dsend[self.p], drecv[self.p].at[i - 1], self.k_prefix[i], self.k_prefix[i], dev(y_=yo(i))
            )

        def prefix_send(self):
            for j in range(2):
                dsend[self.p][j] = drift[self.p][j].astype(BF16)
            for i in (1, 2, 3):

                @pl.when(y + i < 4)
                def _(i=i):
                    self.prefix_copy(i).start()

        def prefix_add(self):
            pref[:, self.rows(), :] = jnp.zeros((2, self.n, W), F32)
            for i in (3, 2, 1):

                @pl.when(y - i >= 0)
                def _(i=i):
                    got(self.k_prefix[i], drecv[self.p].at[i - 1])
                    for j in range(2):
                        pref[j, self.rows(), :] += drecv[self.p][i - 1, j].astype(F32)

        def prefix_sent(self):
            for i in (1, 2, 3):

                @pl.when(y + i < 4)
                def _(i=i):
                    self.prefix_copy(i).wait_send()

        def current(self):
            return [abuf[j, self.rows(), :] + pref[j, self.rows(), :] for j in range(2)]

        def out_copy(self, k, i):
            there = frecv.at[k, half, pl.ds(self.first, self.n)]
            to = swap[i] if k == 0 else swap_y[i, k]
            return remote(fsend[self.p].at[i], there, self.k_out[k, i], self.k_out[k, 0] + half, to)

        def out_send(self):
            self.k_out = {(k, i): next(ids) for k in range(4) for i in range(2)}
            for i in range(2):
                fsend[self.p][i] = drift[self.p][i].astype(BF16)
            for k in (3, 2, 1, 0):
                for i in range(2):
                    if k:

                        @pl.when(y + k < 4)
                        def _(i=i, k=k):
                            self.out_copy(k, i).start()

                    else:
                        there = frecv.at[0, half, pl.ds(self.first, self.n)]

                        @pl.when(own[i])
                        def _(i=i):
                            pltpu.make_async_copy(
                                fsend[self.p].at[i], there, recv.at[self.k_out[0, 0] + half]
                            ).start()

                        @pl.when(jnp.logical_not(own[i]))
                        def _(i=i):
                            self.out_copy(0, i).start()

        def out_sent(self):
            for k in range(4):
                for i in range(2):

                    @pl.when(y + k < 4 if k else jnp.logical_not(own[i]))
                    def _(i=i, k=k):
                        self.out_copy(k, i).wait_send()

        def out_add(self):
            for i in range(2):
                rows = slice(T * i + self.first, T * i + self.first + self.n)
                out_ref[rows, :] = jnp.zeros((self.n, W), F32)
                for k in (3, 2, 1, 0):

                    @pl.when(y - k >= 0)
                    def _(i=i, k=k):
                        got(self.k_out[k, i], frecv.at[k, i, pl.ds(self.first, self.n)])
                        out_ref[rows, :] += frecv[k, i, self.rows(), :].astype(F32)

    parts = [[Part(it, p) for p in range(2)] for it in range(ITERS)]
    a, b = parts[0]

    for copy in loads[2:]:
        copy.wait()

    for k in (1, 2, 3):
        got(k_mx[k], modx.at[xo(-k)])
    k_ms = next(ids)
    put(k_ms, modx.at[pl.ds(2 * (1 - c), 2)], msib, sib)
    swap_in(ks_state, sbuf)
    for v in (a, b):
        v.stats([sbuf[j, v.rows(), :] for j in range(2)])
    w_out.far_start()
    got(k_ms, msib)
    m1[...] = modx[pl.ds(2 * c, 2)] + msib[...]
    k_ml = {k: next(ids) for k in (1, 2, 3)}
    for k in (1, 2, 3):
        put(k_ml[k], m1, mrecv.at[k - 1], lo(k))
    w_in.arrive(4)
    w_in.arrive(0)
    w_in.spread(4)
    w_out.arrive(0)
    w_out.near_start()
    w_in.spread(0)
    for k in (1, 2, 3):
        got(k_ml[k], mrecv.at[k - 1])
    modall[...] = m1[...] + mrecv[0] + mrecv[1] + mrecv[2]
    for v in (a, b):
        v.normalise()
    w_out.spread(0)
    w_in.arrive(2)
    for v in (a, b):
        v.gather(1)
    w_in.arrive(1)
    w_in.arrive(3)
    for v in (a, b):
        v.gather(2)
    w_in.spread(2)
    w_out.arrive(2)
    w_in.spread(1)
    w_out.arrive(1)
    w_out.arrive(3)
    for v in (a, b):
        v.gather(3)
    w_in.spread(3)
    for v in (a, b):
        v.gather(4)
    w_out.forward()
    w_out.spread(2)
    w_out.spread(1)
    w_out.spread(3)
    a.gathered()
    b.gathered()
    w_in.end()
    a.first_matmul()
    b.first_matmul()
    w_out.end()
    ks_anchor = swap_out(lambda i: a_any.at[pl.ds(T * i, T)], abuf)

    u = (0, W)
    for it in range(ITERS):
        a, b = parts[it]
        if it:
            a.gathered()
            a.first_matmul()
        a.second_other(u)
        a.second_own(u)
        if it:
            b.gather(4)
            b.gathered()
        a.halves(u)
        a.scatter(1, u)
        if it:
            b.first_matmul()
        b.second_other(u)
        b.second_own(u)
        a.scatter(2, u)
        b.halves(u)
        b.scatter(1, u)
        a.scatter(3, u)
        b.scatter(2, u)
        a.scatter(4, u)
        b.scatter(3, u)
        a.scattered(u)
        if it + 1 == ITERS:
            a.out_send()
            b.scatter(4, u)
            b.scattered(u)
            b.out_send()
            a.out_add()
            b.out_add()
            continue
        a.prefix_send()
        b.scatter(4, u)
        b.scattered(u)
        b.prefix_send()
        swap_in(ks_anchor, abuf)
        after, later = parts[it + 1]
        a.prefix_add()
        after.stats(a.current())
        b.prefix_add()
        later.stats(b.current())
        after.normalise()
        later.normalise()
        for s in range(1, 4):
            after.gather(s)
            later.gather(s)
        after.gather(4)

    for copy in pending:
        copy.wait_send()
    for v in parts[0]:
        v.prefix_sent()
    for v in parts[1]:
        v.out_sent()
    for ks, src_of, dst in swaps:
        for i in range(2):

            @pl.when(jnp.logical_not(own[i]))
            def _(i=i):
                remote(src_of(i), dst.at[half], ks[i], ks[0] + half, swap[i]).wait_send()


def local(states, anchor, timesteps, step_sizes, weight_in, weight_out, mod_weight):
    vmem = pl.BlockSpec(memory_space=pltpu.VMEM)

    def each(make):
        return [make(n) for _, n in PARTS]

    scratch = [
        pltpu.SMEM((1,), jnp.int32),
        pltpu.SMEM((1,), F32),
        pltpu.VMEM(anchor.shape, F32),
        pltpu.VMEM((3, W, W), BF16),
        pltpu.VMEM((2, T, W), F32),
        pltpu.VMEM((2, T, W), F32),
        pltpu.VMEM((4, 8, W), F32),
        pltpu.VMEM((2, 8, W), F32),
        pltpu.VMEM((2, 8, W), F32),
        pltpu.VMEM((3, 2, 8, W), F32),
        pltpu.VMEM((2, 8, W), F32),
        pltpu.VMEM((D, U), BF16),
        pltpu.VMEM((4, U, 2 * W), BF16),
        pltpu.VMEM((2, T, W), F32),
        pltpu.VMEM((4, 2, T, W), BF16),
        each(lambda n: pltpu.VMEM((ITERS, n, 128), F32)),
        each(lambda n: pltpu.VMEM((ITERS, 3, n, 128), F32)),
        each(lambda n: pltpu.VMEM((ITERS, 4 * n, D), BF16)),
        each(lambda n: pltpu.VMEM((4 * n, U), BF16)),
        each(lambda n: pltpu.VMEM((ITERS, 2, 2, 4 * n, W), BF16)),
        each(lambda n: pltpu.VMEM((ITERS, 2, 2, 4 * n, W), BF16)),
        each(lambda n: pltpu.VMEM((2, 4, n, 2 * W), F32)),
        each(lambda n: pltpu.VMEM((ITERS, 4, 2, 2, n, W), BF16)),
        each(lambda n: pltpu.VMEM((ITERS, 4, 2, 2, n, W), BF16)),
        each(lambda n: pltpu.VMEM((2, n, W), BF16)),
        each(lambda n: pltpu.VMEM((3, 2, n, W), BF16)),
        each(lambda n: pltpu.VMEM((2, n, W), BF16)),
        each(lambda n: pltpu.VMEM((2, n, W), F32)),
        pltpu.SemaphoreType.DMA((COPIES,)),
        pltpu.SemaphoreType.DMA((COPIES,)),
    ]
    out = pl.pallas_call(
        kernel,
        out_shape=jax.ShapeDtypeStruct(anchor.shape, F32),
        in_specs=[pl.BlockSpec(memory_space=pl.ANY)] * 7,
        out_specs=vmem,
        scratch_shapes=scratch,
        compiler_params=pltpu.CompilerParams(
            collective_id=0, has_side_effects=True, vmem_limit_bytes=60 << 20
        ),
        name="picard",
    )(timesteps, step_sizes, states[0], anchor, mod_weight.transpose(1, 0, 2), weight_in, weight_out)
    return (anchor + out)[None]


def solution(mesh):
    placed = (
        P("tm", "row", "col"),
        P("row", "col"),
        P("tm"),
        P("tm"),
        P("col", "row"),
        P("row", "col"),
        P("row", None, "col"),
    )
    return jax.shard_map(
        local, mesh=mesh, in_specs=placed, out_specs=P("tm", "row", "col"), check_vma=False
    )
```

```python
import math

import jax
import jax.numpy as jnp
from jax import lax
from jax.experimental import pallas as pl
from jax.experimental.pallas import tpu as pltpu
from jax.sharding import PartitionSpec as P

D = 3072
ITERS = 2
EPSILON = 1e-06
MESH = pl.DeviceIdType.MESH
F32 = jnp.float32
BF16 = jnp.bfloat16

T = 80
W = 384
U = 768

PARTS = ((0, 32), (32, 48))

ORDER = ((0, 0), (1, 1), (0, 1), (1, 0))

COPIES = 304


def kernel(
    time_any, step_any, s_ref, a_any, m_any, wi_ref, wo_ref, out_ref,
    time_ref, step_ref, a_ref, m_ref,
    sbuf, abuf, modx, msib, m1, mrecv, modall, win, wout, pref, frecv,
    stat, statr, xall, hid, obs, obr, part, rss, rsr, dsend, drecv, fsend, drift, acc,
    send, recv,
):
    y = lax.axis_index("tm")
    row = lax.axis_index("row")
    col = lax.axis_index("col")
    l, c = row // 2, lax.rem(row, 2)
    h, x = col // 4, lax.rem(col, 4)
    z = 4 * h + l

    def dev(x_=None, y_=None, z_=None, c_=None):
        x_ = x if x_ is None else x_
        y_ = y if y_ is None else y_
        z_ = z if z_ is None else z_
        c_ = c if c_ is None else c_
        return (y_, 2 * lax.rem(z_, 4) + c_, 4 * (z_ // 4) + x_)

    def xo(k):
        return lax.rem(x + k + 4, 4)

    def yo(k):
        return lax.rem(y + k + 4, 4)

    def zo(k):
        return lax.rem(z + k + 8, 8)

    sib = dev(c_=1 - c)
    z4 = dev(z_=zo(4))
    z4sib = dev(z_=zo(4), c_=1 - c)

    def lo(k):
        return dev(z_=4 * h + lax.rem(l + k, 4))

    ids = iter(range(COPIES))
    pending = []

    def remote(src, dst, ss, rs, to):
        return pltpu.make_async_remote_copy(
            src_ref=src, dst_ref=dst, send_sem=send.at[ss], recv_sem=recv.at[rs],
            device_id=to, device_id_type=MESH,
        )

    def put(k, src, dst, to):
        copy = remote(src, dst, k, k, to)
        copy.start()
        pending.append(copy)

    def got(k, dst):
        remote(dst, dst, k, k, sib).wait_recv()

    loads = [(time_any, time_ref), (m_any, m_ref), (step_any, step_ref)]
    loads = [pltpu.make_async_copy(*pair, recv.at[next(ids)]) for pair in loads]
    for copy in loads:
        copy.start()

    partners = [sib, z4, z4sib, dev(z_=zo(1)), dev(z_=zo(-1))]
    partners += [dev(x_=xo(k)) for k in (1, 2, 3)]
    partners += [dev(y_=yo(k)) for k in (1, 2, 3)]
    partners += [lo(k) for k in (1, 2, 3)]
    barrier = pltpu.get_barrier_semaphore()
    for p in partners:
        pl.semaphore_signal(barrier, inc=1, device_id=p, device_id_type=MESH)
    half = lax.rem(x, 2)
    same = x // 2 == c
    swap = [dev(x_=2 * c + i, c_=x // 2) for i in range(2)]
    swap_y = {(i, k): dev(x_=2 * c + i, c_=x // 2, y_=yo(k)) for i in range(2) for k in (1, 2, 3)}
    for p in swap_y.values():
        pl.semaphore_signal(barrier, inc=1, device_id=p, device_id_type=MESH)
    own = [jnp.logical_and(same, half == i) for i in range(2)]
    for i in range(2):

        @pl.when(jnp.logical_not(own[i]))
        def _(i=i):
            pl.semaphore_signal(barrier, inc=1, device_id=swap[i], device_id_type=MESH)

    for copy in loads[:2]:
        copy.wait()

    entry = (lax.rem(row, 4) * W + lax.broadcasted_iota(jnp.int32, (16, W), 1)).astype(F32)
    phase = time_ref[0].astype(F32) * jnp.exp(-math.log(10000.0) * entry / (D // 2))
    embedding = jnp.where(row < 4, jnp.cos(phase), jnp.sin(phase))
    high = embedding.astype(BF16).astype(F32)
    middle = (embedding - high).astype(BF16).astype(F32)
    low = embedding - high - middle
    line = lax.broadcasted_iota(jnp.int32, (16, W), 0)
    terms = jnp.where(line == 0, high, jnp.where(line == 1, middle, jnp.where(line == 2, low, 0.0)))
    modx[x] = jnp.zeros((8, W), F32)
    for r in range(3):
        products = jnp.dot(terms.astype(BF16), m_ref[r], preferred_element_type=F32)
        modx[x, r : r + 1, :] = jnp.sum(products, axis=0, keepdims=True)
    pl.semaphore_wait(barrier, len(partners) + len(swap_y) + 2 - same.astype(jnp.int32))

    swaps = []

    def swap_out(src_of, dst):
        ks = (next(ids), next(ids))
        for i in range(2):

            @pl.when(own[i])
            def _(i=i):
                pltpu.make_async_copy(src_of(i), dst.at[half], recv.at[ks[0] + half]).start()

            @pl.when(jnp.logical_not(own[i]))
            def _(i=i):
                remote(src_of(i), dst.at[half], ks[i], ks[0] + half, swap[i]).start()

        swaps.append((ks, src_of, dst))
        return ks

    def swap_in(ks, dst):
        for i in range(2):
            got(ks[i], dst.at[i])

    k_mx = {k: next(ids) for k in (1, 2, 3)}
    for k in (1, 2, 3):
        put(k_mx[k], modx.at[x], modx.at[x], dev(x_=xo(k)))
    ks_state = swap_out(lambda i: s_ref.at[pl.ds(T * i, T)], sbuf)

    mine = 4 * h + x
    far = 4 * (1 - h)

    def win_side():
        def slot_of(hx, first=0, rows=W):
            return win.at[pl.ds(pl.multiple_of(hx * W + first, 16), rows), :]

        def part_of(hd, first, rows):
            return wi_ref.at[pl.ds(pl.multiple_of(first, 16), rows), pl.ds(pl.multiple_of(hd * U, 128), U)]

        return part_of, slot_of, W

    def wout_side(col, cols):
        def slot_of(hx, first=0, rows=U):
            return wout.at[
                hx // 2,
                pl.ds(pl.multiple_of(first, 16), rows),
                pl.ds(pl.multiple_of(lax.rem(hx, 2) * W + col, 128), cols),
            ]

        def part_of(hd, first, rows):
            return wo_ref.at[pl.ds(pl.multiple_of(hd * U + first, 16), rows), col : col + cols]

        return part_of, slot_of, U

    class Side:
        def __init__(self, part_of, slot_of, rows, cross):
            self.part_of, self.slot_of, self.rows, self.q = part_of, slot_of, rows, rows // 4
            self.flows = range(5 if cross else 4)
            self.k_x = {k: next(ids) for k in (1, 3)}
            self.k_fwd = {} if cross else {k: next(ids) for k in (1, 3)}
            self.k_in = [next(ids) for _ in self.flows]
            self.k_y = {(s, k, f): next(ids) for s in self.flows for k in (1, 3) for f in range(2)}
            self.k_own = next(ids)

        def quarter(self, s, yy, first=0, rows=None):
            hx = 4 * h + xo(2) if s == 4 else far + xo(-s)
            return self.slot_of(hx, yy * self.q + first, rows or self.q)

        def far_start(self):
            put(self.k_in[0], self.part_of(1 - h, y * self.q, self.q), self.slot_of(mine, y * self.q, self.q), z4)

        def cross_start(self):
            to = dev(x_=xo(2))
            put(self.k_in[4], self.part_of(h, y * self.q, self.q), self.slot_of(mine, y * self.q, self.q), to)

        def near_start(self):
            for k in (1, 3):
                put(self.k_x[k], self.part_of(h, 0, self.rows), self.slot_of(mine), dev(x_=xo(k)))
            self.copy = pltpu.make_async_copy(self.part_of(h, 0, self.rows), self.slot_of(mine), recv.at[self.k_own])
            self.copy.start()

        def arrive(self, s):
            here = self.quarter(s, y)
            got(self.k_in[s], here)
            if s == 0:
                for k in (2, 1, 3):
                    put(self.k_in[k], here, here, dev(x_=xo(k)))
            for k in (1, 3):
                put(self.k_y[s, k, 0], here, here, dev(y_=yo(k)))

        def spread(self, s):
            for k, first in ((1, 0), (3, self.q // 2)):
                got(self.k_y[s, k, 0], self.quarter(s, yo(-k)))
                there = self.quarter(s, yo(-k), first, self.q // 2)
                put(self.k_y[s, k, 1], there, there, dev(y_=yo(k)))

        def forward(self):
            for k, first in ((1, 0), (3, self.rows // 2)):
                got(self.k_x[k], self.slot_of(4 * h + xo(-k)))
                there = self.slot_of(4 * h + xo(-k), first, self.rows // 2)
                put(self.k_fwd[k], there, there, dev(x_=xo(k)))

        def end(self):
            for k, first in ((1, 0), (3, self.rows // 2)):
                if self.k_fwd:
                    got(self.k_fwd[k], self.slot_of(4 * h + xo(2), first, self.rows // 2))
                else:
                    got(self.k_x[k], self.slot_of(4 * h + xo(-k)))
            for s in self.flows:
                for k, first in ((1, 0), (3, self.q // 2)):
                    got(self.k_y[s, k, 1], self.quarter(s, yo(2), first, self.q // 2))
            self.copy.wait()

    w_in = Side(*win_side(), True)
    w_out = Side(*wout_side(0, W), False)
    w_in.cross_start()
    w_in.far_start()
    w_in.near_start()

    def mod(j, r):
        return modall[j, r : r + 1, :]

    sign = (1, -1)

    class Part:
        def __init__(self, it, p):
            self.it, self.p = it, p
            self.first, self.n = PARTS[p]
            self.x, self.hid, self.part = xall[p].at[it], hid[p], part[p]
            self.k_stat = [next(ids) for _ in range(3)]
            steps = [(s, g, j) for s in range(1, 5) for j in range(2) for g in range(2)]
            self.k_ring = {key: next(ids) for key in steps if key[0] < 4 or key[1] == key[2]}
            self.k_sib = {key: next(ids) for key in self.k_ring}
            self.k_own = [next(ids) for _ in range(2)]
            self.units = ((0, W),)
            self.k_half = {(u, hh): next(ids) for u in self.units for hh in range(2)}
            self.k_sum = {
                u: {key: next(ids) for key in steps if key[0] > 1 or key[1] == key[2]} for u in self.units
            }
            self.k_prefix = {i: next(ids) for i in (1, 2, 3)}

        def rows(self):
            return slice(self.first, self.first + self.n)

        def stats(self, cur):
            self.cur = cur
            own, there = stat[self.p].at[self.it], statr[self.p].at[self.it]
            total = sum(jnp.sum(v, axis=1, keepdims=True) for v in cur)
            squares = sum(jnp.sum(v * v, axis=1, keepdims=True) for v in cur)
            lane = lax.broadcasted_iota(jnp.int32, (self.n, 128), 1)
            own[...] = jnp.where(lane < 64, total, squares)
            for i, to in enumerate((z4, z4sib, sib)):
                put(self.k_stat[i], own, there.at[i], to)

        def slot(self, zz, cc, j):
            hh, ll = zz // 4, lax.rem(zz, 4)
            return self.x.at[
                pl.ds(pl.multiple_of(ll * self.n, 16), self.n),
                pl.ds(pl.multiple_of((4 * hh + 2 * cc + j) * W, 128), W),
            ]

        def normalise(self):
            own, there = stat[self.p].at[self.it], statr[self.p].at[self.it]
            for i, k in enumerate(self.k_stat):
                got(k, there.at[i])
            total = own[...] + there[0] + there[1] + there[2]
            mean = total[:, 0:1] / D
            var = total[:, 64:65] / D - mean * mean
            scale = lax.rsqrt(var + EPSILON)
            for j in range(2):
                value = (self.cur[j] - mean) * scale * (1.0 + mod(j, 1)) + mod(j, 0)
                slot = self.slot(z, c, j)
                slot[...] = value.astype(BF16)
            for g, j in ORDER:
                slot = self.slot(z, c, j)
                put(self.k_ring[1, g, j], slot, slot, dev(z_=zo(sign[g])))
            for j in range(2):
                slot = self.slot(z, c, j)
                put(self.k_own[j], slot, slot, sib)

        def gather(self, s):
            for g, j in ORDER:
                if (s, g, j) not in self.k_ring:
                    continue
                slot = self.slot(zo(-sign[g] * s), c, j)
                got(self.k_ring[s, g, j], slot)
                if (s + 1, g, j) in self.k_ring:
                    put(self.k_ring[s + 1, g, j], slot, slot, dev(z_=zo(sign[g])))
                put(self.k_sib[s, g, j], slot, slot, sib)

        def gathered(self, steps=(1, 2, 3, 4)):
            if 1 in steps:
                for j in range(2):
                    got(self.k_own[j], self.slot(z, 1 - c, j))
            for (s, g, j), k in self.k_sib.items():
                if s in steps:
                    got(k, self.slot(zo(-sign[g] * s), 1 - c, j))

        def first_matmul(self):
            def tile(n, _):
                cols = pl.ds(pl.multiple_of(n * 256, 256), 256)
                pre = jnp.dot(self.x[...], win[:, cols], preferred_element_type=F32)
                self.hid[:, cols] = jax.nn.gelu(pre, approximate=True).astype(BF16)
                return 0

            lax.fori_loop(0, U // 256, tile, 0)

        def tiles(self, u):
            if u[1] < W:
                return [(j, u[0], u[1]) for j in range(2)]
            return [(None, 256 * n, 256) for n in range(3)]

        def first_half(self, hh, last):
            rows = pl.ds(pl.multiple_of(hh * (D // 2), 128), D // 2)
            for n in range(U // 256):
                cols = slice(256 * n, 256 * n + 256)
                pre = jnp.dot(self.x[:, rows], win[rows, cols], preferred_element_type=F32)
                if last:
                    pre = pre + acc[self.p][:, cols]
                    self.hid[:, cols] = jax.nn.gelu(pre, approximate=True).astype(BF16)
                else:
                    acc[self.p][:, cols] = pre

        def second(self, cc, hh, u):
            for j, col, cols in self.tiles(u):
                at = col if j is None else W * j + col
                yield at, cols, jnp.dot(self.hid[...], wout[2 * hh + cc, :, at : at + cols], preferred_element_type=F32)

        def second_other(self, u):
            there, back = obs[self.p].at[self.it], obr[self.p].at[self.it]
            for hh in range(2):
                for at, cols, value in self.second(1 - c, hh, u):
                    for j, col in ((n // 3, n % 3 * 128) for n in range(at // 128, (at + cols) // 128)):
                        first = W * j + col - at
                        there[hh, j, :, col : col + 128] = value[:, first : first + 128].astype(BF16)
                cols = slice(u[0], u[0] + u[1])
                put(self.k_half[u, hh], there.at[hh, :, :, cols], back.at[hh, :, :, cols], sib)

        def second_own(self, u):
            for hh in range(2):
                for at, cols, value in self.second(c, hh, u):
                    self.part[hh, :, :, at : at + cols] = value.reshape(4, self.n, cols)

        def halves(self, u):
            back = obr[self.p].at[self.it]
            cols = slice(u[0], u[0] + u[1])
            for hh in range(2):
                got(self.k_half[u, hh], back.at[hh, :, :, cols])
                for j in range(2):
                    at = slice(W * j + u[0], W * j + u[0] + u[1])
                    self.part[hh, :, :, at] += back[hh, j, :, cols].astype(F32).reshape(4, self.n, u[1])

        def term(self, d, j, u):
            return self.part[d // 4, lax.rem(d, 4), :, W * j + u[0] : W * j + u[0] + u[1]]

        def scatter(self, s, u):
            k = self.k_sum[u]
            cols = slice(u[0], u[0] + u[1])
            out, back = rss[self.p].at[self.it], rsr[self.p].at[self.it]
            for g, j in ORDER:
                t = s if g == j else s + 1
                if t > 4:
                    continue
                value = self.term(zo(sign[g] * (5 - t)), j, u)
                if (t - 1, g, j) in k:
                    got(k[t - 1, g, j], back.at[t - 2, g, j, :, cols])
                    value = value + back[t - 2, g, j, :, cols].astype(F32)
                out[t - 1, g, j, :, cols] = value.astype(BF16)
                here, there = out.at[t - 1, g, j, :, cols], back.at[t - 1, g, j, :, cols]
                put(k[t, g, j], here, there, dev(z_=zo(sign[g])))

        def scattered(self, u):
            k = self.k_sum[u]
            cols = slice(u[0], u[0] + u[1])
            back = rsr[self.p].at[self.it]
            for j in range(2):
                value = self.term(z, j, u)
                for g in range(2):
                    got(k[4, g, j], back.at[3, g, j, :, cols])
                    value = value + back[3, g, j, :, cols].astype(F32)
                drift[self.p][j, :, cols] = step_ref[0] * mod(j, 2)[:, cols] * value

        def prefix_copy(self, i):
            return remote(
                dsend[self.p], drecv[self.p].at[i - 1], self.k_prefix[i], self.k_prefix[i], dev(y_=yo(i))
            )

        def prefix_send(self):
            for j in range(2):
                dsend[self.p][j] = drift[self.p][j].astype(BF16)
            for i in (1, 2, 3):

                @pl.when(y + i < 4)
                def _(i=i):
                    self.prefix_copy(i).start()

        def prefix_add(self):
            pref[:, self.rows(), :] = jnp.zeros((2, self.n, W), F32)
            for i in (3, 2, 1):

                @pl.when(y - i >= 0)
                def _(i=i):
                    got(self.k_prefix[i], drecv[self.p].at[i - 1])
                    for j in range(2):
                        pref[j, self.rows(), :] += drecv[self.p][i - 1, j].astype(F32)

        def prefix_sent(self):
            for i in (1, 2, 3):

                @pl.when(y + i < 4)
                def _(i=i):
                    self.prefix_copy(i).wait_send()

        def current(self):
            return [abuf[j, self.rows(), :] + pref[j, self.rows(), :] for j in range(2)]

        def out_copy(self, k, i):
            there = frecv.at[k, half, pl.ds(self.first, self.n)]
            to = swap[i] if k == 0 else swap_y[i, k]
            return remote(fsend[self.p].at[i], there, self.k_out[k, i], self.k_out[k, 0] + half, to)

        def out_send(self):
            self.k_out = {(k, i): next(ids) for k in range(4) for i in range(2)}
            for i in range(2):
                fsend[self.p][i] = drift[self.p][i].astype(BF16)
            for k in (3, 2, 1, 0):
                for i in range(2):
                    if k:

                        @pl.when(y + k < 4)
                        def _(i=i, k=k):
                            self.out_copy(k, i).start()

                    else:
                        there = frecv.at[0, half, pl.ds(self.first, self.n)]

                        @pl.when(own[i])
                        def _(i=i):
                            pltpu.make_async_copy(
                                fsend[self.p].at[i], there, recv.at[self.k_out[0, 0] + half]
                            ).start()

                        @pl.when(jnp.logical_not(own[i]))
                        def _(i=i):
                            self.out_copy(0, i).start()

        def out_sent(self):
            for k in range(4):
                for i in range(2):

                    @pl.when(y + k < 4 if k else jnp.logical_not(own[i]))
                    def _(i=i, k=k):
                        self.out_copy(k, i).wait_send()

        def out_add(self):
            for i in range(2):
                rows = slice(T * i + self.first, T * i + self.first + self.n)
                out_ref[rows, :] = jnp.zeros((self.n, W), F32)
                for k in (3, 2, 1, 0):

                    @pl.when(y - k >= 0)
                    def _(i=i, k=k):
                        got(self.k_out[k, i], frecv.at[k, i, pl.ds(self.first, self.n)])
                        out_ref[rows, :] += frecv[k, i, self.rows(), :].astype(F32)

    parts = [[Part(it, p) for p in range(2)] for it in range(ITERS)]
    a, b = parts[0]

    for copy in loads[2:]:
        copy.wait()

    for k in (1, 2, 3):
        got(k_mx[k], modx.at[xo(-k)])
    k_ms = next(ids)
    put(k_ms, modx.at[pl.ds(2 * (1 - c), 2)], msib, sib)
    swap_in(ks_state, sbuf)
    for v in (a, b):
        v.stats([sbuf[j, v.rows(), :] for j in range(2)])
    w_out.far_start()
    got(k_ms, msib)
    m1[...] = modx[pl.ds(2 * c, 2)] + msib[...]
    k_ml = {k: next(ids) for k in (1, 2, 3)}
    for k in (1, 2, 3):
        put(k_ml[k], m1, mrecv.at[k - 1], lo(k))
    w_in.arrive(4)
    w_in.arrive(0)
    w_in.spread(4)
    w_out.arrive(0)
    w_out.near_start()
    w_in.spread(0)
    for k in (1, 2, 3):
        got(k_ml[k], mrecv.at[k - 1])
    modall[...] = m1[...] + mrecv[0] + mrecv[1] + mrecv[2]
    for v in (a, b):
        v.normalise()
    w_out.spread(0)
    w_in.arrive(2)
    for v in (a, b):
        v.gather(1)
    w_in.arrive(1)
    w_in.arrive(3)
    for v in (a, b):
        v.gather(2)
    w_in.spread(2)
    w_out.arrive(2)
    w_in.spread(1)
    w_out.arrive(1)
    w_out.arrive(3)
    for v in (a, b):
        v.gather(3)
    w_in.spread(3)
    for v in (a, b):
        v.gather(4)
    w_out.forward()
    w_out.spread(2)
    w_out.spread(1)
    w_out.spread(3)
    a.gathered()
    b.gathered()
    w_in.end()
    a.first_matmul()
    b.first_matmul()
    w_out.end()
    ks_anchor = swap_out(lambda i: a_any.at[pl.ds(T * i, T)], abuf)

    u = (0, W)
    for it in range(ITERS):
        a, b = parts[it]
        if it:
            a.gathered((4,))
            a.first_half(1 - h, True)
        a.second_other(u)
        a.second_own(u)
        if it:
            b.gathered((4,))
        a.halves(u)
        a.scatter(1, u)
        if it:
            b.first_half(1 - h, True)
        b.second_other(u)
        b.second_own(u)
        a.scatter(2, u)
        b.halves(u)
        b.scatter(1, u)
        a.scatter(3, u)
        b.scatter(2, u)
        a.scatter(4, u)
        b.scatter(3, u)
        a.scattered(u)
        if it + 1 == ITERS:
            a.out_send()
            b.scatter(4, u)
            b.scattered(u)
            b.out_send()
            a.out_add()
            b.out_add()
            continue
        a.prefix_send()
        b.scatter(4, u)
        b.scattered(u)
        b.prefix_send()
        swap_in(ks_anchor, abuf)
        after, later = parts[it + 1]
        a.prefix_add()
        after.stats(a.current())
        b.prefix_add()
        later.stats(b.current())
        after.normalise()
        later.normalise()
        for s in range(1, 4):
            after.gather(s)
            later.gather(s)
        after.gathered((1, 2, 3))
        after.first_half(h, False)
        after.gather(4)
        later.gathered((1, 2, 3))
        later.first_half(h, False)
        later.gather(4)

    for copy in pending:
        copy.wait_send()
    for v in parts[0]:
        v.prefix_sent()
    for v in parts[1]:
        v.out_sent()
    for ks, src_of, dst in swaps:
        for i in range(2):

            @pl.when(jnp.logical_not(own[i]))
            def _(i=i):
                remote(src_of(i), dst.at[half], ks[i], ks[0] + half, swap[i]).wait_send()


def local(states, anchor, timesteps, step_sizes, weight_in, weight_out, mod_weight):
    vmem = pl.BlockSpec(memory_space=pltpu.VMEM)

    def each(make):
        return [make(n) for _, n in PARTS]

    scratch = [
        pltpu.SMEM((1,), jnp.int32),
        pltpu.SMEM((1,), F32),
        pltpu.VMEM(anchor.shape, F32),
        pltpu.VMEM((3, W, W), BF16),
        pltpu.VMEM((2, T, W), F32),
        pltpu.VMEM((2, T, W), F32),
        pltpu.VMEM((4, 8, W), F32),
        pltpu.VMEM((2, 8, W), F32),
        pltpu.VMEM((2, 8, W), F32),
        pltpu.VMEM((3, 2, 8, W), F32),
        pltpu.VMEM((2, 8, W), F32),
        pltpu.VMEM((D, U), BF16),
        pltpu.VMEM((4, U, 2 * W), BF16),
        pltpu.VMEM((2, T, W), F32),
        pltpu.VMEM((4, 2, T, W), BF16),
        each(lambda n: pltpu.VMEM((ITERS, n, 128), F32)),
        each(lambda n: pltpu.VMEM((ITERS, 3, n, 128), F32)),
        each(lambda n: pltpu.VMEM((ITERS, 4 * n, D), BF16)),
        each(lambda n: pltpu.VMEM((4 * n, U), BF16)),
        each(lambda n: pltpu.VMEM((ITERS, 2, 2, 4 * n, W), BF16)),
        each(lambda n: pltpu.VMEM((ITERS, 2, 2, 4 * n, W), BF16)),
        each(lambda n: pltpu.VMEM((2, 4, n, 2 * W), F32)),
        each(lambda n: pltpu.VMEM((ITERS, 4, 2, 2, n, W), BF16)),
        each(lambda n: pltpu.VMEM((ITERS, 4, 2, 2, n, W), BF16)),
        each(lambda n: pltpu.VMEM((2, n, W), BF16)),
        each(lambda n: pltpu.VMEM((3, 2, n, W), BF16)),
        each(lambda n: pltpu.VMEM((2, n, W), BF16)),
        each(lambda n: pltpu.VMEM((2, n, W), F32)),
        each(lambda n: pltpu.VMEM((4 * n, U), F32)),
        pltpu.SemaphoreType.DMA((COPIES,)),
        pltpu.SemaphoreType.DMA((COPIES,)),
    ]
    out = pl.pallas_call(
        kernel,
        out_shape=jax.ShapeDtypeStruct(anchor.shape, F32),
        in_specs=[pl.BlockSpec(memory_space=pl.ANY)] * 7,
        out_specs=vmem,
        scratch_shapes=scratch,
        compiler_params=pltpu.CompilerParams(
            collective_id=0, has_side_effects=True, vmem_limit_bytes=60 << 20
        ),
        name="picard",
    )(timesteps, step_sizes, states[0], anchor, mod_weight.transpose(1, 0, 2), weight_in, weight_out)
    return (anchor + out)[None]


def solution(mesh):
    placed = (
        P("tm", "row", "col"),
        P("row", "col"),
        P("tm"),
        P("tm"),
        P("col", "row"),
        P("row", "col"),
        P("row", None, "col"),
    )
    return jax.shard_map(
        local, mesh=mesh, in_specs=placed, out_specs=P("tm", "row", "col"), check_vma=False
    )
```

```python
import math

import jax
import jax.numpy as jnp
from jax import lax
from jax.experimental import pallas as pl
from jax.experimental.pallas import tpu as pltpu
from jax.sharding import PartitionSpec as P

D = 3072
ITERS = 2
EPSILON = 1e-06
MESH = pl.DeviceIdType.MESH
F32 = jnp.float32
BF16 = jnp.bfloat16

T = 80
W = 384
U = 768

PARTS = ((0, 32), (32, 48))

ORDER = ((0, 0), (1, 1), (0, 1), (1, 0))

COPIES = 304


def kernel(
    time_any, step_any, s_ref, a_any, m_any, wi_ref, wo_ref, out_ref,
    time_ref, step_ref, a_ref, m_ref,
    sbuf, abuf, modx, msib, m1, mrecv, modall, win, wout, pref, frecv,
    stat, statr, xall, hid, obs, obr, part, rss, rsr, dsend, drecv, fsend, drift, acc,
    send, recv,
):
    y = lax.axis_index("tm")
    row = lax.axis_index("row")
    col = lax.axis_index("col")
    l, c = row // 2, lax.rem(row, 2)
    h, x = col // 4, lax.rem(col, 4)
    z = 4 * h + l

    def dev(x_=None, y_=None, z_=None, c_=None):
        x_ = x if x_ is None else x_
        y_ = y if y_ is None else y_
        z_ = z if z_ is None else z_
        c_ = c if c_ is None else c_
        return (y_, 2 * lax.rem(z_, 4) + c_, 4 * (z_ // 4) + x_)

    def xo(k):
        return lax.rem(x + k + 4, 4)

    def yo(k):
        return lax.rem(y + k + 4, 4)

    def zo(k):
        return lax.rem(z + k + 8, 8)

    sib = dev(c_=1 - c)
    z4 = dev(z_=zo(4))
    z4sib = dev(z_=zo(4), c_=1 - c)

    def lo(k):
        return dev(z_=4 * h + lax.rem(l + k, 4))

    ids = iter(range(COPIES))
    pending = []

    def remote(src, dst, ss, rs, to):
        return pltpu.make_async_remote_copy(
            src_ref=src, dst_ref=dst, send_sem=send.at[ss], recv_sem=recv.at[rs],
            device_id=to, device_id_type=MESH,
        )

    def put(k, src, dst, to):
        copy = remote(src, dst, k, k, to)
        copy.start()
        pending.append(copy)

    def got(k, dst):
        remote(dst, dst, k, k, sib).wait_recv()

    loads = [(time_any, time_ref), (m_any, m_ref), (step_any, step_ref)]
    loads = [pltpu.make_async_copy(*pair, recv.at[next(ids)]) for pair in loads]
    for copy in loads:
        copy.start()

    partners = [sib, z4, z4sib, dev(z_=zo(1)), dev(z_=zo(-1))]
    partners += [dev(x_=xo(k)) for k in (1, 2, 3)]
    partners += [dev(y_=yo(k)) for k in (1, 2, 3)]
    partners += [lo(k) for k in (1, 2, 3)]
    barrier = pltpu.get_barrier_semaphore()
    for p in partners:
        pl.semaphore_signal(barrier, inc=1, device_id=p, device_id_type=MESH)
    half = lax.rem(x, 2)
    same = x // 2 == c
    swap = [dev(x_=2 * c + i, c_=x // 2) for i in range(2)]
    swap_y = {(i, k): dev(x_=2 * c + i, c_=x // 2, y_=yo(k)) for i in range(2) for k in (1, 2, 3)}
    for p in swap_y.values():
        pl.semaphore_signal(barrier, inc=1, device_id=p, device_id_type=MESH)
    own = [jnp.logical_and(same, half == i) for i in range(2)]
    for i in range(2):

        @pl.when(jnp.logical_not(own[i]))
        def _(i=i):
            pl.semaphore_signal(barrier, inc=1, device_id=swap[i], device_id_type=MESH)

    for copy in loads[:2]:
        copy.wait()

    entry = (lax.rem(row, 4) * W + lax.broadcasted_iota(jnp.int32, (16, W), 1)).astype(F32)
    phase = time_ref[0].astype(F32) * jnp.exp(-math.log(10000.0) * entry / (D // 2))
    embedding = jnp.where(row < 4, jnp.cos(phase), jnp.sin(phase))
    high = embedding.astype(BF16).astype(F32)
    middle = (embedding - high).astype(BF16).astype(F32)
    low = embedding - high - middle
    line = lax.broadcasted_iota(jnp.int32, (16, W), 0)
    terms = jnp.where(line == 0, high, jnp.where(line == 1, middle, jnp.where(line == 2, low, 0.0)))
    modx[x] = jnp.zeros((8, W), F32)
    for r in range(3):
        products = jnp.dot(terms.astype(BF16), m_ref[r], preferred_element_type=F32)
        modx[x, r : r + 1, :] = jnp.sum(products, axis=0, keepdims=True)
    pl.semaphore_wait(barrier, len(partners) + len(swap_y) + 2 - same.astype(jnp.int32))

    swaps = []

    def swap_out(src_of, dst):
        ks = (next(ids), next(ids))
        for i in range(2):

            @pl.when(own[i])
            def _(i=i):
                pltpu.make_async_copy(src_of(i), dst.at[half], recv.at[ks[0] + half]).start()

            @pl.when(jnp.logical_not(own[i]))
            def _(i=i):
                remote(src_of(i), dst.at[half], ks[i], ks[0] + half, swap[i]).start()

        swaps.append((ks, src_of, dst))
        return ks

    def swap_in(ks, dst):
        for i in range(2):
            got(ks[i], dst.at[i])

    k_mx = {k: next(ids) for k in (1, 2, 3)}
    for k in (1, 2, 3):
        put(k_mx[k], modx.at[x], modx.at[x], dev(x_=xo(k)))
    ks_state = swap_out(lambda i: s_ref.at[pl.ds(T * i, T)], sbuf)

    mine = 4 * h + x
    far = 4 * (1 - h)

    def win_side():
        def slot_of(hx, first=0, rows=W):
            return win.at[pl.ds(pl.multiple_of(hx * W + first, 16), rows), :]

        def part_of(hd, first, rows):
            return wi_ref.at[pl.ds(pl.multiple_of(first, 16), rows), pl.ds(pl.multiple_of(hd * U, 128), U)]

        return part_of, slot_of, W

    def wout_side(col, cols):
        def slot_of(hx, first=0, rows=U):
            return wout.at[
                hx // 2,
                pl.ds(pl.multiple_of(first, 16), rows),
                pl.ds(pl.multiple_of(lax.rem(hx, 2) * W + col, 128), cols),
            ]

        def part_of(hd, first, rows):
            return wo_ref.at[pl.ds(pl.multiple_of(hd * U + first, 16), rows), col : col + cols]

        return part_of, slot_of, U

    class Side:
        def __init__(self, part_of, slot_of, rows, cross):
            self.part_of, self.slot_of, self.rows, self.q = part_of, slot_of, rows, rows // 4
            self.flows = range(5 if cross else 4)
            self.k_x = {k: next(ids) for k in (1, 3)}
            self.k_fwd = {} if cross else {k: next(ids) for k in (1, 3)}
            self.k_in = [next(ids) for _ in self.flows]
            self.k_y = {(s, k, f): next(ids) for s in self.flows for k in (1, 3) for f in range(2)}
            self.k_own = next(ids)

        def quarter(self, s, yy, first=0, rows=None):
            hx = 4 * h + xo(2) if s == 4 else far + xo(-s)
            return self.slot_of(hx, yy * self.q + first, rows or self.q)

        def far_start(self):
            put(self.k_in[0], self.part_of(1 - h, y * self.q, self.q), self.slot_of(mine, y * self.q, self.q), z4)

        def cross_start(self):
            to = dev(x_=xo(2))
            put(self.k_in[4], self.part_of(h, y * self.q, self.q), self.slot_of(mine, y * self.q, self.q), to)

        def near_start(self):
            for k in (1, 3):
                put(self.k_x[k], self.part_of(h, 0, self.rows), self.slot_of(mine), dev(x_=xo(k)))
            self.copy = pltpu.make_async_copy(self.part_of(h, 0, self.rows), self.slot_of(mine), recv.at[self.k_own])
            self.copy.start()

        def arrive(self, s):
            here = self.quarter(s, y)
            got(self.k_in[s], here)
            if s == 0:
                for k in (2, 1, 3):
                    put(self.k_in[k], here, here, dev(x_=xo(k)))
            for k in (1, 3):
                put(self.k_y[s, k, 0], here, here, dev(y_=yo(k)))

        def spread(self, s):
            for k, first in ((1, 0), (3, self.q // 2)):
                got(self.k_y[s, k, 0], self.quarter(s, yo(-k)))
                there = self.quarter(s, yo(-k), first, self.q // 2)
                put(self.k_y[s, k, 1], there, there, dev(y_=yo(k)))

        def forward(self):
            for k, first in ((1, 0), (3, self.rows // 2)):
                got(self.k_x[k], self.slot_of(4 * h + xo(-k)))
                there = self.slot_of(4 * h + xo(-k), first, self.rows // 2)
                put(self.k_fwd[k], there, there, dev(x_=xo(k)))

        def end(self):
            for k, first in ((1, 0), (3, self.rows // 2)):
                if self.k_fwd:
                    got(self.k_fwd[k], self.slot_of(4 * h + xo(2), first, self.rows // 2))
                else:
                    got(self.k_x[k], self.slot_of(4 * h + xo(-k)))
            for s in self.flows:
                for k, first in ((1, 0), (3, self.q // 2)):
                    got(self.k_y[s, k, 1], self.quarter(s, yo(2), first, self.q // 2))
            self.copy.wait()

    w_in = Side(*win_side(), True)
    w_out = Side(*wout_side(0, W), False)
    w_in.cross_start()
    w_in.far_start()
    w_in.near_start()

    def mod(j, r):
        return modall[j, r : r + 1, :]

    sign = (1, -1)

    class Part:
        def __init__(self, it, p):
            self.it, self.p = it, p
            self.first, self.n = PARTS[p]
            self.x, self.hid, self.part = xall[p].at[it], hid[p], part[p]
            self.k_stat = [next(ids) for _ in range(3)]
            steps = [(s, g, j) for s in range(1, 5) for j in range(2) for g in range(2)]
            self.k_ring = {key: next(ids) for key in steps if key[0] < 4 or key[1] == key[2]}
            self.k_sib = {key: next(ids) for key in self.k_ring}
            self.k_own = [next(ids) for _ in range(2)]
            self.units = ((0, W),)
            self.k_half = {(u, hh): next(ids) for u in self.units for hh in range(2)}
            self.k_sum = {
                u: {key: next(ids) for key in steps if key[0] > 1 or key[1] == key[2]} for u in self.units
            }
            self.k_prefix = {i: next(ids) for i in (1, 2, 3)}

        def rows(self):
            return slice(self.first, self.first + self.n)

        def stats(self, cur):
            self.cur = cur
            own, there = stat[self.p].at[self.it], statr[self.p].at[self.it]
            total = sum(jnp.sum(v, axis=1, keepdims=True) for v in cur)
            squares = sum(jnp.sum(v * v, axis=1, keepdims=True) for v in cur)
            lane = lax.broadcasted_iota(jnp.int32, (self.n, 128), 1)
            own[...] = jnp.where(lane < 64, total, squares)
            for i, to in enumerate((z4, z4sib, sib)):
                put(self.k_stat[i], own, there.at[i], to)

        def slot(self, zz, cc, j):
            hh, ll = zz // 4, lax.rem(zz, 4)
            return self.x.at[
                pl.ds(pl.multiple_of(ll * self.n, 16), self.n),
                pl.ds(pl.multiple_of((4 * hh + 2 * cc + j) * W, 128), W),
            ]

        def normalise(self):
            own, there = stat[self.p].at[self.it], statr[self.p].at[self.it]
            for i, k in enumerate(self.k_stat):
                got(k, there.at[i])
            total = own[...] + there[0] + there[1] + there[2]
            mean = total[:, 0:1] / D
            var = total[:, 64:65] / D - mean * mean
            scale = lax.rsqrt(var + EPSILON)
            for j in range(2):
                value = (self.cur[j] - mean) * scale * (1.0 + mod(j, 1)) + mod(j, 0)
                slot = self.slot(z, c, j)
                slot[...] = value.astype(BF16)
            for g, j in ORDER:
                slot = self.slot(z, c, j)
                put(self.k_ring[1, g, j], slot, slot, dev(z_=zo(sign[g])))
            for j in range(2):
                slot = self.slot(z, c, j)
                put(self.k_own[j], slot, slot, sib)

        def gather(self, s):
            for g, j in ORDER:
                if (s, g, j) not in self.k_ring:
                    continue
                slot = self.slot(zo(-sign[g] * s), c, j)
                got(self.k_ring[s, g, j], slot)
                if (s + 1, g, j) in self.k_ring:
                    put(self.k_ring[s + 1, g, j], slot, slot, dev(z_=zo(sign[g])))
                put(self.k_sib[s, g, j], slot, slot, sib)

        def gathered(self, steps=(1, 2, 3, 4)):
            if 1 in steps:
                for j in range(2):
                    got(self.k_own[j], self.slot(z, 1 - c, j))
            for (s, g, j), k in self.k_sib.items():
                if s in steps:
                    got(k, self.slot(zo(-sign[g] * s), 1 - c, j))

        def first_matmul(self):
            def tile(n, _):
                cols = pl.ds(pl.multiple_of(n * 256, 256), 256)
                pre = jnp.dot(self.x[...], win[:, cols], preferred_element_type=F32)
                self.hid[:, cols] = jax.nn.gelu(pre, approximate=True).astype(BF16)
                return 0

            lax.fori_loop(0, U // 256, tile, 0)

        def tiles(self, u):
            if u[1] < W:
                return [(j, u[0], u[1]) for j in range(2)]
            return [(None, 256 * n, 256) for n in range(3)]

        def first_half(self, hh, last):
            rows = pl.ds(pl.multiple_of(hh * (D // 2), 128), D // 2)
            for n in range(U // 256):
                cols = slice(256 * n, 256 * n + 256)
                pre = jnp.dot(self.x[:, rows], win[rows, cols], preferred_element_type=F32)
                if last:
                    pre = pre + acc[self.p][:, cols]
                    self.hid[:, cols] = jax.nn.gelu(pre, approximate=True).astype(BF16)
                else:
                    acc[self.p][:, cols] = pre

        def second(self, cc, hh, u):
            for j, col, cols in self.tiles(u):
                at = col if j is None else W * j + col
                yield at, cols, jnp.dot(self.hid[...], wout[2 * hh + cc, :, at : at + cols], preferred_element_type=F32)

        def second_other(self, u):
            there, back = obs[self.p].at[self.it], obr[self.p].at[self.it]
            for hh in range(2):
                for at, cols, value in self.second(1 - c, hh, u):
                    for j, col in ((n // 3, n % 3 * 128) for n in range(at // 128, (at + cols) // 128)):
                        first = W * j + col - at
                        there[hh, j, :, col : col + 128] = value[:, first : first + 128].astype(BF16)
                cols = slice(u[0], u[0] + u[1])
                put(self.k_half[u, hh], there.at[hh, :, :, cols], back.at[hh, :, :, cols], sib)

        def second_own(self, u):
            for hh in range(2):
                for at, cols, value in self.second(c, hh, u):
                    self.part[hh, :, :, at : at + cols] = value.reshape(4, self.n, cols)

        def halves(self, u):
            back = obr[self.p].at[self.it]
            cols = slice(u[0], u[0] + u[1])
            for hh in range(2):
                got(self.k_half[u, hh], back.at[hh, :, :, cols])
                for j in range(2):
                    at = slice(W * j + u[0], W * j + u[0] + u[1])
                    self.part[hh, :, :, at] += back[hh, j, :, cols].astype(F32).reshape(4, self.n, u[1])

        def term(self, d, j, u):
            return self.part[d // 4, lax.rem(d, 4), :, W * j + u[0] : W * j + u[0] + u[1]]

        def scatter(self, s, u):
            k = self.k_sum[u]
            cols = slice(u[0], u[0] + u[1])
            out, back = rss[self.p].at[self.it], rsr[self.p].at[self.it]
            for g, j in ORDER:
                t = s if g == j else s + 1
                if t > 4:
                    continue
                value = self.term(zo(sign[g] * (5 - t)), j, u)
                if (t - 1, g, j) in k:
                    got(k[t - 1, g, j], back.at[t - 2, g, j, :, cols])
                    value = value + back[t - 2, g, j, :, cols].astype(F32)
                out[t - 1, g, j, :, cols] = value.astype(BF16)
                here, there = out.at[t - 1, g, j, :, cols], back.at[t - 1, g, j, :, cols]
                put(k[t, g, j], here, there, dev(z_=zo(sign[g])))

        def scattered(self, u):
            k = self.k_sum[u]
            cols = slice(u[0], u[0] + u[1])
            back = rsr[self.p].at[self.it]
            for j in range(2):
                value = self.term(z, j, u)
                for g in range(2):
                    got(k[4, g, j], back.at[3, g, j, :, cols])
                    value = value + back[3, g, j, :, cols].astype(F32)
                drift[self.p][j, :, cols] = step_ref[0] * mod(j, 2)[:, cols] * value

        def prefix_copy(self, i):
            return remote(
                dsend[self.p], drecv[self.p].at[i - 1], self.k_prefix[i], self.k_prefix[i], dev(y_=yo(i))
            )

        def prefix_send(self):
            for j in range(2):
                dsend[self.p][j] = drift[self.p][j].astype(BF16)
            for i in (1, 2, 3):

                @pl.when(y + i < 4)
                def _(i=i):
                    self.prefix_copy(i).start()

        def prefix_add(self):
            pref[:, self.rows(), :] = jnp.zeros((2, self.n, W), F32)
            for i in (3, 2, 1):

                @pl.when(y - i >= 0)
                def _(i=i):
                    got(self.k_prefix[i], drecv[self.p].at[i - 1])
                    for j in range(2):
                        pref[j, self.rows(), :] += drecv[self.p][i - 1, j].astype(F32)

        def prefix_sent(self):
            for i in (1, 2, 3):

                @pl.when(y + i < 4)
                def _(i=i):
                    self.prefix_copy(i).wait_send()

        def current(self):
            return [abuf[j, self.rows(), :] + pref[j, self.rows(), :] for j in range(2)]

        def out_copy(self, k, i):
            there = frecv.at[k, half, pl.ds(self.first, self.n)]
            to = swap[i] if k == 0 else swap_y[i, k]
            return remote(fsend[self.p].at[i], there, self.k_out[k, i], self.k_out[k, 0] + half, to)

        def out_send(self):
            self.k_out = {(k, i): next(ids) for k in range(4) for i in range(2)}
            for i in range(2):
                fsend[self.p][i] = drift[self.p][i].astype(BF16)
            for k in (3, 2, 1, 0):
                for i in range(2):
                    if k:

                        @pl.when(y + k < 4)
                        def _(i=i, k=k):
                            self.out_copy(k, i).start()

                    else:
                        there = frecv.at[0, half, pl.ds(self.first, self.n)]

                        @pl.when(own[i])
                        def _(i=i):
                            pltpu.make_async_copy(
                                fsend[self.p].at[i], there, recv.at[self.k_out[0, 0] + half]
                            ).start()

                        @pl.when(jnp.logical_not(own[i]))
                        def _(i=i):
                            self.out_copy(0, i).start()

        def out_sent(self):
            for k in range(4):
                for i in range(2):

                    @pl.when(y + k < 4 if k else jnp.logical_not(own[i]))
                    def _(i=i, k=k):
                        self.out_copy(k, i).wait_send()

        def out_add(self):
            for i in range(2):
                rows = slice(T * i + self.first, T * i + self.first + self.n)
                out_ref[rows, :] = jnp.zeros((self.n, W), F32)
                for k in (3, 2, 1, 0):

                    @pl.when(y - k >= 0)
                    def _(i=i, k=k):
                        got(self.k_out[k, i], frecv.at[k, i, pl.ds(self.first, self.n)])
                        out_ref[rows, :] += frecv[k, i, self.rows(), :].astype(F32)

    parts = [[Part(it, p) for p in range(2)] for it in range(ITERS)]
    a, b = parts[0]

    for copy in loads[2:]:
        copy.wait()

    for k in (1, 2, 3):
        got(k_mx[k], modx.at[xo(-k)])
    k_ms = next(ids)
    put(k_ms, modx.at[pl.ds(2 * (1 - c), 2)], msib, sib)
    swap_in(ks_state, sbuf)
    for v in (a, b):
        v.stats([sbuf[j, v.rows(), :] for j in range(2)])
    w_out.far_start()
    got(k_ms, msib)
    m1[...] = modx[pl.ds(2 * c, 2)] + msib[...]
    k_ml = {k: next(ids) for k in (1, 2, 3)}
    for k in (1, 2, 3):
        put(k_ml[k], m1, mrecv.at[k - 1], lo(k))
    w_in.arrive(4)
    w_in.arrive(0)
    w_in.spread(4)
    w_out.arrive(0)
    w_out.near_start()
    w_in.spread(0)
    for k in (1, 2, 3):
        got(k_ml[k], mrecv.at[k - 1])
    modall[...] = m1[...] + mrecv[0] + mrecv[1] + mrecv[2]
    for v in (a, b):
        v.normalise()
    w_out.spread(0)
    w_in.arrive(2)
    for v in (a, b):
        v.gather(1)
    w_in.arrive(1)
    w_in.arrive(3)
    for v in (a, b):
        v.gather(2)
    w_in.spread(2)
    w_out.arrive(2)
    w_in.spread(1)
    w_out.arrive(1)
    w_out.arrive(3)
    for v in (a, b):
        v.gather(3)
    w_in.spread(3)
    for v in (a, b):
        v.gather(4)
    w_out.forward()
    w_out.spread(2)
    w_out.spread(1)
    w_out.spread(3)
    a.gathered()
    b.gathered()
    w_in.end()
    a.first_matmul()
    b.first_matmul()
    w_out.end()
    ks_anchor = swap_out(lambda i: a_any.at[pl.ds(T * i, T)], abuf)

    u = (0, W)
    for it in range(ITERS):
        a, b = parts[it]
        if it:
            a.gathered((4,))
            a.first_half(1 - h, True)
        a.second_other(u)
        a.second_own(u)
        if it:
            b.gathered((4,))
        a.halves(u)
        a.scatter(1, u)
        if it:
            b.first_half(1 - h, True)
        b.second_other(u)
        b.second_own(u)
        a.scatter(2, u)
        b.halves(u)
        b.scatter(1, u)
        a.scatter(3, u)
        b.scatter(2, u)
        a.scatter(4, u)
        b.scatter(3, u)
        a.scattered(u)
        if it + 1 == ITERS:
            a.out_send()
            b.scatter(4, u)
            b.scattered(u)
            b.out_send()
            a.out_add()
            b.out_add()
            continue
        a.prefix_send()
        b.scatter(4, u)
        b.scattered(u)
        b.prefix_send()
        swap_in(ks_anchor, abuf)
        after, later = parts[it + 1]
        a.prefix_add()
        after.stats(a.current())
        b.prefix_add()
        later.stats(b.current())
        after.normalise()
        later.normalise()
        for s in range(1, 4):
            after.gather(s)
            later.gather(s)
        after.gather(4)
        after.gathered((1, 2, 3))
        after.first_half(h, False)
        later.gathered((1, 2, 3))
        later.first_half(h, False)
        later.gather(4)

    for copy in pending:
        copy.wait_send()
    for v in parts[0]:
        v.prefix_sent()
    for v in parts[1]:
        v.out_sent()
    for ks, src_of, dst in swaps:
        for i in range(2):

            @pl.when(jnp.logical_not(own[i]))
            def _(i=i):
                remote(src_of(i), dst.at[half], ks[i], ks[0] + half, swap[i]).wait_send()


def local(states, anchor, timesteps, step_sizes, weight_in, weight_out, mod_weight):
    vmem = pl.BlockSpec(memory_space=pltpu.VMEM)

    def each(make):
        return [make(n) for _, n in PARTS]

    scratch = [
        pltpu.SMEM((1,), jnp.int32),
        pltpu.SMEM((1,), F32),
        pltpu.VMEM(anchor.shape, F32),
        pltpu.VMEM((3, W, W), BF16),
        pltpu.VMEM((2, T, W), F32),
        pltpu.VMEM((2, T, W), F32),
        pltpu.VMEM((4, 8, W), F32),
        pltpu.VMEM((2, 8, W), F32),
        pltpu.VMEM((2, 8, W), F32),
        pltpu.VMEM((3, 2, 8, W), F32),
        pltpu.VMEM((2, 8, W), F32),
        pltpu.VMEM((D, U), BF16),
        pltpu.VMEM((4, U, 2 * W), BF16),
        pltpu.VMEM((2, T, W), F32),
        pltpu.VMEM((4, 2, T, W), BF16),
        each(lambda n: pltpu.VMEM((ITERS, n, 128), F32)),
        each(lambda n: pltpu.VMEM((ITERS, 3, n, 128), F32)),
        each(lambda n: pltpu.VMEM((ITERS, 4 * n, D), BF16)),
        each(lambda n: pltpu.VMEM((4 * n, U), BF16)),
        each(lambda n: pltpu.VMEM((ITERS, 2, 2, 4 * n, W), BF16)),
        each(lambda n: pltpu.VMEM((ITERS, 2, 2, 4 * n, W), BF16)),
        each(lambda n: pltpu.VMEM((2, 4, n, 2 * W), F32)),
        each(lambda n: pltpu.VMEM((ITERS, 4, 2, 2, n, W), BF16)),
        each(lambda n: pltpu.VMEM((ITERS, 4, 2, 2, n, W), BF16)),
        each(lambda n: pltpu.VMEM((2, n, W), BF16)),
        each(lambda n: pltpu.VMEM((3, 2, n, W), BF16)),
        each(lambda n: pltpu.VMEM((2, n, W), BF16)),
        each(lambda n: pltpu.VMEM((2, n, W), F32)),
        each(lambda n: pltpu.VMEM((4 * n, U), F32)),
        pltpu.SemaphoreType.DMA((COPIES,)),
        pltpu.SemaphoreType.DMA((COPIES,)),
    ]
    out = pl.pallas_call(
        kernel,
        out_shape=jax.ShapeDtypeStruct(anchor.shape, F32),
        in_specs=[pl.BlockSpec(memory_space=pl.ANY)] * 7,
        out_specs=vmem,
        scratch_shapes=scratch,
        compiler_params=pltpu.CompilerParams(
            collective_id=0, has_side_effects=True, vmem_limit_bytes=60 << 20
        ),
        name="picard",
    )(timesteps, step_sizes, states[0], anchor, mod_weight.transpose(1, 0, 2), weight_in, weight_out)
    return (anchor + out)[None]


def solution(mesh):
    placed = (
        P("tm", "row", "col"),
        P("row", "col"),
        P("tm"),
        P("tm"),
        P("col", "row"),
        P("row", "col"),
        P("row", None, "col"),
    )
    return jax.shard_map(
        local, mesh=mesh, in_specs=placed, out_specs=P("tm", "row", "col"), check_vma=False
    )
```
